128 devices in a mesh: dp: 32 (over x, y_hi, z), mp: 4 (over y_lo, core).
Axes of the slice: x: 4, y: 4 (y_hi: 2, y_lo: 2; y = y_hi * 2 + y_lo), z: 4, core: 2. Of those that a mesh axis runs over, the one named last changes fastest.
Arguments:
- block_input: bfloat16 [32, 512, 2048], P('dp', 'mp'), may hold values from -6 to 6
- lengths: int32 [32, 3], P('dp'), may hold values from 1 to 510, as said below
- gain_attn: float32 [2048], replicated, may hold values from 0.5 to 1.5
- gain_ffn: float32 [2048], replicated, may hold values from 0.5 to 1.5
- w_query: bfloat16 [2048, 256], P(None, 'mp'), may hold values from -0.125 to 0.125
- w_key: bfloat16 [2048, 256], P(None, 'mp'), may hold values from -0.125 to 0.125
- w_value: bfloat16 [2048, 2048], P(None, 'mp'), may hold values from -0.125 to 0.125
- w_out: bfloat16 [2048, 2048], P('mp'), may hold values from -0.5 to 0.5
- w_gate: bfloat16 [2048, 5504], P(None, 'mp'), may hold values from -0.125 to 0.125
- w_up: bfloat16 [2048, 5504], P(None, 'mp'), may hold values from -0.125 to 0.125
- w_down: bfloat16 [5504, 2048], P('mp'), may hold values from -0.078125 to 0.078125
- cotangent: bfloat16 [32, 512, 2048], P('dp', 'mp'), may hold values from -6 to 6
Outputs:
- block_output: bfloat16 [32, 512, 2048], P('dp', 'mp')
- grad_input: float32 [32, 512, 2048], P('dp', 'mp')
- grad_gain_attn: float32 [2048], P(('dp', 'mp'))
- grad_gain_ffn: float32 [2048], P(('dp', 'mp'))
- grad_query: float32 [2048, 256], P('dp', 'mp')
- grad_key: float32 [2048, 256], P('dp', 'mp')
- grad_value: float32 [2048, 2048], P('dp', 'mp')
- grad_out: float32 [2048, 2048], P('mp', 'dp')
- grad_gate: float32 [2048, 5504], P('dp', 'mp')
- grad_up: float32 [2048, 5504], P('dp', 'mp')
- grad_down: float32 [5504, 2048], P('mp', 'dp')
The draws below stay inside these ranges and needn't reach their ends.
Inputs may be any that keep to these rules, and one draw needn't show every extreme that they name: `lengths`: each row holds three documents in order; the first and the last have 1 to 64 positions each, the middle one the rest of the row's 512 positions. Some row has first and last documents of one position each.
All inputs are finite; a program needn't handle non-finite values.
Results may differ from the reference program's by a relative error of at most 0.025.
Values may be sent and summed in bfloat16 or wider, within the bound.
A program may use at most 192 MiB of HBM per device.

```python
from functools import partial
import jax
import jax.numpy as jnp
from jax import lax

D = 2048
HEADS = 16
FEAT = 16
VDIM = 128
FF = 5504
WINDOW = 64
TOK_DEV = 128
LEN = 512
ROWS = 32


def draw_lengths(key, part):
    key = jax.random.fold_in(key, 7)
    first_key, last_key, pick_key = jax.random.split(key, 3)
    first_len = jax.random.randint(first_key, (ROWS, 1), 1, TOK_DEV // 2 + 1)
    last_len = jax.random.randint(last_key, (ROWS, 1), 1, TOK_DEV // 2 + 1)
    chosen = jax.random.randint(pick_key, (), 0, ROWS)
    row_ids = jnp.arange(ROWS, dtype=jnp.int32)[:, None]
    first_len = jnp.where(row_ids == chosen, 1, first_len)
    last_len = jnp.where(row_ids == chosen, 1, last_len)
    middle_len = LEN - first_len - last_len
    return jnp.concatenate([first_len, middle_len, last_len], axis=1).astype(jnp.int32)


def block_scale(stream_key, extent, shards, smallest, top_value):
    def one(dim, parts):
        heights = jax.random.uniform(jax.random.fold_in(jax.random.fold_in(stream_key, 6), dim), (parts,), jnp.float32, smallest / len(shards), top_value / len(shards))
        return jnp.repeat(jnp.exp(heights), extent[dim] // parts).reshape((-1,) + (1,) * (len(extent) - dim - 1))

    gain = one(*shards[0])
    for cut in shards[1:]:
        gain = gain * one(*cut)
    return gain


def gaussian(stream_key, dims, deviation, reach, cuts=(), kind=jnp.bfloat16):
    entries = jax.random.normal(stream_key, dims, jnp.float32) * deviation
    if len(cuts) > 0:
        entries = block_scale(stream_key, dims, cuts, -0.22, 0.18) * entries
    return jnp.clip(entries, min=-reach, max=reach).astype(kind)


def setup_inputs(seed: int = 0) -> dict:
    splits = jax.random.split(jax.random.key(seed), 13)
    return {
        "block_input": gaussian(splits[0], (ROWS, LEN, D), 1.0, 6.0, ((0, 32), (1, 4))),
        "lengths": draw_lengths(jax.random.fold_in(splits[12], 71), 0),
        "gain_attn": jnp.clip(1.0 + 0.1 * jax.random.normal(splits[2], (D,), jnp.float32), 0.5, 1.5),
        "gain_ffn": jnp.clip(1.0 + 0.1 * jax.random.normal(splits[3], (D,), jnp.float32), 0.5, 1.5),
        "w_query": gaussian(splits[4], (D, HEADS * FEAT), D ** -0.5, 0.125, ((1, 4),)),
        "w_key": gaussian(splits[5], (D, HEADS * FEAT), D ** -0.5, 0.125, ((1, 4),)),
        "w_value": gaussian(splits[6], (D, HEADS * VDIM), D ** -0.5, 0.125, ((1, 4),)),
        "w_out": gaussian(splits[7], (HEADS * VDIM, D), (HEADS * VDIM // 16) ** -0.5, 0.5, ((0, 4),)),
        "w_gate": gaussian(splits[8], (D, FF), D ** -0.5, 0.125, ((1, 4),)),
        "w_up": gaussian(splits[9], (D, FF), D ** -0.5, 0.125, ((1, 4),)),
        "w_down": gaussian(splits[10], (FF, D), FF ** -0.5, 0.078125, ((0, 4),)),
        "cotangent": gaussian(splits[11], (ROWS, LEN, D), 1.0, 6.0, ((0, 32), (1, 4))),
    }


@jax.custom_vjp
def low(v):
    return lax.optimization_barrier(v.astype(jnp.bfloat16)).astype(jnp.float32)

@jax.custom_vjp
def low_back(v):
    return v

def low_keep(v):
    return (low(v), None)

def low_pass(kept, grad):
    return (grad,)

def back_keep(v):
    return (v, None)

def back_low(kept, grad):
    return (low(grad),)
low.defvjp(low_keep, low_pass)
low_back.defvjp(back_keep, back_low)
norm_eps = 1e-05
masked_score = -1e+30

def matmul(left, right):
    return jnp.dot(left, right, precision=lax.Precision.HIGHEST)

def rms_scale(values, gain_vec):
    return values * lax.rsqrt(lax.optimization_barrier(jnp.mean(values * values, axis=-1, keepdims=True)) + norm_eps) * gain_vec

def doc_table(lengths):
    doc_ends = jnp.cumsum(lengths, axis=1).astype(jnp.int32)
    positions = jnp.arange(LEN, dtype=jnp.int32)
    return lax.optimization_barrier(jnp.sum((positions[None, :, None] >= doc_ends[:, None, :]).astype(jnp.int32), axis=2))

def mixer_row(packed):
    query, key_rows, value_rows, doc_ids = packed
    q_heads = query.reshape(LEN, HEADS, FEAT)
    k_heads = key_rows.reshape(LEN, HEADS, FEAT)
    v_heads = value_rows.reshape(LEN, HEADS, VDIM)
    raw_score = low_back(jnp.einsum('thf,shf->hts', q_heads, k_heads, precision=lax.Precision.HIGHEST))
    positions = jnp.arange(LEN, dtype=jnp.int32)
    causal = (positions[:, None] >= positions[None, :]) & (doc_ids[:, None] == doc_ids[None, :])
    window = causal & (positions[:, None] - positions[None, :] < WINDOW)
    feat_scale = FEAT ** (-0.5)
    kernel = jnp.where(causal[None], 1.0 + raw_score * feat_scale + raw_score * raw_score * (0.5 / FEAT), 0.0)
    denominator = lax.optimization_barrier(jnp.sum(kernel, axis=2))
    numerator = low_back(jnp.einsum('hts,shv->htv', low(kernel), v_heads, precision=lax.Precision.HIGHEST))
    linear = numerator / denominator[:, :, None]
    scores = jnp.where(window[None], raw_score * feat_scale, masked_score)
    probs_low = low(jax.nn.softmax(scores, axis=2))
    windowed = jnp.einsum('hts,shv->htv', probs_low, v_heads, precision=lax.Precision.HIGHEST)
    mixed_out = low(low_back(linear + windowed))
    return jnp.transpose(mixed_out, (1, 0, 2)).reshape(LEN, HEADS * VDIM)

def forward(block_input, gain_attn, gain_ffn, w_query, w_key, w_value, w_out, w_gate, w_up, w_down, doc_ids):
    flat_in = block_input.reshape(ROWS * LEN, D)
    normed = low(rms_scale(flat_in, gain_attn))
    query = low(low_back(matmul(normed, w_query)))
    key_rows = low(low_back(matmul(normed, w_key)))
    value_rows = low(low_back(matmul(normed, w_value)))
    mixed_rows = lax.map(jax.checkpoint(mixer_row), (query.reshape(ROWS, LEN, HEADS * FEAT), key_rows.reshape(ROWS, LEN, HEADS * FEAT), value_rows.reshape(ROWS, LEN, HEADS * VDIM), doc_ids))
    attn_out = low_back(matmul(mixed_rows.reshape(ROWS * LEN, HEADS * VDIM), w_out))
    hidden_one = flat_in + attn_out
    normed_two = low(rms_scale(hidden_one, gain_ffn))
    gate_pre = low_back(matmul(normed_two, w_gate))
    up_pre = low_back(matmul(normed_two, w_up))
    act_low = low(jax.nn.silu(gate_pre) * up_pre)
    block_out = hidden_one + low_back(matmul(act_low, w_down))
    return block_out.reshape(ROWS, LEN, D)

def reference(block_input, lengths, gain_attn, gain_ffn, w_query, w_key, w_value, w_out, w_gate, w_up, w_down, cotangent):
    doc_ids = doc_table(lengths)
    floats = (block_input.astype(jnp.float32), gain_attn.astype(jnp.float32), gain_ffn.astype(jnp.float32), w_query.astype(jnp.float32), w_key.astype(jnp.float32), w_value.astype(jnp.float32), w_out.astype(jnp.float32), w_gate.astype(jnp.float32), w_up.astype(jnp.float32), w_down.astype(jnp.float32))
    block_out, pullback = jax.vjp(partial(forward, doc_ids=doc_ids), *floats)
    grads = pullback(cotangent.astype(jnp.float32))
    return (block_out.astype(jnp.bfloat16), grads[0], grads[1], grads[2], grads[3], grads[4], grads[5], grads[6], grads[7], grads[8], grads[9])
```

```python
import functools

import jax
import jax.numpy as jnp
from jax import lax
from jax.experimental import pallas as pl
from jax.experimental.pallas import tpu as pltpu
from jax.sharding import PartitionSpec as P

MESH = pl.DeviceIdType.MESH
F32 = jnp.float32
BF16 = jnp.bfloat16

FEAT = 16
VDIM = 128
WINDOW = 64


norm_eps = 1e-05
masked_score = -1e30


def place():
    dp, mp = lax.axis_index("dp"), lax.axis_index("mp")
    return dp // 8, (dp // 4) % 2, dp % 4, mp // 2, mp % 2


def device(x, yh, z, yl, core):
    return (x * 8 + yh * 4 + z, yl * 2 + core)


def greet(devices):
    barrier = pltpu.get_barrier_semaphore()
    for target in devices:
        pl.semaphore_signal(barrier, inc=1, device_id=target, device_id_type=MESH)
    pl.semaphore_wait(barrier, len(devices))


def remote(src, dst, send_sem, recv_sem, target):
    return pltpu.make_async_remote_copy(
        src_ref=src,
        dst_ref=dst,
        send_sem=send_sem,
        recv_sem=recv_sem,
        device_id=target,
        device_id_type=MESH,
    )


PARTS = 4


def gather_kernel(own_ref, full_ref, send, recv):
    x, yh, z, yl, core = place()
    mate, pair = device(x, yh, z, yl, 1 - core), device(x, yh, z, 1 - yl, core)
    tok = own_ref.shape[0]
    piece = tok // PARTS
    greet((mate, pair))
    mine, far = yl * 2 + core, (1 - yl) * 2 + core
    outgoing = []
    for i in range(PARTS):
        copy = remote(
            own_ref.at[pl.ds(i * piece, piece)],
            full_ref.at[pl.ds(pl.multiple_of(mine * tok + i * piece, piece), piece)],
            send.at[i],
            recv.at[i],
            pair,
        )
        copy.start()
        outgoing.append(copy)
    near = remote(
        own_ref,
        full_ref.at[pl.ds(pl.multiple_of(mine * tok, tok), tok)],
        send.at[PARTS],
        recv.at[PARTS],
        mate,
    )
    near.start()
    full_ref[pl.ds(pl.multiple_of(mine * tok, tok), tok), :] = own_ref[...]
    passed = []
    for i in range(PARTS):
        outgoing[i].wait_recv()
        rows = pl.ds(pl.multiple_of(far * tok + i * piece, piece), piece)
        copy = remote(
            full_ref.at[rows],
            full_ref.at[rows],
            send.at[PARTS + 1 + i],
            recv.at[PARTS + 1 + i],
            mate,
        )
        copy.start()
        passed.append(copy)
    near.wait()
    for i in range(PARTS):
        outgoing[i].wait_send()
        passed[i].wait()


def gather_rows(own):
    tok, width = own.shape
    return pl.pallas_call(
        gather_kernel,
        out_shape=jax.ShapeDtypeStruct((4 * tok, width), own.dtype),
        in_specs=[pl.BlockSpec(memory_space=pltpu.VMEM)],
        out_specs=pl.BlockSpec(memory_space=pltpu.VMEM),
        scratch_shapes=[
            pltpu.SemaphoreType.DMA((2 * PARTS + 1,)),
            pltpu.SemaphoreType.DMA((2 * PARTS + 1,)),
        ],
        compiler_params=pltpu.CompilerParams(
            collective_id=0, has_side_effects=True, vmem_limit_bytes=32 << 20
        ),
        name="gather_rows",
    )(own)


def scatter_kernel(part_ref, out_ref, near_out, near_in, far_out, far_in, send, recv):
    x, yh, z, yl, core = place()
    mate, pair = device(x, yh, z, yl, 1 - core), device(x, yh, z, 1 - yl, core)
    tok = out_ref.shape[0]
    piece = tok // PARTS
    greet((mate, pair))
    near_copies = []
    for k, side in enumerate((1 - yl, yl)):
        start = pl.multiple_of((side * 2 + 1 - core) * tok, tok)
        near_out[k] = part_ref[pl.ds(start, tok), :].astype(BF16)
        copy = remote(near_out.at[k], near_in.at[k], send.at[k], recv.at[k], mate)
        copy.start()
        near_copies.append(copy)
    near_copies[0].wait_recv()
    far_copies = []
    far_start = pl.multiple_of(((1 - yl) * 2 + core) * tok, tok)
    for i in range(PARTS):
        rows = pl.ds(i * piece, piece)
        far_out[rows] = (
            part_ref[pl.ds(far_start + i * piece, piece), :] + near_in[0, rows].astype(F32)
        ).astype(BF16)
        copy = remote(far_out.at[rows], far_in.at[rows], send.at[2 + i], recv.at[2 + i], pair)
        copy.start()
        far_copies.append(copy)
    near_copies[1].wait_recv()
    own_start = pl.multiple_of((yl * 2 + core) * tok, tok)
    for i in range(PARTS):
        rows = pl.ds(i * piece, piece)
        far_copies[i].wait_recv()
        out_ref[rows, :] = (
            part_ref[pl.ds(own_start + i * piece, piece), :]
            + near_in[1, rows].astype(F32)
            + far_in[rows].astype(F32)
        )
    for copy in near_copies + far_copies:
        copy.wait_send()


def scatter_rows(part):
    rows, width = part.shape
    tok = rows // 4
    return pl.pallas_call(
        scatter_kernel,
        out_shape=jax.ShapeDtypeStruct((tok, width), F32),
        in_specs=[pl.BlockSpec(memory_space=pltpu.VMEM)],
        out_specs=pl.BlockSpec(memory_space=pltpu.VMEM),
        scratch_shapes=[
            pltpu.VMEM((2, tok, width), BF16),
            pltpu.VMEM((2, tok, width), BF16),
            pltpu.VMEM((tok, width), BF16),
            pltpu.VMEM((tok, width), BF16),
            pltpu.SemaphoreType.DMA((2 + PARTS,)),
            pltpu.SemaphoreType.DMA((2 + PARTS,)),
        ],
        compiler_params=pltpu.CompilerParams(
            collective_id=1, has_side_effects=True, vmem_limit_bytes=48 << 20
        ),
        name="scatter_rows",
    )(part)


def add_into(dst, terms, rows, step):
    def body(i, _):
        at = pl.ds(pl.multiple_of(i * step, step), step)
        total = dst[at, :].astype(F32)
        for term in terms:
            total = total + term[at, :].astype(F32)
        dst[at, :] = total.astype(dst.dtype)
        return 0

    lax.fori_loop(0, rows // step, body, 0)


class RowSum:
    def __init__(self, grad, bufs, send, recv):
        self.grad = grad
        self.t1, self.m1, self.t2, self.m2, self.last = bufs
        self.send, self.recv = send, recv
        self.x, self.yh, self.z, self.yl, self.core = place()

    def near(self, path, stage, step):
        if (path == 0) == (stage == 0):
            return device((self.x + step + 4) % 4, self.yh, self.z, self.yl, self.core)
        return device(self.x, self.yh, (self.z + step + 4) % 4, self.yl, self.core)

    def at(self, path, stage):
        return self.x if (path == 0) == (stage == 0) else self.z

    def block(self, path, b, k):
        return self.grad.at[b, 0, k] if path == 0 else self.grad.at[k, 1, b]

    def copy(self, src, dst, path, slot, target):
        return remote(src, dst, self.send.at[path, slot], self.recv.at[path, slot], target)

    def transit_one(self, path, side):
        b = (self.at(path, 0) + 2) % 4
        return self.copy(
            self.block(path, b, pl.ds(2 * side, 2)),
            self.t1.at[path, side],
            path,
            side,
            self.near(path, 0, 1 - 2 * side),
        )

    def main_one(self, path, side, half):
        step = 1 - 2 * side
        b = (self.at(path, 0) + step + 4) % 4
        src = (
            self.t1.at[path, side]
            if half == side
            else self.block(path, b, pl.ds(2 * half, 2))
        )
        return self.copy(
            src,
            self.m1.at[path, side, pl.ds(2 * half, 2)],
            path,
            2 + 2 * side + half,
            self.near(path, 0, step),
        )

    def transit_two(self, path, side):
        k = (self.at(path, 1) + 2) % 4
        return self.copy(
            self.m1.at[path, 0, k, pl.ds(32 * side, 32)],
            self.t2.at[path, side],
            path,
            6 + side,
            self.near(path, 1, 1 - 2 * side),
        )

    def main_two(self, path, side, half):
        step = 1 - 2 * side
        k = (self.at(path, 1) + step + 4) % 4
        rows = pl.ds(32 * half, 32)
        src = self.t2.at[path, side] if half == side else self.m1.at[path, 0, k, rows]
        return self.copy(
            src,
            self.m2.at[path, side, rows],
            path,
            8 + 2 * side + half,
            self.near(path, 1, step),
        )

    def last_copy(self):
        target = device(self.x, 1 - self.yh, self.z, self.yl, self.core)
        return self.copy(self.m2.at[1 - self.yh, 0], self.last, 0, 12, target)

    def start_one(self):
        for path in (0, 1):
            for side in (0, 1):
                self.transit_one(path, side).start()
        for path in (0, 1):
            for side in (0, 1):
                self.main_one(path, side, 1 - side).start()

    def pass_one(self):
        for path in (0, 1):
            for side in (0, 1):
                self.transit_one(path, side).wait_recv()
                b = (self.at(path, 0) + 1 - 2 * side + 4) % 4
                for k in (0, 1):
                    add_into(
                        self.t1.at[path, side, k],
                        (self.block(path, b, 2 * side + k),),
                        64,
                        16,
                    )
                self.main_one(path, side, side).start()

    def join_one(self):
        for path in (0, 1):
            for side in (0, 1):
                for half in (0, 1):
                    self.main_one(path, side, half).wait_recv()
            b = self.at(path, 0)

            def body(k, _):
                add_into(
                    self.m1.at[path, 0, k],
                    (self.m1.at[path, 1, k], self.block(path, b, k)),
                    64,
                    16,
                )
                return 0

            lax.fori_loop(0, 4, body, 0)
            for side in (0, 1):
                self.transit_two(path, side).start()
            for side in (0, 1):
                self.main_two(path, side, 1 - side).start()

    def pass_two(self):
        for path in (0, 1):
            for side in (0, 1):
                self.transit_two(path, side).wait_recv()
                k = (self.at(path, 1) + 1 - 2 * side + 4) % 4
                add_into(
                    self.t2.at[path, side],
                    (self.m1.at[path, 0, k, pl.ds(32 * side, 32)],),
                    32,
                    16,
                )
                self.main_two(path, side, side).start()

    def join_two(self):
        for path in (0, 1):
            for side in (0, 1):
                for half in (0, 1):
                    self.main_two(path, side, half).wait_recv()
            k = self.at(path, 1)
            add_into(self.m2.at[path, 0], (self.m2.at[path, 1], self.m1.at[path, 0, k]), 64, 16)
        self.last_copy().start()

    def finish(self, out):
        self.last_copy().wait_recv()
        out[...] = self.m2[self.yh, 0].astype(F32) + self.last[...].astype(F32)
        for path in (0, 1):
            for side in (0, 1):
                self.transit_one(path, side).wait_send()
                self.transit_two(path, side).wait_send()
                for half in (0, 1):
                    self.main_one(path, side, half).wait_send()
                    self.main_two(path, side, half).wait_send()
        self.last_copy().wait_send()


def sum_buffers(width):
    return [
        pltpu.VMEM((2, 2, 2, 64, width), BF16),
        pltpu.VMEM((2, 2, 4, 64, width), BF16),
        pltpu.VMEM((2, 2, 32, width), BF16),
        pltpu.VMEM((2, 2, 64, width), BF16),
        pltpu.VMEM((64, width), BF16),
        pltpu.SemaphoreType.DMA((2, 13)),
        pltpu.SemaphoreType.DMA((2, 13)),
    ]


def sum_neighbours():
    x, yh, z, yl, core = place()
    return (
        device((x + 1) % 4, yh, z, yl, core),
        device((x + 3) % 4, yh, z, yl, core),
        device(x, yh, (z + 1) % 4, yl, core),
        device(x, yh, (z + 3) % 4, yl, core),
        device(x, 1 - yh, z, yl, core),
    )


def weights_kernel(n, *refs):
    grads, outs, scratch = refs[:n], refs[n : 2 * n], refs[2 * n :]
    greet(sum_neighbours())
    units = [
        RowSum(grads[i], scratch[7 * i : 7 * i + 5], scratch[7 * i + 5], scratch[7 * i + 6])
        for i in range(n)
    ]
    for u in units:
        u.start_one()
    for u in units:
        u.pass_one()
    for u in units:
        u.join_one()
    for u in units:
        u.pass_two()
    for u in units:
        u.join_two()
    for u, out in zip(units, outs):
        u.finish(out)


def sum_weights(grads):
    n = len(grads)
    grads = [g.reshape(4, 2, 4, 64, g.shape[-1]) for g in grads]
    return pl.pallas_call(
        functools.partial(weights_kernel, n),
        out_shape=[jax.ShapeDtypeStruct((64, g.shape[-1]), F32) for g in grads],
        in_specs=[pl.BlockSpec(memory_space=pltpu.VMEM)] * n,
        out_specs=[pl.BlockSpec(memory_space=pltpu.VMEM)] * n,
        scratch_shapes=[b for g in grads for b in sum_buffers(g.shape[-1])],
        compiler_params=pltpu.CompilerParams(
            collective_id=2, has_side_effects=True, vmem_limit_bytes=60 << 20
        ),
        name="sum_weights",
    )(*grads)


def rms_scale(values, gain_vec):
    return (
        values * lax.rsqrt(jnp.mean(values * values, axis=-1, keepdims=True) + norm_eps) * gain_vec
    )


def norm_back(values, gain_vec, grad_in):
    inverse = lax.rsqrt(jnp.mean(values * values, axis=-1, keepdims=True) + norm_eps)
    unit_rows = values * inverse
    d_unit = grad_in * gain_vec
    d_values = inverse * (d_unit - unit_rows * jnp.mean(d_unit * unit_rows, axis=-1, keepdims=True))
    return (d_values, jnp.sum(grad_in * unit_rows, axis=0))


def doc_numbers(lengths, seq_len):
    doc_ends = jnp.cumsum(lengths[0])
    positions = jnp.arange(seq_len, dtype=jnp.int32)
    return jnp.sum((positions[:, None] >= doc_ends[None, :]).astype(jnp.int32), axis=1)


def block_scores(q_block, key_rows, blk_start, doc_ids):
    blk_size = q_block.shape[1]
    seq_len = key_rows.shape[0]
    raw_score = jnp.einsum("htf,shf->hts", q_block, key_rows, preferred_element_type=jnp.float32)
    rows_at = blk_start + jnp.arange(blk_size, dtype=jnp.int32)
    cols_at = jnp.arange(seq_len, dtype=jnp.int32)
    causal = (rows_at[:, None] >= cols_at[None, :]) & (doc_ids[:, None] == doc_ids[None, :])
    window = causal & (rows_at[:, None] - cols_at[None, :] < WINDOW)
    feat_scale = FEAT ** (-0.5)
    kernel = jnp.where(
        causal[None], 1.0 + raw_score * feat_scale + raw_score * raw_score * (0.5 / FEAT), 0.0
    )
    scores = jnp.where(window[None], raw_score * feat_scale, masked_score)
    return (raw_score, kernel, scores, causal)


def mixer_block(q_block, blk_start, key_rows, value_rows, doc_ids):
    raw_score, kernel, scores, causal = block_scores(q_block, key_rows, blk_start, doc_ids)
    denominator = jnp.sum(kernel, axis=2)
    numerator = jnp.einsum(
        "hts,shv->htv", kernel.astype(jnp.bfloat16), value_rows, preferred_element_type=jnp.float32
    )
    row_top = jnp.max(scores, axis=2, keepdims=True)
    weights = jnp.exp(scores - row_top)
    row_total = jnp.sum(weights, axis=2, keepdims=True)
    probs_low = (weights / row_total).astype(jnp.bfloat16)
    windowed = jnp.einsum("hts,shv->htv", probs_low, value_rows, preferred_element_type=jnp.float32)
    mixed_out = (numerator / denominator[:, :, None] + windowed).astype(jnp.bfloat16)
    return (mixed_out, denominator, (row_top + jnp.log(row_total))[:, :, 0])


def mixer_block_back(carry, inputs, key_rows, value_rows, doc_ids):
    d_keys, d_values = carry
    q_block, blk_start, d_block, denominator, log_total = inputs
    raw_score, kernel, scores, causal = block_scores(q_block, key_rows, blk_start, doc_ids)
    feat_scale = FEAT ** (-0.5)
    kernel_low = kernel.astype(jnp.bfloat16)
    numerator = jnp.einsum(
        "hts,shv->htv", kernel_low, value_rows, preferred_element_type=jnp.float32
    )
    linear = numerator / denominator[:, :, None]
    probs = jnp.exp(scores - log_total[:, :, None])
    d_mix = d_block.astype(jnp.float32)
    d_numer = (d_mix / denominator[:, :, None]).astype(jnp.bfloat16)
    d_denom = -jnp.sum(d_mix * linear, axis=2) / denominator
    d_kernel = (
        jnp.einsum("htv,shv->hts", d_numer, value_rows, preferred_element_type=jnp.float32)
        + d_denom[:, :, None]
    )
    d_probs = jnp.einsum("htv,shv->hts", d_block, value_rows, preferred_element_type=jnp.float32)
    d_scores = probs * (d_probs - jnp.sum(d_probs * probs, axis=2, keepdims=True))
    d_raw = (
        jnp.where(causal[None], d_kernel * (feat_scale + raw_score / FEAT), 0.0)
        + d_scores * feat_scale
    )
    d_raw_low = d_raw.astype(jnp.bfloat16)
    d_query = jnp.einsum(
        "hts,shf->htf", d_raw_low, key_rows, preferred_element_type=jnp.float32
    ).astype(jnp.bfloat16)
    d_keys = d_keys + jnp.einsum(
        "hts,htf->shf", d_raw_low, q_block, preferred_element_type=jnp.float32
    )
    d_values = d_values + jnp.einsum(
        "hts,htv->shv", kernel_low, d_numer, preferred_element_type=jnp.float32
    )
    d_values = d_values + jnp.einsum(
        "hts,htv->shv", probs.astype(jnp.bfloat16), d_block, preferred_element_type=jnp.float32
    )
    return ((d_keys, d_values), d_query)


def on_device(
    block_input,
    lengths,
    gain_attn,
    gain_ffn,
    w_query,
    w_key,
    w_value,
    w_out,
    w_gate,
    w_up,
    w_down,
    cotangent,
):
    model_width = block_input.shape[-1]
    own_rows = block_input.reshape(-1, model_width).astype(jnp.float32)
    tok_count = own_rows.shape[0]
    heads_here = w_query.shape[1] // FEAT
    normed = rms_scale(own_rows, gain_attn).astype(jnp.bfloat16)
    gathered = gather_rows(normed)
    seq_len = gathered.shape[0]
    blk_size = min(512, seq_len)
    blk_count = seq_len // blk_size
    query = jnp.dot(gathered, w_query, preferred_element_type=jnp.float32).astype(jnp.bfloat16)
    key_rows = (
        jnp.dot(gathered, w_key, preferred_element_type=jnp.float32)
        .astype(jnp.bfloat16)
        .reshape(seq_len, heads_here, FEAT)
    )
    value_rows = (
        jnp.dot(gathered, w_value, preferred_element_type=jnp.float32)
        .astype(jnp.bfloat16)
        .reshape(seq_len, heads_here, VDIM)
    )
    doc_ids = doc_numbers(lengths, seq_len)
    q_blocks = jnp.transpose(query.reshape(blk_count, blk_size, heads_here, FEAT), (0, 2, 1, 3))
    blk_starts = jnp.arange(blk_count, dtype=jnp.int32) * blk_size

    def forward_block(packed):
        return mixer_block(packed[0], packed[1], key_rows, value_rows, doc_ids)

    mixed_blocks, den_blocks, lse_blocks = lax.map(forward_block, (q_blocks, blk_starts))
    mixed_flat = jnp.transpose(mixed_blocks, (0, 2, 1, 3)).reshape(seq_len, heads_here * VDIM)
    attn_out = scatter_rows(jnp.dot(mixed_flat, w_out, preferred_element_type=jnp.float32))
    hidden_one = own_rows + attn_out
    normed_two = rms_scale(hidden_one, gain_ffn).astype(jnp.bfloat16)
    gathered_two = gather_rows(normed_two)
    gate_pre = jnp.dot(gathered_two, w_gate, preferred_element_type=jnp.float32)
    up_pre = jnp.dot(gathered_two, w_up, preferred_element_type=jnp.float32)
    gate_sig = jax.nn.sigmoid(gate_pre)
    gate_silu = gate_pre * gate_sig
    act_low = (gate_silu * up_pre).astype(jnp.bfloat16)
    ffn_out = scatter_rows(jnp.dot(act_low, w_down, preferred_element_type=jnp.float32))
    block_output = (hidden_one + ffn_out).astype(jnp.bfloat16).reshape(block_input.shape)
    grad_own = cotangent.reshape(tok_count, model_width)
    grad_all = gather_rows(grad_own)
    d_act = jnp.einsum("td,fd->tf", grad_all, w_down, preferred_element_type=jnp.float32)
    d_gate = (d_act * up_pre * (gate_sig * (1.0 + gate_pre * (1.0 - gate_sig)))).astype(
        jnp.bfloat16
    )
    d_up = (d_act * gate_silu).astype(jnp.bfloat16)
    down_part = jnp.einsum("td,tf->df", grad_all, act_low, preferred_element_type=jnp.float32)
    gate_part = jnp.einsum("td,tf->df", gathered_two, d_gate, preferred_element_type=jnp.float32)
    up_part = jnp.einsum("td,tf->df", gathered_two, d_up, preferred_element_type=jnp.float32)
    d_normed_two = scatter_rows(
        jnp.einsum("tf,df->td", d_gate, w_gate, preferred_element_type=jnp.float32)
        + jnp.einsum("tf,df->td", d_up, w_up, preferred_element_type=jnp.float32)
    )
    d_from_norm, d_gain_ffn = norm_back(hidden_one, gain_ffn, d_normed_two)
    d_hidden = grad_own.astype(jnp.float32) + d_from_norm
    d_attn = d_hidden.astype(jnp.bfloat16)
    d_attn_all = gather_rows(d_attn)
    out_part = jnp.einsum("td,tv->dv", d_attn_all, mixed_flat, preferred_element_type=jnp.float32)
    d_mixed = jnp.einsum("td,vd->tv", d_attn_all, w_out, preferred_element_type=jnp.float32).astype(
        jnp.bfloat16
    )
    d_mixed_blocks = jnp.transpose(
        d_mixed.reshape(blk_count, blk_size, heads_here, VDIM), (0, 2, 1, 3)
    )

    def backward_block(carry, inputs):
        return mixer_block_back(carry, inputs, key_rows, value_rows, doc_ids)

    start_carry = (
        jnp.zeros((seq_len, heads_here, FEAT), jnp.float32),
        jnp.zeros((seq_len, heads_here, VDIM), jnp.float32),
    )
    (d_keys, d_values), d_q_blocks = lax.scan(
        backward_block, start_carry, (q_blocks, blk_starts, d_mixed_blocks, den_blocks, lse_blocks)
    )
    d_query = jnp.transpose(d_q_blocks, (0, 2, 1, 3)).reshape(seq_len, heads_here * FEAT)
    d_key = d_keys.reshape(seq_len, heads_here * FEAT).astype(jnp.bfloat16)
    d_value = d_values.reshape(seq_len, heads_here * VDIM).astype(jnp.bfloat16)
    query_part = jnp.einsum("td,tf->df", gathered, d_query, preferred_element_type=jnp.float32)
    key_part = jnp.einsum("td,tf->df", gathered, d_key, preferred_element_type=jnp.float32)
    value_part = jnp.einsum("td,tf->df", gathered, d_value, preferred_element_type=jnp.float32)
    total_rows = jnp.einsum("tf,df->td", d_query, w_query, preferred_element_type=jnp.float32)
    total_rows = total_rows + jnp.einsum(
        "tf,df->td", d_key, w_key, preferred_element_type=jnp.float32
    )
    d_normed = scatter_rows(
        total_rows + jnp.einsum("tf,df->td", d_value, w_value, preferred_element_type=jnp.float32)
    )
    d_from_input, d_gain_attn = norm_back(own_rows, gain_attn, d_normed)
    grad_input = (d_hidden + d_from_input).reshape(block_input.shape)
    mixer_part = jnp.concatenate(
        [query_part.astype(BF16), key_part.astype(BF16), value_part.astype(BF16)], axis=1
    )
    mixer_summed, out_summed, grad_gate, grad_up, down_summed = sum_weights(
        [
            mixer_part,
            out_part.astype(BF16),
            gate_part.astype(BF16),
            up_part.astype(BF16),
            down_part.astype(BF16),
        ]
    )
    grad_query, grad_key, grad_value = (
        mixer_summed[:, :64],
        mixer_summed[:, 64:128],
        mixer_summed[:, 128:],
    )
    grad_gain_attn, grad_gain_ffn = (
        lax.psum_scatter(d_gain_attn, ("dp", "mp"), scatter_dimension=0, tiled=True),
        lax.psum_scatter(d_gain_ffn, ("dp", "mp"), scatter_dimension=0, tiled=True),
    )
    return (
        block_output,
        grad_input,
        grad_gain_attn,
        grad_gain_ffn,
        grad_query,
        grad_key,
        grad_value,
        out_summed.T,
        grad_gate,
        grad_up,
        down_summed.T,
    )


def solution(mesh):
    return jax.shard_map(
        on_device,
        mesh=mesh,
        in_specs=(
            P("dp", "mp", None),
            P("dp", None),
            P(),
            P(),
            P(None, "mp"),
            P(None, "mp"),
            P(None, "mp"),
            P("mp", None),
            P(None, "mp"),
            P(None, "mp"),
            P("mp", None),
            P("dp", "mp", None),
        ),
        out_specs=(
            P("dp", "mp", None),
            P("dp", "mp", None),
            P(("dp", "mp")),
            P(("dp", "mp")),
            P("dp", "mp"),
            P("dp", "mp"),
            P("dp", "mp"),
            P("mp", "dp"),
            P("dp", "mp"),
            P("dp", "mp"),
            P("mp", "dp"),
        ),
        check_vma=False,
    )
```

```python
import functools

import jax
import jax.numpy as jnp
from jax import lax
from jax.experimental import pallas as pl
from jax.experimental.pallas import tpu as pltpu
from jax.sharding import PartitionSpec as P

MESH = pl.DeviceIdType.MESH
F32 = jnp.float32
BF16 = jnp.bfloat16

FEAT = 16
VDIM = 128
WINDOW = 64


norm_eps = 1e-05
masked_score = -1e30


def place():
    dp, mp = lax.axis_index("dp"), lax.axis_index("mp")
    return dp // 8, (dp // 4) % 2, dp % 4, mp // 2, mp % 2


def device(x, yh, z, yl, core):
    return (x * 8 + yh * 4 + z, yl * 2 + core)


def greet(devices):
    barrier = pltpu.get_barrier_semaphore()
    for target in devices:
        pl.semaphore_signal(barrier, inc=1, device_id=target, device_id_type=MESH)
    pl.semaphore_wait(barrier, len(devices))


def remote(src, dst, send_sem, recv_sem, target):
    return pltpu.make_async_remote_copy(
        src_ref=src,
        dst_ref=dst,
        send_sem=send_sem,
        recv_sem=recv_sem,
        device_id=target,
        device_id_type=MESH,
    )


PARTS = 4


def gather_kernel(own_ref, full_ref, send, recv):
    x, yh, z, yl, core = place()
    mate, pair = device(x, yh, z, yl, 1 - core), device(x, yh, z, 1 - yl, core)
    tok = own_ref.shape[0]
    piece = tok // PARTS
    greet((mate, pair))
    mine, far = yl * 2 + core, (1 - yl) * 2 + core
    outgoing = []
    for i in range(PARTS):
        copy = remote(
            own_ref.at[pl.ds(i * piece, piece)],
            full_ref.at[pl.ds(pl.multiple_of(mine * tok + i * piece, piece), piece)],
            send.at[i],
            recv.at[i],
            pair,
        )
        copy.start()
        outgoing.append(copy)
    near = remote(
        own_ref,
        full_ref.at[pl.ds(pl.multiple_of(mine * tok, tok), tok)],
        send.at[PARTS],
        recv.at[PARTS],
        mate,
    )
    near.start()
    full_ref[pl.ds(pl.multiple_of(mine * tok, tok), tok), :] = own_ref[...]
    passed = []
    for i in range(PARTS):
        outgoing[i].wait_recv()
        rows = pl.ds(pl.multiple_of(far * tok + i * piece, piece), piece)
        copy = remote(
            full_ref.at[rows],
            full_ref.at[rows],
            send.at[PARTS + 1 + i],
            recv.at[PARTS + 1 + i],
            mate,
        )
        copy.start()
        passed.append(copy)
    near.wait()
    for i in range(PARTS):
        outgoing[i].wait_send()
        passed[i].wait()


def gather_rows(own):
    tok, width = own.shape
    return pl.pallas_call(
        gather_kernel,
        out_shape=jax.ShapeDtypeStruct((4 * tok, width), own.dtype),
        in_specs=[pl.BlockSpec(memory_space=pltpu.VMEM)],
        out_specs=pl.BlockSpec(memory_space=pltpu.VMEM),
        scratch_shapes=[
            pltpu.SemaphoreType.DMA((2 * PARTS + 1,)),
            pltpu.SemaphoreType.DMA((2 * PARTS + 1,)),
        ],
        compiler_params=pltpu.CompilerParams(
            collective_id=0, has_side_effects=True, vmem_limit_bytes=32 << 20
        ),
        name="gather_rows",
    )(own)


def scatter_kernel(part_ref, out_ref, near_out, near_in, far_out, far_in, send, recv):
    x, yh, z, yl, core = place()
    mate, pair = device(x, yh, z, yl, 1 - core), device(x, yh, z, 1 - yl, core)
    tok = out_ref.shape[0]
    piece = tok // PARTS
    greet((mate, pair))
    near_copies = []
    for k, side in enumerate((1 - yl, yl)):
        start = pl.multiple_of((side * 2 + 1 - core) * tok, tok)
        near_out[k] = part_ref[pl.ds(start, tok), :].astype(BF16)
        copy = remote(near_out.at[k], near_in.at[k], send.at[k], recv.at[k], mate)
        copy.start()
        near_copies.append(copy)
    near_copies[0].wait_recv()
    far_copies = []
    far_start = pl.multiple_of(((1 - yl) * 2 + core) * tok, tok)
    for i in range(PARTS):
        rows = pl.ds(i * piece, piece)
        far_out[rows] = (
            part_ref[pl.ds(far_start + i * piece, piece), :] + near_in[0, rows].astype(F32)
        ).astype(BF16)
        copy = remote(far_out.at[rows], far_in.at[rows], send.at[2 + i], recv.at[2 + i], pair)
        copy.start()
        far_copies.append(copy)
    near_copies[1].wait_recv()
    own_start = pl.multiple_of((yl * 2 + core) * tok, tok)
    for i in range(PARTS):
        rows = pl.ds(i * piece, piece)
        far_copies[i].wait_recv()
        out_ref[rows, :] = (
            part_ref[pl.ds(own_start + i * piece, piece), :]
            + near_in[1, rows].astype(F32)
            + far_in[rows].astype(F32)
        )
    for copy in near_copies + far_copies:
        copy.wait_send()


def scatter_rows(part):
    rows, width = part.shape
    tok = rows // 4
    return pl.pallas_call(
        scatter_kernel,
        out_shape=jax.ShapeDtypeStruct((tok, width), F32),
        in_specs=[pl.BlockSpec(memory_space=pltpu.VMEM)],
        out_specs=pl.BlockSpec(memory_space=pltpu.VMEM),
        scratch_shapes=[
            pltpu.VMEM((2, tok, width), BF16),
            pltpu.VMEM((2, tok, width), BF16),
            pltpu.VMEM((tok, width), BF16),
            pltpu.VMEM((tok, width), BF16),
            pltpu.SemaphoreType.DMA((2 + PARTS,)),
            pltpu.SemaphoreType.DMA((2 + PARTS,)),
        ],
        compiler_params=pltpu.CompilerParams(
            collective_id=1, has_side_effects=True, vmem_limit_bytes=48 << 20
        ),
        name="scatter_rows",
    )(part)


def add_into(dst, terms, rows, step):
    def body(i, _):
        at = pl.ds(pl.multiple_of(i * step, step), step)
        total = dst[at, :].astype(F32)
        for term in terms:
            total = total + term[at, :].astype(F32)
        dst[at, :] = total.astype(dst.dtype)
        return 0

    lax.fori_loop(0, rows // step, body, 0)


class RowSum:
    def __init__(self, grad, bufs, send, recv):
        self.grad = grad
        self.t1, self.m1, self.t2, self.m2, self.last = bufs
        self.send, self.recv = send, recv
        self.x, self.yh, self.z, self.yl, self.core = place()

    def near(self, path, stage, step):
        if (path == 0) == (stage == 0):
            return device((self.x + step + 4) % 4, self.yh, self.z, self.yl, self.core)
        return device(self.x, self.yh, (self.z + step + 4) % 4, self.yl, self.core)

    def at(self, path, stage):
        return self.x if (path == 0) == (stage == 0) else self.z

    def block(self, path, b, k):
        return self.grad.at[b, 0, k] if path == 0 else self.grad.at[k, 1, b]

    def copy(self, src, dst, path, slot, target):
        return remote(src, dst, self.send.at[path, slot], self.recv.at[path, slot], target)

    def transit_one(self, path, side):
        b = (self.at(path, 0) + 2) % 4
        return self.copy(
            self.block(path, b, pl.ds(2 * side, 2)),
            self.t1.at[path, side],
            path,
            side,
            self.near(path, 0, 1 - 2 * side),
        )

    def main_one(self, path, side, half):
        step = 1 - 2 * side
        b = (self.at(path, 0) + step + 4) % 4
        src = (
            self.t1.at[path, side]
            if half == side
            else self.block(path, b, pl.ds(2 * half, 2))
        )
        return self.copy(
            src,
            self.m1.at[path, side, pl.ds(2 * half, 2)],
            path,
            2 + 2 * side + half,
            self.near(path, 0, step),
        )

    def transit_two(self, path, side):
        k = (self.at(path, 1) + 2) % 4
        return self.copy(
            self.m1.at[path, 0, k, pl.ds(32 * side, 32)],
            self.t2.at[path, side],
            path,
            6 + side,
            self.near(path, 1, 1 - 2 * side),
        )

    def main_two(self, path, side, half):
        step = 1 - 2 * side
        k = (self.at(path, 1) + step + 4) % 4
        rows = pl.ds(32 * half, 32)
        src = self.t2.at[path, side] if half == side else self.m1.at[path, 0, k, rows]
        return self.copy(
            src,
            self.m2.at[path, side, rows],
            path,
            8 + 2 * side + half,
            self.near(path, 1, step),
        )

    def last_copy(self):
        target = device(self.x, 1 - self.yh, self.z, self.yl, self.core)
        return self.copy(self.m2.at[1 - self.yh, 0], self.last, 0, 12, target)

    def start_one(self):
        for path in (0, 1):
            for side in (0, 1):
                self.transit_one(path, side).start()
        for path in (0, 1):
            for side in (0, 1):
                self.main_one(path, side, 1 - side).start()

    def pass_one(self):
        for path in (0, 1):
            for side in (0, 1):
                self.transit_one(path, side).wait_recv()
                b = (self.at(path, 0) + 1 - 2 * side + 4) % 4
                for k in (0, 1):
                    add_into(
                        self.t1.at[path, side, k],
                        (self.block(path, b, 2 * side + k),),
                        64,
                        16,
                    )
                self.main_one(path, side, side).start()

    def join_one(self):
        for path in (0, 1):
            for side in (0, 1):
                for half in (0, 1):
                    self.main_one(path, side, half).wait_recv()
            b = self.at(path, 0)

            def body(k, _):
                add_into(
                    self.m1.at[path, 0, k],
                    (self.m1.at[path, 1, k], self.block(path, b, k)),
                    64,
                    16,
                )
                return 0

            lax.fori_loop(0, 4, body, 0)
            for side in (0, 1):
                self.transit_two(path, side).start()
            for side in (0, 1):
                self.main_two(path, side, 1 - side).start()

    def pass_two(self):
        for path in (0, 1):
            for side in (0, 1):
                self.transit_two(path, side).wait_recv()
                k = (self.at(path, 1) + 1 - 2 * side + 4) % 4
                add_into(
                    self.t2.at[path, side],
                    (self.m1.at[path, 0, k, pl.ds(32 * side, 32)],),
                    32,
                    16,
                )
                self.main_two(path, side, side).start()

    def join_two(self):
        for path in (0, 1):
            for side in (0, 1):
                for half in (0, 1):
                    self.main_two(path, side, half).wait_recv()
            k = self.at(path, 1)
            add_into(self.m2.at[path, 0], (self.m2.at[path, 1], self.m1.at[path, 0, k]), 64, 16)
        self.last_copy().start()

    def finish(self, use):
        self.last_copy().wait_recv()
        use(self.m2[self.yh, 0].astype(F32) + self.last[...].astype(F32))
        for path in (0, 1):
            for side in (0, 1):
                self.transit_one(path, side).wait_send()
                self.transit_two(path, side).wait_send()
                for half in (0, 1):
                    self.main_one(path, side, half).wait_send()
                    self.main_two(path, side, half).wait_send()
        self.last_copy().wait_send()


def sum_buffers(width):
    return [
        pltpu.VMEM((2, 2, 2, 64, width), BF16),
        pltpu.VMEM((2, 2, 4, 64, width), BF16),
        pltpu.VMEM((2, 2, 32, width), BF16),
        pltpu.VMEM((2, 2, 64, width), BF16),
        pltpu.VMEM((64, width), BF16),
        pltpu.SemaphoreType.DMA((2, 13)),
        pltpu.SemaphoreType.DMA((2, 13)),
    ]


def sum_neighbours():
    x, yh, z, yl, core = place()
    return (
        device((x + 1) % 4, yh, z, yl, core),
        device((x + 3) % 4, yh, z, yl, core),
        device(x, yh, (z + 1) % 4, yl, core),
        device(x, yh, (z + 3) % 4, yl, core),
        device(x, 1 - yh, z, yl, core),
    )


SETS = 3
FF_TILE = 256


def dot_nn(a, b):
    return lax.dot_general(a, b, (((1,), (0,)), ((), ())), preferred_element_type=F32)


def dot_nt(a, b):
    return lax.dot_general(a, b, (((1,), (1,)), ((), ())), preferred_element_type=F32)


def dot_tn(a, b):
    return lax.dot_general(a, b, (((0,), (0,)), ((), ())), preferred_element_type=F32)


def each(count, step, body):
    def run(i, _):
        body(pl.ds(pl.multiple_of(i * step, step), step))
        return 0

    lax.fori_loop(0, count // step, run, 0)


class Gather:
    def __init__(self, own, full, send, recv):
        self.own, self.full, self.send, self.recv = own, full, send, recv
        x, yh, z, yl, core = place()
        self.mate, self.pair = device(x, yh, z, yl, 1 - core), device(x, yh, z, 1 - yl, core)
        self.tok = own.shape[0]
        self.piece = self.tok // PARTS
        self.mine, self.far = yl * 2 + core, (1 - yl) * 2 + core

    def rows(self, part, i):
        start = part * self.tok + i * self.piece
        return pl.ds(pl.multiple_of(start, self.piece), self.piece)

    def far_copy(self, i):
        return remote(
            self.own.at[pl.ds(i * self.piece, self.piece)],
            self.full.at[self.rows(self.mine, i)],
            self.send.at[i],
            self.recv.at[i],
            self.pair,
        )

    def near_copy(self):
        return remote(
            self.own,
            self.full.at[pl.ds(pl.multiple_of(self.mine * self.tok, self.tok), self.tok)],
            self.send.at[PARTS],
            self.recv.at[PARTS],
            self.mate,
        )

    def pass_copy(self, i):
        rows = self.rows(self.far, i)
        return remote(
            self.full.at[rows],
            self.full.at[rows],
            self.send.at[PARTS + 1 + i],
            self.recv.at[PARTS + 1 + i],
            self.mate,
        )

    def start(self):
        for i in range(PARTS):
            self.far_copy(i).start()
        self.near_copy().start()
        at = pl.ds(pl.multiple_of(self.mine * self.tok, self.tok), self.tok)
        self.full[at, :] = self.own[...]

    def finish(self):
        for i in range(PARTS):
            self.far_copy(i).wait_recv()
            self.pass_copy(i).start()
        self.near_copy().wait()
        for i in range(PARTS):
            self.far_copy(i).wait_send()
            self.pass_copy(i).wait()


class Scatter:
    def __init__(self, part, bufs, send, recv):
        self.part = part
        self.near_out, self.near_in, self.far_out, self.far_in = bufs
        self.send, self.recv = send, recv
        x, yh, z, yl, core = place()
        self.yl, self.core = yl, core
        self.mate, self.pair = device(x, yh, z, yl, 1 - core), device(x, yh, z, 1 - yl, core)
        self.tok = self.far_in.shape[0]
        self.piece = self.tok // PARTS

    def near_copy(self, k):
        return remote(
            self.near_out.at[k], self.near_in.at[k], self.send.at[k], self.recv.at[k], self.mate
        )

    def far_copy(self, i):
        rows = pl.ds(i * self.piece, self.piece)
        return remote(
            self.far_out.at[rows],
            self.far_in.at[rows],
            self.send.at[2 + i],
            self.recv.at[2 + i],
            self.pair,
        )

    def start(self):
        for k, side in enumerate((1 - self.yl, self.yl)):
            start = pl.multiple_of((side * 2 + 1 - self.core) * self.tok, self.tok)

            def cast(rows, k=k, start=start):
                self.near_out[k, rows, :] = self.part[
                    pl.ds(pl.multiple_of(start + rows.start, 16), 16), :
                ].astype(BF16)

            each(self.tok, 16, cast)
            self.near_copy(k).start()
        self.near_copy(0).wait_recv()
        far = pl.multiple_of(((1 - self.yl) * 2 + self.core) * self.tok, self.tok)
        for i in range(PARTS):

            def join(rows, i=i):
                at = pl.ds(pl.multiple_of(i * self.piece + rows.start, 16), 16)
                src = pl.ds(pl.multiple_of(far + i * self.piece + rows.start, 16), 16)
                self.far_out[at, :] = (
                    self.part[src, :] + self.near_in[0, at, :].astype(F32)
                ).astype(BF16)

            each(self.piece, 16, join)
            self.far_copy(i).start()

    def finish(self, use):
        self.near_copy(1).wait_recv()
        own = pl.multiple_of((self.yl * 2 + self.core) * self.tok, self.tok)
        for i in range(PARTS):
            self.far_copy(i).wait_recv()

            def join(rows, i=i):
                at = pl.ds(pl.multiple_of(i * self.piece + rows.start, 16), 16)
                src = pl.ds(pl.multiple_of(own + i * self.piece + rows.start, 16), 16)
                use(
                    at,
                    self.part[src, :]
                    + self.near_in[1, at, :].astype(F32)
                    + self.far_in[at, :].astype(F32),
                )

            each(self.piece, 16, join)
        for k in (0, 1):
            self.near_copy(k).wait_send()
        for i in range(PARTS):
            self.far_copy(i).wait_send()


class Pump:
    def __init__(self, grads, sets, sends, recvs, credit):
        self.grads, self.sets, self.sends, self.recvs, self.credit = (
            grads,
            sets,
            sends,
            recvs,
            credit,
        )
        self.queue, self.flight, self.begun, self.total = [], [], 0, 0

    def add(self, width, fill, done):
        self.queue.append((width, fill, done))

    def begin(self):
        if not self.queue or len(self.flight) >= SETS:
            return False
        width, fill, done = self.queue.pop(0)
        slot = self.begun % SETS
        lanes = pl.ds(0, width)
        grad = self.grads[slot]
        view = lambda ref: ref.at[tuple([slice(None)] * (len(ref.shape) - 1) + [lanes])]
        unit = RowSum(
            view(grad), [view(b) for b in self.sets[slot]], self.sends.at[slot], self.recvs.at[slot]
        )
        fill(grad)
        if self.begun >= SETS:
            pl.semaphore_wait(self.credit.at[slot], 5)
        unit.start_one()
        stages = [unit.pass_one, unit.join_one, unit.pass_two, unit.join_two]
        self.flight.append((stages, unit, slot, self.begun, done))
        self.begun += 1
        return True

    def advance(self, entry):
        stages, unit, slot, index, done = entry
        if stages:
            stages.pop(0)()
            return
        unit.finish(done)
        self.flight.remove(entry)
        if index + SETS < self.total:
            for target in sum_neighbours():
                pl.semaphore_signal(
                    self.credit.at[slot], inc=1, device_id=target, device_id_type=MESH
                )

    def step(self):
        for entry in list(self.flight):
            self.advance(entry)
        self.begin()

    def drain(self):
        while self.flight or self.queue:
            self.step()


def norm_rows(values):
    return lax.rsqrt(jnp.mean(values * values, axis=-1, keepdims=True) + norm_eps)


def doc_of(positions, ends):
    return sum((positions >= e).astype(jnp.int32) for e in ends)


def pair_weights(raw, t0, ends):
    rows, cols = raw.shape
    t = t0 + lax.broadcasted_iota(jnp.int32, (rows, 1), 0)
    s = lax.broadcasted_iota(jnp.int32, (1, cols), 1)
    causal = (t >= s) & (doc_of(t, ends) == doc_of(s, ends))
    window = causal & (t - s < WINDOW)
    scaled = raw * (FEAT ** (-0.5))
    kernel = jnp.where(causal, 1.0 + scaled + 0.5 * scaled * scaled, 0.0)
    inv_den = 1.0 / jnp.sum(kernel, axis=1, keepdims=True)
    scores = jnp.where(window, scaled, masked_score)
    weights = jnp.exp(scores - jnp.max(scores, axis=1, keepdims=True))
    probs = weights * (1.0 / jnp.sum(weights, axis=1, keepdims=True))
    return scaled, kernel, inv_den, probs, causal


def back_kernel(
    lengths,
    n2_own,
    g_all,
    g_own,
    h1,
    x_own,
    q_ref,
    k_ref,
    v_ref,
    mixed,
    gain_attn,
    gain_ffn,
    normed_hbm,
    wq_hbm,
    wk_hbm,
    wv_hbm,
    wo_hbm,
    wg_hbm,
    wu_hbm,
    wd_hbm,
    block_out,
    grad_in,
    gains_out,
    o_query,
    o_key,
    o_value,
    o_out,
    o_gate,
    o_up,
    o_down,
    n2,
    da_all,
    da_own,
    dhid,
    w_gu,
    w_d,
    wg_last,
    wu_last,
    wq,
    wk,
    wo,
    rows_gu,
    rows_qk,
    rows_v,
    acc,
    acts,
    dgus,
    act_last,
    dgu_last,
    gu,
    da,
    dmixed,
    dqkv,
    gsum,
    gnear,
    gfar,
    near_out,
    near_in,
    far_out,
    far_in,
    near_in2,
    far_in2,
    grad0,
    grad1,
    grad2,
    *rest,
):
    sets = [rest[5 * i : 5 * i + 5] for i in range(SETS)]
    sends, recvs, credit, mp_send, mp_recv, wsem = rest[5 * SETS :]
    x, yh, z, yl, core = place()
    dp = lax.axis_index("dp")
    mate, pair = device(x, yh, z, yl, 1 - core), device(x, yh, z, 1 - yl, core)
    ff = wg_hbm.shape[1]
    full_tiles = ff // FF_TILE
    last = ff - full_tiles * FF_TILE
    pad = act_last.shape[1]
    order = [full_tiles] + list(range(full_tiles))
    ends = [lengths[0, 0], lengths[0, 0] + lengths[0, 1]]
    ends.append(ends[1] + lengths[0, 2])

    def load(src, dst, i):
        return pltpu.make_async_copy(src, dst, wsem.at[i])

    def tile_loads(i):
        t = order[i]
        cols = pl.ds(t * FF_TILE, FF_TILE)
        if t == full_tiles:
            cols = pl.ds(t * FF_TILE, last)
            return [
                load(wg_hbm.at[:, cols], wg_last, 0),
                load(wu_hbm.at[:, cols], wu_last, 1),
                load(wd_hbm.at[cols], w_d.at[0, pl.ds(0, last)], 2),
            ]
        s = i % 2
        return [
            load(wg_hbm.at[:, cols], w_gu.at[s, :, pl.ds(0, FF_TILE)], 3 * s),
            load(wu_hbm.at[:, cols], w_gu.at[s, :, pl.ds(FF_TILE, FF_TILE)], 3 * s + 1),
            load(wd_hbm.at[cols], w_d.at[s], 3 * s + 2),
        ]

    own_rows = pl.ds(pl.multiple_of(dp * 64, 64), 64)
    small = [
        load(wq_hbm, wq, 6),
        load(wk_hbm, wk, 7),
        load(wo_hbm, wo, 8),
        load(wg_hbm.at[own_rows], rows_gu.at[0], 9),
        load(wu_hbm.at[own_rows], rows_gu.at[1], 10),
        load(wq_hbm.at[own_rows], rows_qk.at[0], 11),
        load(wk_hbm.at[own_rows], rows_qk.at[1], 12),
        load(wv_hbm.at[own_rows], rows_v, 13),
    ]
    for i in (0, 1):
        for c in tile_loads(i):
            c.start()
    greet(sum_neighbours() + (mate, pair))
    gather_two = Gather(n2_own, n2, mp_send.at[0], mp_recv.at[0])
    gather_two.start()
    for c in small:
        c.start()
    gather_two.finish()
    for c in small:
        c.wait()

    pump = Pump((grad0, grad1, grad2), sets, sends, recvs, credit)
    pump.total = full_tiles + 3

    def fill_ffn(t):
        def fill(grad):
            def block(b, _):
                lanes = pl.ds(pl.multiple_of(b * 512, 512), 512)
                if t == full_tiles:
                    top = dot_tn(n2[:, lanes], dgu_last[...])
                    bottom = dot_tn(g_all[:, lanes], act_last[...])
                    w = 2 * pad
                else:
                    top = dot_tn(n2[:, lanes], dgus[t])
                    bottom = dot_tn(g_all[:, lanes], acts[t])
                    w = 2 * FF_TILE
                grad[b, :, :, :, 0:w] = top.astype(BF16).reshape(2, 4, 64, w)
                grad[b, :, :, :, w : w + w // 2] = bottom.astype(BF16).reshape(2, 4, 64, w // 2)
                return 0

            lax.fori_loop(0, 4, block, 0)

        return fill

    def done_ffn(t):
        def done(total):
            if t == full_tiles:
                n, p = last, pad
            else:
                n, p = FF_TILE, FF_TILE
            cols = slice(t * FF_TILE, t * FF_TILE + n)
            value_gate, value_up = total[:, 0:n], total[:, p : p + n]
            o_gate[:, cols] = value_gate
            o_up[:, cols] = value_up
            o_down[:, cols] = total[:, 2 * p : 2 * p + n]
            part = value_gate * rows_gu[0, :, cols].astype(F32) + value_up * rows_gu[
                1, :, cols
            ].astype(F32)
            column = jnp.sum(part, axis=1, keepdims=True)
            if t == full_tiles:
                gsum[0] = jnp.broadcast_to(column, gsum.shape[1:])
            else:
                gsum[0] += jnp.broadcast_to(column, gsum.shape[1:])

        return done

    for i, t in enumerate(order):
        for c in tile_loads(i):
            c.wait()
        s = i % 2
        if t == full_tiles:
            n = last

            def forward(rows):
                gu[rows, 0:n] = dot_nn(n2[rows, :], wg_last[...])
                gu[rows, FF_TILE : FF_TILE + n] = dot_nn(n2[rows, :], wu_last[...])
                da[rows, 0:n] = dot_nt(g_all[rows, :], w_d[0, 0:n, :])

        else:
            n = FF_TILE

            def forward(rows, s=s):
                gu[rows, :] = dot_nn(n2[rows, :], w_gu[s])
                da[rows, 0:FF_TILE] = dot_nt(g_all[rows, :], w_d[s])

        each(n2.shape[0], 256, forward)

        def pointwise(rows, t=t, n=n):
            gate, up, d_act = gu[rows, 0:n], gu[rows, FF_TILE : FF_TILE + n], da[rows, 0:n]
            sig = jax.nn.sigmoid(gate)
            silu = gate * sig
            act = (silu * up).astype(BF16)
            d_gate = (d_act * up * (sig * (1.0 + gate * (1.0 - sig)))).astype(BF16)
            d_up = (d_act * silu).astype(BF16)
            if t == full_tiles:
                zero = jnp.zeros((act.shape[0], pad - n), BF16)
                act_last[rows, 0:n] = act
                act_last[rows, n:pad] = zero
                dgu_last[rows, 0:n] = d_gate
                dgu_last[rows, n:pad] = zero
                dgu_last[rows, pad : pad + n] = d_up
                dgu_last[rows, pad + n : 2 * pad] = zero
            else:
                acts[t, rows, :] = act
                dgus[t, rows, 0:n] = d_gate
                dgus[t, rows, n : 2 * n] = d_up

        each(n2.shape[0], 64, pointwise)

        def back(rows, t=t, s=s, n=n):
            if t == full_tiles:
                acc[rows, :] = dot_nt(dgu_last[rows, 0:n], wg_last[...]) + dot_nt(
                    dgu_last[rows, pad : pad + n], wu_last[...]
                )
            else:
                acc[rows, :] += dot_nt(dgus[t, rows, :], w_gu[s])

        pump.add(3 * (pad if t == full_tiles else FF_TILE), fill_ffn(t), done_ffn(t))
        pump.step()
        each(n2.shape[0], 256, back)
        if i + 2 < len(order):
            for c in tile_loads(i + 2):
                c.start()

    wv = w_gu.at[0]
    load(wv_hbm, wv, 0).start()
    down_order = order

    def down_load(i):
        t = down_order[i]
        n = last if t == full_tiles else FF_TILE
        return load(
            wd_hbm.at[pl.ds(t * FF_TILE, n)], w_d.at[i % 2, pl.ds(0, n)], 14 + i % 2
        )

    down_load(0).start()
    down_load(1).start()
    bufs = (near_out, near_in, far_out, far_in)
    scatter_two = Scatter(acc, bufs, mp_send.at[1], mp_recv.at[1])
    scatter_two.start()
    pump.step()

    gain = gain_ffn[...]

    def norm_two_back(rows, d_normed_two):
        hidden = h1[rows, :]
        inverse = norm_rows(hidden)
        unit = hidden * inverse
        e = d_normed_two * gain
        d_hidden = g_own[rows, :].astype(F32) + inverse * (
            e - unit * jnp.mean(e * unit, axis=-1, keepdims=True)
        )
        dhid[rows, :] = d_hidden
        da_own[rows, :] = d_hidden.astype(BF16)

    scatter_two.finish(norm_two_back)
    gather_attn = Gather(da_own, da_all, mp_send.at[2], mp_recv.at[2])
    gather_attn.start()
    pump.step()

    for i, t in enumerate(down_order):
        down_load(i).wait()
        n = last if t == full_tiles else FF_TILE

        def down(rows, i=i, t=t, n=n):
            if t == full_tiles:
                acc[rows, :] = dot_nn(act_last[rows, 0:n], w_d[i % 2, 0:n, :])
            else:
                acc[rows, :] += dot_nn(acts[t, rows, :], w_d[i % 2])

        each(n2.shape[0], 256, down)
        if i + 2 < len(down_order):
            down_load(i + 2).start()
        if i == 2:
            pump.step()
    gather_attn.finish()
    scatter_out = Scatter(acc, (near_out, near_in2, far_out, far_in2), mp_send.at[3], mp_recv.at[3])
    scatter_out.start()

    def mix_back(rows):
        dmixed[rows, :] = dot_nt(da_all[rows, :], wo[...]).astype(BF16)

    each(n2.shape[0], 256, mix_back)

    def fill_out(grad):
        def block(b, _):
            lanes = pl.ds(pl.multiple_of(b * 512, 512), 512)
            top = dot_tn(da_all[:, lanes], mixed[...])
            grad[b, :, :, :, 0:512] = top.astype(BF16).reshape(2, 4, 64, 512)
            return 0

        lax.fori_loop(0, 4, block, 0)

    def done_out(total):
        o_out[...] = total

    pump.add(512, fill_out, done_out)
    pump.step()

    heads = v_ref.shape[1] // VDIM
    for h in range(heads):
        qh, kh = q_ref[:, h * FEAT : (h + 1) * FEAT], k_ref[:, h * FEAT : (h + 1) * FEAT]
        vcols = slice(h * VDIM, (h + 1) * VDIM)
        raw_s, probs_s, d_raw_s, mass_s = gu, da, dgus.at[0], dgus.at[1]
        raw_s[...] = dot_nt(qh, kh)
        probs_s[...] = dot_nt(dmixed[:, vcols], v_ref[:, vcols])

        def attend(rows):
            scaled, kernel, inv_den, probs, causal = pair_weights(raw_s[rows, :], rows.start, ends)
            d_probs = probs_s[rows, :]
            drop = jnp.sum(kernel * d_probs, axis=1, keepdims=True) * inv_den
            d_kernel = (d_probs - drop) * inv_den
            d_scores = probs * (d_probs - jnp.sum(probs * d_probs, axis=1, keepdims=True))
            d_raw = FEAT ** (-0.5) * (
                jnp.where(causal, d_kernel * (1.0 + scaled), 0.0) + d_scores
            )
            d_raw_s[rows, :] = d_raw.astype(BF16)
            mass_s[rows, :] = (kernel * inv_den + probs).astype(BF16)

        each(n2.shape[0], 32, attend)
        dqkv[:, h * FEAT : (h + 1) * FEAT] = dot_nn(d_raw_s[...], kh).astype(BF16)
        dqkv[:, 64 + h * FEAT : 64 + (h + 1) * FEAT] = dot_tn(d_raw_s[...], qh).astype(BF16)
        dqkv[:, 128 + h * VDIM : 128 + (h + 1) * VDIM] = dot_tn(
            mass_s[...], dmixed[:, vcols]
        ).astype(BF16)
        if h == 0:

            def output(rows, total):
                block_out[rows, :] = (h1[rows, :] + total).astype(BF16)

            scatter_out.finish(output)
        if h == 1:
            pump.step()
            assert not pump.queue or pump.queue[0][0] < 768
            load(normed_hbm, n2, 1).start()

    load(wv_hbm, wv, 0).wait()

    def normed_back(rows):
        acc[rows, :] = (
            dot_nt(dqkv[rows, 0:64], wq[...])
            + dot_nt(dqkv[rows, 64:128], wk[...])
            + dot_nt(dqkv[rows, 128:640], wv[...])
        )

    each(n2.shape[0], 256, normed_back)
    scatter_in = Scatter(acc, bufs, mp_send.at[4], mp_recv.at[4])
    scatter_in.start()
    load(normed_hbm, n2, 1).wait()

    def fill_qkv(grad):
        def block(b, _):
            lanes = pl.ds(pl.multiple_of(b * 512, 512), 512)
            top = dot_tn(n2[:, lanes], dqkv[...])
            grad[b, :, :, :, 0:640] = top.astype(BF16).reshape(2, 4, 64, 640)
            return 0

        lax.fori_loop(0, 4, block, 0)

    def done_qkv(total):
        o_query[...] = total[:, 0:64]
        o_key[...] = total[:, 64:128]
        o_value[...] = total[:, 128:640]
        part = jnp.sum(total[:, 0:64] * rows_qk[0].astype(F32), axis=1, keepdims=True)
        part += jnp.sum(total[:, 64:128] * rows_qk[1].astype(F32), axis=1, keepdims=True)
        part += jnp.sum(total[:, 128:640] * rows_v[...].astype(F32), axis=1, keepdims=True)
        gsum[1] = jnp.broadcast_to(part, gsum.shape[1:])

    pump.add(640, fill_qkv, done_qkv)
    pump.step()
    gain_a = gain_attn[...]

    def norm_one_back(rows, d_normed):
        values = x_own[rows, :].astype(F32)
        inverse = norm_rows(values)
        unit = values * inverse
        e = d_normed * gain_a
        grad_in[rows, :] = dhid[rows, :] + inverse * (
            e - unit * jnp.mean(e * unit, axis=-1, keepdims=True)
        )

    pump.step()
    scatter_in.finish(norm_one_back)
    pump.drain()

    near = remote(gsum, gnear, mp_send.at[5, 0], mp_recv.at[5, 0], mate)
    near.start()
    near.wait()
    gsum[...] += gnear[...]
    far = remote(gsum, gfar, mp_send.at[5, 1], mp_recv.at[5, 1], pair)
    far.start()
    far.wait()
    gains_out[...] = gsum[...] + gfar[...]


def backward(lengths, n2_own, g_all, g_own, h1, x_own, q, k, v, mixed, gain_attn, gain_ffn, normed,
             wq, wk, wv, wo, wg, wu, wd):
    tok, width = n2_own.shape
    seq, ff = g_all.shape[0], wg.shape[1]
    full_tiles = ff // FF_TILE
    last = ff - full_tiles * FF_TILE
    pad = -(-last // 128) * 128
    wide = 3 * FF_TILE
    vmem, hbm = pl.BlockSpec(memory_space=pltpu.VMEM), pl.BlockSpec(memory_space=pl.ANY)
    shape = jax.ShapeDtypeStruct
    sems = pltpu.SemaphoreType.DMA
    scratch = [
        pltpu.VMEM((seq, width), BF16),
        pltpu.VMEM((seq, width), BF16),
        pltpu.VMEM((tok, width), BF16),
        pltpu.VMEM((tok, width), F32),
        pltpu.VMEM((2, width, 2 * FF_TILE), BF16),
        pltpu.VMEM((2, FF_TILE, width), BF16),
        pltpu.VMEM((width, last), BF16),
        pltpu.VMEM((width, last), BF16),
        pltpu.VMEM(wq.shape, BF16),
        pltpu.VMEM(wk.shape, BF16),
        pltpu.VMEM(wo.shape, BF16),
        pltpu.VMEM((2, 64, ff), BF16),
        pltpu.VMEM((2, 64, 64), BF16),
        pltpu.VMEM((64, wv.shape[1]), BF16),
        pltpu.VMEM((seq, width), F32),
        pltpu.VMEM((full_tiles, seq, FF_TILE), BF16),
        pltpu.VMEM((full_tiles, seq, 2 * FF_TILE), BF16),
        pltpu.VMEM((seq, pad), BF16),
        pltpu.VMEM((seq, 2 * pad), BF16),
        pltpu.VMEM((seq, 512), F32),
        pltpu.VMEM((seq, 512), F32),
        pltpu.VMEM((seq, 512), BF16),
        pltpu.VMEM((seq, 640), BF16),
        pltpu.VMEM((2, 64, 128), F32),
        pltpu.VMEM((2, 64, 128), F32),
        pltpu.VMEM((2, 64, 128), F32),
        pltpu.VMEM((2, tok, width), BF16),
        pltpu.VMEM((2, tok, width), BF16),
        pltpu.VMEM((tok, width), BF16),
        pltpu.VMEM((tok, width), BF16),
        pltpu.VMEM((2, tok, width), BF16),
        pltpu.VMEM((tok, width), BF16),
    ]
    scratch += [pltpu.VMEM((4, 2, 4, 64, wide), BF16) for _ in range(SETS)]
    scratch += [b for _ in range(SETS) for b in sum_buffers(wide)[:5]]
    scratch += [
        sems((SETS, 2, 13)),
        sems((SETS, 2, 13)),
        pltpu.SemaphoreType.REGULAR((SETS,)),
        sems((6, 2 * PARTS + 1)),
        sems((6, 2 * PARTS + 1)),
        sems((16,)),
    ]
    return pl.pallas_call(
        back_kernel,
        out_shape=[
            shape((tok, width), BF16),
            shape((tok, width), F32),
            shape((2, 64, 128), F32),
            shape((64, wq.shape[1]), F32),
            shape((64, wk.shape[1]), F32),
            shape((64, wv.shape[1]), F32),
            shape((64, wo.shape[0]), F32),
            shape((64, ff), F32),
            shape((64, ff), F32),
            shape((64, ff), F32),
        ],
        in_specs=[pl.BlockSpec(memory_space=pltpu.SMEM)] + [vmem] * 11 + [hbm] * 8,
        out_specs=[vmem] * 10,
        scratch_shapes=scratch,
        compiler_params=pltpu.CompilerParams(
            collective_id=2, has_side_effects=True, vmem_limit_bytes=63 << 20
        ),
        name="backward",
    )(lengths, n2_own, g_all, g_own, h1, x_own, q, k, v, mixed, gain_attn, gain_ffn, normed,
      wq, wk, wv, wo, wg, wu, wd)


def rms_scale(values, gain_vec):
    return (
        values * lax.rsqrt(jnp.mean(values * values, axis=-1, keepdims=True) + norm_eps) * gain_vec
    )


def doc_numbers(lengths, seq_len):
    doc_ends = jnp.cumsum(lengths[0])
    positions = jnp.arange(seq_len, dtype=jnp.int32)
    return jnp.sum((positions[:, None] >= doc_ends[None, :]).astype(jnp.int32), axis=1)


def block_scores(q_block, key_rows, blk_start, doc_ids):
    blk_size = q_block.shape[1]
    seq_len = key_rows.shape[0]
    raw_score = jnp.einsum("htf,shf->hts", q_block, key_rows, preferred_element_type=jnp.float32)
    rows_at = blk_start + jnp.arange(blk_size, dtype=jnp.int32)
    cols_at = jnp.arange(seq_len, dtype=jnp.int32)
    causal = (rows_at[:, None] >= cols_at[None, :]) & (doc_ids[:, None] == doc_ids[None, :])
    window = causal & (rows_at[:, None] - cols_at[None, :] < WINDOW)
    feat_scale = FEAT ** (-0.5)
    kernel = jnp.where(
        causal[None], 1.0 + raw_score * feat_scale + raw_score * raw_score * (0.5 / FEAT), 0.0
    )
    scores = jnp.where(window[None], raw_score * feat_scale, masked_score)
    return (raw_score, kernel, scores, causal)


def mixer_block(q_block, blk_start, key_rows, value_rows, doc_ids):
    raw_score, kernel, scores, causal = block_scores(q_block, key_rows, blk_start, doc_ids)
    denominator = jnp.sum(kernel, axis=2)
    numerator = jnp.einsum(
        "hts,shv->htv", kernel.astype(jnp.bfloat16), value_rows, preferred_element_type=jnp.float32
    )
    row_top = jnp.max(scores, axis=2, keepdims=True)
    weights = jnp.exp(scores - row_top)
    row_total = jnp.sum(weights, axis=2, keepdims=True)
    probs_low = (weights / row_total).astype(jnp.bfloat16)
    windowed = jnp.einsum("hts,shv->htv", probs_low, value_rows, preferred_element_type=jnp.float32)
    mixed_out = (numerator / denominator[:, :, None] + windowed).astype(jnp.bfloat16)
    return (mixed_out, denominator, (row_top + jnp.log(row_total))[:, :, 0])


def on_device(
    block_input,
    lengths,
    gain_attn,
    gain_ffn,
    w_query,
    w_key,
    w_value,
    w_out,
    w_gate,
    w_up,
    w_down,
    cotangent,
):
    model_width = block_input.shape[-1]
    own_rows = block_input.reshape(-1, model_width).astype(jnp.float32)
    tok_count = own_rows.shape[0]
    heads_here = w_query.shape[1] // FEAT
    normed = rms_scale(own_rows, gain_attn).astype(jnp.bfloat16)
    gathered = gather_rows(normed)
    seq_len = gathered.shape[0]
    blk_size = min(512, seq_len)
    blk_count = seq_len // blk_size
    query = jnp.dot(gathered, w_query, preferred_element_type=jnp.float32).astype(jnp.bfloat16)
    key_rows = (
        jnp.dot(gathered, w_key, preferred_element_type=jnp.float32)
        .astype(jnp.bfloat16)
        .reshape(seq_len, heads_here, FEAT)
    )
    value_rows = (
        jnp.dot(gathered, w_value, preferred_element_type=jnp.float32)
        .astype(jnp.bfloat16)
        .reshape(seq_len, heads_here, VDIM)
    )
    doc_ids = doc_numbers(lengths, seq_len)
    q_blocks = jnp.transpose(query.reshape(blk_count, blk_size, heads_here, FEAT), (0, 2, 1, 3))
    blk_starts = jnp.arange(blk_count, dtype=jnp.int32) * blk_size

    def forward_block(packed):
        return mixer_block(packed[0], packed[1], key_rows, value_rows, doc_ids)

    mixed_blocks, den_blocks, lse_blocks = lax.map(forward_block, (q_blocks, blk_starts))
    mixed_flat = jnp.transpose(mixed_blocks, (0, 2, 1, 3)).reshape(seq_len, heads_here * VDIM)
    attn_out = scatter_rows(jnp.dot(mixed_flat, w_out, preferred_element_type=jnp.float32))
    hidden_one = own_rows + attn_out
    normed_two = rms_scale(hidden_one, gain_ffn).astype(jnp.bfloat16)
    grad_own = cotangent.reshape(tok_count, model_width)
    grad_all = gather_rows(grad_own)
    (
        block_output,
        grad_input,
        gains,
        grad_query,
        grad_key,
        grad_value,
        grad_out,
        grad_gate,
        grad_up,
        grad_down,
    ) = backward(
        lengths,
        normed_two,
        grad_all,
        grad_own,
        hidden_one,
        block_input.reshape(-1, model_width),
        query,
        key_rows.reshape(seq_len, -1),
        value_rows.reshape(seq_len, -1),
        mixed_flat,
        gain_attn.reshape(1, -1),
        gain_ffn.reshape(1, -1),
        gathered,
        w_query,
        w_key,
        w_value,
        w_out,
        w_gate,
        w_up,
        w_down,
    )
    dp, mp = lax.axis_index("dp"), lax.axis_index("mp")
    piece = model_width // (lax.axis_size("dp") * lax.axis_size("mp"))
    grad_gain_ffn, grad_gain_attn = (
        lax.dynamic_slice(gains[i, :, 0], (mp * piece,), (piece,))
        / lax.dynamic_slice(gain, (dp * 64 + mp * piece,), (piece,))
        for i, gain in enumerate((gain_ffn, gain_attn))
    )
    return (
        block_output.reshape(block_input.shape),
        grad_input.reshape(block_input.shape),
        grad_gain_attn,
        grad_gain_ffn,
        grad_query,
        grad_key,
        grad_value,
        grad_out.T,
        grad_gate,
        grad_up,
        grad_down.T,
    )


def solution(mesh):
    return jax.shard_map(
        on_device,
        mesh=mesh,
        in_specs=(
            P("dp", "mp", None),
            P("dp", None),
            P(),
            P(),
            P(None, "mp"),
            P(None, "mp"),
            P(None, "mp"),
            P("mp", None),
            P(None, "mp"),
            P(None, "mp"),
            P("mp", None),
            P("dp", "mp", None),
        ),
        out_specs=(
            P("dp", "mp", None),
            P("dp", "mp", None),
            P(("dp", "mp")),
            P(("dp", "mp")),
            P("dp", "mp"),
            P("dp", "mp"),
            P("dp", "mp"),
            P("mp", "dp"),
            P("dp", "mp"),
            P("dp", "mp"),
            P("mp", "dp"),
        ),
        check_vma=False,
    )
```

```python
import functools

import jax
import jax.numpy as jnp
from jax import lax
from jax.experimental import pallas as pl
from jax.experimental.pallas import tpu as pltpu
from jax.sharding import PartitionSpec as P

MESH = pl.DeviceIdType.MESH
F32 = jnp.float32
BF16 = jnp.bfloat16

FEAT = 16
VDIM = 128
WINDOW = 64
SETS = 3
FF_TILE = 256
PARTS = 4

norm_eps = 1e-05
masked_score = -1e30


def place():
    dp, mp = lax.axis_index("dp"), lax.axis_index("mp")
    return dp // 8, (dp // 4) % 2, dp % 4, mp // 2, mp % 2


def device(x, yh, z, yl, core):
    return (x * 8 + yh * 4 + z, yl * 2 + core)


def greet(devices):
    barrier = pltpu.get_barrier_semaphore()
    for target in devices:
        pl.semaphore_signal(barrier, inc=1, device_id=target, device_id_type=MESH)
    pl.semaphore_wait(barrier, len(devices))


def remote(src, dst, send_sem, recv_sem, target):
    return pltpu.make_async_remote_copy(
        src_ref=src,
        dst_ref=dst,
        send_sem=send_sem,
        recv_sem=recv_sem,
        device_id=target,
        device_id_type=MESH,
    )


def dot_nn(a, b):
    return lax.dot_general(a, b, (((1,), (0,)), ((), ())), preferred_element_type=F32)


def dot_nt(a, b):
    return lax.dot_general(a, b, (((1,), (1,)), ((), ())), preferred_element_type=F32)


def dot_tn(a, b):
    return lax.dot_general(a, b, (((0,), (0,)), ((), ())), preferred_element_type=F32)


def each(count, step, body, base=0):
    def run(i, _):
        body(pl.ds(pl.multiple_of(base + i * step, step), step))
        return 0

    lax.fori_loop(0, count // step, run, 0)


class Gather:
    def __init__(self, own, full, send, recv):
        self.own, self.full, self.send, self.recv = own, full, send, recv
        x, yh, z, yl, core = place()
        self.mate, self.pair = device(x, yh, z, yl, 1 - core), device(x, yh, z, 1 - yl, core)
        self.tok = own.shape[0]
        self.piece = self.tok // PARTS
        self.mine, self.far = yl * 2 + core, (1 - yl) * 2 + core

    def rows(self, part, i):
        start = part * self.tok + i * self.piece
        return pl.ds(pl.multiple_of(start, self.piece), self.piece)

    def far_copy(self, i):
        return remote(
            self.own.at[pl.ds(i * self.piece, self.piece)],
            self.full.at[self.rows(self.mine, i)],
            self.send.at[i],
            self.recv.at[i],
            self.pair,
        )

    def near_copy(self):
        return remote(
            self.own,
            self.full.at[pl.ds(pl.multiple_of(self.mine * self.tok, self.tok), self.tok)],
            self.send.at[PARTS],
            self.recv.at[PARTS],
            self.mate,
        )

    def pass_copy(self, i):
        rows = self.rows(self.far, i)
        return remote(
            self.full.at[rows],
            self.full.at[rows],
            self.send.at[PARTS + 1 + i],
            self.recv.at[PARTS + 1 + i],
            self.mate,
        )

    def start(self):
        for i in range(PARTS):
            self.far_copy(i).start()
        self.start_near()

    def start_near(self):
        self.near_copy().start()
        at = pl.ds(pl.multiple_of(self.mine * self.tok, self.tok), self.tok)
        self.full[at, :] = self.own[...]

    def finish_near(self):
        self.near_copy().wait()

    def finish_far(self):
        for i in range(PARTS):
            self.far_copy(i).wait_recv()
            self.pass_copy(i).start()
        for i in range(PARTS):
            self.far_copy(i).wait_send()
            self.pass_copy(i).wait()

    def finish(self):
        self.finish_near()
        self.finish_far()


class Scatter:
    def __init__(self, part, bufs, send, recv):
        self.part = part
        self.near_out, self.near_in, self.far_out, self.far_in = bufs
        self.send, self.recv = send, recv
        x, yh, z, yl, core = place()
        self.yl, self.core = yl, core
        self.mate, self.pair = device(x, yh, z, yl, 1 - core), device(x, yh, z, 1 - yl, core)
        self.tok = self.far_in.shape[0]
        self.piece = self.tok // PARTS

    def near_copy(self, k):
        return remote(
            self.near_out.at[k], self.near_in.at[k], self.send.at[k], self.recv.at[k], self.mate
        )

    def far_copy(self, i):
        rows = pl.ds(i * self.piece, self.piece)
        return remote(
            self.far_out.at[rows],
            self.far_in.at[rows],
            self.send.at[2 + i],
            self.recv.at[2 + i],
            self.pair,
        )

    def start_near(self, k):
        side = self.yl if k else 1 - self.yl
        start = pl.multiple_of((side * 2 + 1 - self.core) * self.tok, self.tok)

        def cast(rows):
            self.near_out[k, rows, :] = self.part[
                pl.ds(pl.multiple_of(start + rows.start, 16), 16), :
            ].astype(BF16)

        each(self.tok, 16, cast)
        self.near_copy(k).start()

    def start_far(self):
        self.near_copy(0).wait_recv()
        far = pl.multiple_of(((1 - self.yl) * 2 + self.core) * self.tok, self.tok)
        for i in range(PARTS):

            def join(rows, i=i):
                at = pl.ds(pl.multiple_of(i * self.piece + rows.start, 16), 16)
                src = pl.ds(pl.multiple_of(far + i * self.piece + rows.start, 16), 16)
                self.far_out[at, :] = (
                    self.part[src, :] + self.near_in[0, at, :].astype(F32)
                ).astype(BF16)

            each(self.piece, 16, join)
            self.far_copy(i).start()

    def start(self):
        self.start_near(0)
        self.start_near(1)
        self.start_far()

    def finish(self, use, after=None):
        self.near_copy(1).wait_recv()
        own = pl.multiple_of((self.yl * 2 + self.core) * self.tok, self.tok)
        for i in range(PARTS):
            self.far_copy(i).wait_recv()

            def join(rows, i=i):
                at = pl.ds(pl.multiple_of(i * self.piece + rows.start, 16), 16)
                src = pl.ds(pl.multiple_of(own + i * self.piece + rows.start, 16), 16)
                use(
                    at,
                    self.part[src, :]
                    + self.near_in[1, at, :].astype(F32)
                    + self.far_in[at, :].astype(F32),
                )

            each(self.piece, 16, join)
            if after is not None:
                after(i)
        for k in (0, 1):
            self.near_copy(k).wait_send()
        for i in range(PARTS):
            self.far_copy(i).wait_send()


def add_into(dst, terms, rows, step):
    def body(i, _):
        at = pl.ds(pl.multiple_of(i * step, step), step)
        total = dst[at, :].astype(F32)
        for term in terms:
            total = total + term[at, :].astype(F32)
        dst[at, :] = total.astype(dst.dtype)
        return 0

    lax.fori_loop(0, rows // step, body, 0)


class RowSum:
    def __init__(self, grad, bufs, send, recv):
        self.grad = grad
        self.t1, self.m1, self.t2, self.m2, self.last = bufs
        self.send, self.recv = send, recv
        self.x, self.yh, self.z, self.yl, self.core = place()

    def near(self, path, stage, step):
        if (path == 0) == (stage == 0):
            return device((self.x + step + 4) % 4, self.yh, self.z, self.yl, self.core)
        return device(self.x, self.yh, (self.z + step + 4) % 4, self.yl, self.core)

    def at(self, path, stage):
        return self.x if (path == 0) == (stage == 0) else self.z

    def block(self, path, b, k):
        return self.grad.at[b, 0, k] if path == 0 else self.grad.at[k, 1, b]

    def copy(self, src, dst, path, slot, target):
        return remote(src, dst, self.send.at[path, slot], self.recv.at[path, slot], target)

    def transit_one(self, path, side):
        b = (self.at(path, 0) + 2) % 4
        return self.copy(
            self.block(path, b, pl.ds(2 * side, 2)),
            self.t1.at[path, side],
            path,
            side,
            self.near(path, 0, 1 - 2 * side),
        )

    def main_one(self, path, side, half):
        step = 1 - 2 * side
        b = (self.at(path, 0) + step + 4) % 4
        src = (
            self.t1.at[path, side]
            if half == side
            else self.block(path, b, pl.ds(2 * half, 2))
        )
        return self.copy(
            src,
            self.m1.at[path, side, pl.ds(2 * half, 2)],
            path,
            2 + 2 * side + half,
            self.near(path, 0, step),
        )

    def transit_two(self, path, side):
        k = (self.at(path, 1) + 2) % 4
        return self.copy(
            self.m1.at[path, 0, k, pl.ds(32 * side, 32)],
            self.t2.at[path, side],
            path,
            6 + side,
            self.near(path, 1, 1 - 2 * side),
        )

    def main_two(self, path, side, half):
        step = 1 - 2 * side
        k = (self.at(path, 1) + step + 4) % 4
        rows = pl.ds(32 * half, 32)
        src = self.t2.at[path, side] if half == side else self.m1.at[path, 0, k, rows]
        return self.copy(
            src,
            self.m2.at[path, side, rows],
            path,
            8 + 2 * side + half,
            self.near(path, 1, step),
        )

    def last_copy(self):
        target = device(self.x, 1 - self.yh, self.z, self.yl, self.core)
        return self.copy(self.m2.at[1 - self.yh, 0], self.last, 0, 12, target)

    def start_one(self):
        for path in (0, 1):
            for side in (0, 1):
                self.transit_one(path, side).start()
        for path in (0, 1):
            for side in (0, 1):
                self.main_one(path, side, 1 - side).start()

    def pass_one(self):
        for path in (0, 1):
            for side in (0, 1):
                self.transit_one(path, side).wait_recv()
                b = (self.at(path, 0) + 1 - 2 * side + 4) % 4
                for k in (0, 1):
                    add_into(
                        self.t1.at[path, side, k],
                        (self.block(path, b, 2 * side + k),),
                        64,
                        16,
                    )
                self.main_one(path, side, side).start()

    def join_one(self):
        for path in (0, 1):
            for side in (0, 1):
                for half in (0, 1):
                    self.main_one(path, side, half).wait_recv()
            b = self.at(path, 0)

            def body(k, _):
                add_into(
                    self.m1.at[path, 0, k],
                    (self.m1.at[path, 1, k], self.block(path, b, k)),
                    64,
                    16,
                )
                return 0

            lax.fori_loop(0, 4, body, 0)
            for side in (0, 1):
                self.transit_two(path, side).start()
            for side in (0, 1):
                self.main_two(path, side, 1 - side).start()

    def pass_two(self):
        for path in (0, 1):
            for side in (0, 1):
                self.transit_two(path, side).wait_recv()
                k = (self.at(path, 1) + 1 - 2 * side + 4) % 4
                add_into(
                    self.t2.at[path, side],
                    (self.m1.at[path, 0, k, pl.ds(32 * side, 32)],),
                    32,
                    16,
                )
                self.main_two(path, side, side).start()

    def join_two(self):
        for path in (0, 1):
            for side in (0, 1):
                for half in (0, 1):
                    self.main_two(path, side, half).wait_recv()
            k = self.at(path, 1)
            add_into(self.m2.at[path, 0], (self.m2.at[path, 1], self.m1.at[path, 0, k]), 64, 16)
        self.last_copy().start()

    def finish(self, use):
        self.last_copy().wait_recv()
        use(self.m2[self.yh, 0].astype(F32) + self.last[...].astype(F32))
        for path in (0, 1):
            for side in (0, 1):
                self.transit_one(path, side).wait_send()
                self.transit_two(path, side).wait_send()
                for half in (0, 1):
                    self.main_one(path, side, half).wait_send()
                    self.main_two(path, side, half).wait_send()
        self.last_copy().wait_send()


def sum_buffers(width):
    return [
        pltpu.VMEM((2, 2, 2, 64, width), BF16),
        pltpu.VMEM((2, 2, 4, 64, width), BF16),
        pltpu.VMEM((2, 2, 32, width), BF16),
        pltpu.VMEM((2, 2, 64, width), BF16),
        pltpu.VMEM((64, width), BF16),
        pltpu.SemaphoreType.DMA((2, 13)),
        pltpu.SemaphoreType.DMA((2, 13)),
    ]


def sum_neighbours():
    x, yh, z, yl, core = place()
    return (
        device((x + 1) % 4, yh, z, yl, core),
        device((x + 3) % 4, yh, z, yl, core),
        device(x, yh, (z + 1) % 4, yl, core),
        device(x, yh, (z + 3) % 4, yl, core),
        device(x, 1 - yh, z, yl, core),
    )


class Pump:
    def __init__(self, grads, sets, sends, recvs, credit):
        self.grads, self.sets, self.sends, self.recvs, self.credit = (
            grads,
            sets,
            sends,
            recvs,
            credit,
        )
        self.queue, self.flight, self.begun, self.total = [], [], 0, 0

    def add(self, width, fill, done):
        self.queue.append((width, fill, done))

    def begin(self):
        if not self.queue or len(self.flight) >= SETS:
            return False
        width, fill, done = self.queue.pop(0)
        slot = self.begun % SETS
        lanes = pl.ds(0, width)
        grad = self.grads[slot]
        view = lambda ref: ref.at[tuple([slice(None)] * (len(ref.shape) - 1) + [lanes])]
        unit = RowSum(
            view(grad), [view(b) for b in self.sets[slot]], self.sends.at[slot], self.recvs.at[slot]
        )
        fill(grad)
        if self.begun >= SETS:
            pl.semaphore_wait(self.credit.at[slot], 5)
        unit.start_one()
        stages = [unit.pass_one, unit.join_one, unit.pass_two, unit.join_two]
        self.flight.append((stages, unit, slot, self.begun, done))
        self.begun += 1
        return True

    def advance(self, entry):
        stages, unit, slot, index, done = entry
        if stages:
            stages.pop(0)()
            return
        unit.finish(done)
        self.flight.remove(entry)
        if index + SETS < self.total:
            for target in sum_neighbours():
                pl.semaphore_signal(
                    self.credit.at[slot], inc=1, device_id=target, device_id_type=MESH
                )

    def step(self):
        for entry in list(self.flight):
            self.advance(entry)
        self.begin()

    def drain(self):
        while self.flight or self.queue:
            self.step()


def norm_rows(values):
    return lax.rsqrt(jnp.mean(values * values, axis=-1, keepdims=True) + norm_eps)


def doc_of(positions, ends):
    return sum((positions >= e).astype(jnp.int32) for e in ends)


def pair_weights(raw, t0, ends):
    rows, cols = raw.shape
    t = t0 + lax.broadcasted_iota(jnp.int32, (rows, 1), 0)
    s = lax.broadcasted_iota(jnp.int32, (1, cols), 1)
    causal = (t >= s) & (doc_of(t, ends) == doc_of(s, ends))
    window = causal & (t - s < WINDOW)
    scaled = raw * (FEAT ** (-0.5))
    kernel = jnp.where(causal, 1.0 + scaled + 0.5 * scaled * scaled, 0.0)
    inv_den = 1.0 / jnp.sum(kernel, axis=1, keepdims=True)
    scores = jnp.where(window, scaled, masked_score)
    weights = jnp.exp(scores - jnp.max(scores, axis=1, keepdims=True))
    probs = weights * (1.0 / jnp.sum(weights, axis=1, keepdims=True))
    return scaled, kernel, inv_den, probs, causal


def layer_kernel(
    lengths,
    x_own,
    g_own,
    gain_attn,
    gain_ffn,
    wq_hbm,
    wk_hbm,
    wv_hbm,
    wo_hbm,
    wg_hbm,
    wu_hbm,
    wd_hbm,
    block_out,
    grad_in,
    gains_out,
    o_query,
    o_key,
    o_value,
    o_out,
    o_gate,
    o_up,
    o_down,
    normed_hbm,
    n2,
    g_all,
    da_all,
    own,
    h1,
    dhid,
    w_gu,
    w_d,
    wqk,
    wv,
    cols_gu,
    qk,
    v_all,
    mixed,
    acc,
    acts,
    dgus,
    gu,
    da,
    dmixed,
    dqkv,
    gsum,
    gnear,
    gfar,
    near_out,
    near_in,
    far_out,
    far_in,
    near_in2,
    far_in2,
    grad0,
    grad1,
    grad2,
    *rest,
):
    sets = [rest[5 * i : 5 * i + 5] for i in range(SETS)]
    sends, recvs, credit, mp_send, mp_recv, wsem = rest[5 * SETS :]
    x, yh, z, yl, core = place()
    dp, mp = lax.axis_index("dp"), lax.axis_index("mp")
    mate, pair = device(x, yh, z, yl, 1 - core), device(x, yh, z, 1 - yl, core)
    seq, width = n2.shape
    ff = wd_hbm.shape[0]
    full_tiles = ff // FF_TILE
    last = ff - full_tiles * FF_TILE
    pad = -(-last // 128) * 128
    order = [full_tiles] + list(range(full_tiles))
    heads = wv.shape[1] // VDIM
    ends = [lengths[0, 0], lengths[0, 0] + lengths[0, 1]]
    ends.append(ends[1] + lengths[0, 2])
    near_base = pl.multiple_of(yl * 256, 256)
    far_base = pl.multiple_of((1 - yl) * 256, 256)

    def valid(t):
        return last if t == full_tiles else FF_TILE

    def wide(t):
        return pad if t == full_tiles else FF_TILE

    def load(src, dst, i):
        return pltpu.make_async_copy(src, dst, wsem.at[i])

    def gu_loads(i):
        t, s = order[i], i % 2
        rows = pl.ds(t * FF_TILE, valid(t))
        return [
            load(wg_hbm.at[rows], w_gu.at[s, pl.ds(0, valid(t))], 3 * s),
            load(wu_hbm.at[rows], w_gu.at[s, pl.ds(wide(t), valid(t))], 3 * s + 1),
        ]

    def down_load(i, sem):
        t, s = order[i], i % 2
        return load(
            wd_hbm.at[pl.ds(t * FF_TILE, valid(t))], w_d.at[s, pl.ds(0, valid(t))], sem + s
        )

    small = [
        load(wq_hbm, wqk.at[pl.ds(0, 64)], 8),
        load(wk_hbm, wqk.at[pl.ds(64, 64)], 9),
        load(wv_hbm, wv, 10),
        load(wo_hbm, w_gu.at[1], 11),
    ]
    chunk = pl.ds(pl.multiple_of((dp // 2) * 128, 128), 128)
    columns = [
        load(wg_hbm.at[:, chunk], cols_gu.at[0], 12),
        load(wu_hbm.at[:, chunk], cols_gu.at[1], 13),
    ]
    for c in small:
        c.start()
    gain_a, gain_f = gain_attn[...], gain_ffn[...]
    tok = own.shape[0]

    def norm_one(rows):
        values = x_own[rows, :].astype(F32)
        own[rows, :] = (values * norm_rows(values) * gain_a).astype(BF16)

    each(tok, 16, norm_one)
    greet(sum_neighbours() + (mate, pair))
    gather_one = Gather(own, da_all, mp_send.at[0], mp_recv.at[0])
    gather_one.start()
    gather_g = Gather(g_own, g_all, mp_send.at[1], mp_recv.at[1])
    gather_g.start()
    for at in (pl.ds(last, pad - last), pl.ds(pad + last, pad - last)):
        w_gu[0, at, :] = jnp.zeros((pad - last, width), BF16)
    w_d[0, pl.ds(last, pad - last), :] = jnp.zeros((pad - last, width), BF16)
    for c in gu_loads(0):
        c.start()
    for i in (0, 1):
        down_load(i, 6).start()
    for c in columns:
        c.start()
    for c in small:
        c.wait()

    def project(rows):
        qk[rows, :] = dot_nt(da_all[rows, :], wqk[...]).astype(BF16)
        v_all[rows, :] = dot_nn(da_all[rows, :], wv[...]).astype(BF16)

    gather_one.finish_near()
    each(256, 256, project, near_base)
    gather_one.finish_far()
    each(256, 256, project, far_base)
    keep_normed = load(da_all, normed_hbm, 14)
    keep_normed.start()

    raw_s, mass_s = gu, dgus.at[1]

    def attend_forward(base, h):
        raw_s[0:256, :] = dot_nt(
            qk[pl.ds(base, 256), h * FEAT : (h + 1) * FEAT],
            qk[:, 64 + h * FEAT : 64 + (h + 1) * FEAT],
        )

        def block(rows):
            _, kernel, inv_den, probs, _ = pair_weights(
                raw_s[rows, :], base + rows.start, ends
            )
            mass_s[rows, :] = (kernel * inv_den + probs).astype(BF16)

        each(256, 32, block)
        vcols = slice(h * VDIM, (h + 1) * VDIM)
        mixed[pl.ds(base, 256), vcols] = dot_nn(mass_s[0:256, :], v_all[:, vcols]).astype(BF16)

    def project_out(rows):
        acc[rows, :] = dot_nn(mixed[rows, :], w_gu[1])

    bufs = (near_out, near_in, far_out, far_in)
    scatter_one = Scatter(acc, bufs, mp_send.at[2], mp_recv.at[2])
    for h in range(heads):
        attend_forward(far_base, h)
    each(256, 256, project_out, far_base)
    scatter_one.start_near(0)
    attend_forward(near_base, 0)
    scatter_one.start_far()
    for h in range(1, heads):
        attend_forward(near_base, h)
    each(256, 256, project_out, near_base)
    scatter_one.start_near(1)
    for c in gu_loads(1):
        c.start()
    gather_g.finish()
    keep_normed.wait()

    gather_two = Gather(own, n2, mp_send.at[3], mp_recv.at[3])

    def norm_two(rows, total):
        hidden = x_own[rows, :].astype(F32) + total
        h1[rows, :] = hidden
        own[rows, :] = (hidden * norm_rows(hidden) * gain_f).astype(BF16)

    scatter_one.finish(norm_two, lambda i: gather_two.far_copy(i).start())
    gather_two.start_near()
    for c in columns:
        c.wait()
    gather_two.finish()

    pump = Pump((grad0, grad1, grad2), sets, sends, recvs, credit)
    pump.total = full_tiles + 3
    lane = lax.broadcasted_iota(jnp.int32, (64, 128), 1)
    row = lax.broadcasted_iota(jnp.int32, (64, 128), 0)
    own_lane = lane == row + (dp % 2) * 64

    def weigh(total, block):
        full = dot_nn(total.astype(BF16), block)
        return jnp.sum(jnp.where(own_lane, full, 0.0), axis=1, keepdims=True)

    def fill_ffn(t):
        p = wide(t)

        def fill(grad):
            def block(b, _):
                lanes = pl.ds(pl.multiple_of(b * 512, 512), 512)
                top = dot_tn(n2[:, lanes], dgus[t, :, 0 : 2 * p])
                bottom = dot_tn(g_all[:, lanes], acts[t, :, 0:p])
                grad[b, :, :, :, 0 : 2 * p] = top.astype(BF16).reshape(2, 4, 64, 2 * p)
                grad[b, :, :, :, 2 * p : 3 * p] = bottom.astype(BF16).reshape(2, 4, 64, p)
                return 0

            lax.fori_loop(0, 4, block, 0)

        return fill

    def done_ffn(t):
        def done(total):
            n, p = valid(t), wide(t)
            cols = slice(t * FF_TILE, t * FF_TILE + n)
            value_gate, value_up = total[:, 0:n], total[:, p : p + n]
            o_gate[:, cols] = value_gate
            o_up[:, cols] = value_up
            o_down[:, cols] = total[:, 2 * p : 2 * p + n]
            column = weigh(value_gate, cols_gu[0, cols, :]) + weigh(value_up, cols_gu[1, cols, :])
            if t == full_tiles:
                gsum[0] = jnp.broadcast_to(column, gsum.shape[1:])
            else:
                gsum[0] += jnp.broadcast_to(column, gsum.shape[1:])

        return done

    for i, t in enumerate(order):
        s, p = i % 2, wide(t)
        for c in gu_loads(i):
            c.wait()
        down_load(i, 6).wait()

        def forward(rows, s=s, p=p):
            gu[rows, 0 : 2 * p] = dot_nt(n2[rows, :], w_gu[s, 0 : 2 * p])
            da[rows, 0:p] = dot_nt(g_all[rows, :], w_d[s, 0:p])

        each(seq, 256, forward)

        def pointwise(rows, t=t, p=p):
            gate, up, d_act = gu[rows, 0:p], gu[rows, p : 2 * p], da[rows, 0:p]
            sig = jax.nn.sigmoid(gate)
            silu = gate * sig
            acts[t, rows, 0:p] = (silu * up).astype(BF16)
            dgus[t, rows, 0:p] = (d_act * up * (sig * (1.0 + gate * (1.0 - sig)))).astype(BF16)
            dgus[t, rows, p : 2 * p] = (d_act * silu).astype(BF16)

        each(seq, 64, pointwise)

        def back(rows, t=t, s=s, p=p):
            part = dot_nn(dgus[t, rows, 0 : 2 * p], w_gu[s, 0 : 2 * p])
            if t == full_tiles:
                acc[rows, :] = part
            else:
                acc[rows, :] += part

        pump.add(3 * p, fill_ffn(t), done_ffn(t))
        pump.step()
        each(seq, 256, back)
        if i + 2 < len(order):
            for c in gu_loads(i + 2):
                c.start()
            down_load(i + 2, 6).start()

    wo = w_gu.at[0]
    load_wo = load(wo_hbm, wo, 0)
    load_wo.start()
    down_load(0, 6).start()
    down_load(1, 6).start()
    scatter_two = Scatter(acc, bufs, mp_send.at[4], mp_recv.at[4])
    scatter_two.start()
    pump.step()

    def norm_two_back(rows, d_normed_two):
        hidden = h1[rows, :]
        inverse = norm_rows(hidden)
        unit = hidden * inverse
        e = d_normed_two * gain_f
        d_hidden = g_own[rows, :].astype(F32) + inverse * (
            e - unit * jnp.mean(e * unit, axis=-1, keepdims=True)
        )
        dhid[rows, :] = d_hidden
        own[rows, :] = d_hidden.astype(BF16)

    gather_attn = Gather(own, da_all, mp_send.at[5], mp_recv.at[5])
    scatter_two.finish(norm_two_back, lambda i: gather_attn.far_copy(i).start())
    gather_attn.start_near()
    pump.step()

    for i, t in enumerate(order):
        down_load(i, 6).wait()

        def down(rows, i=i, t=t, p=wide(t)):
            part = dot_nn(acts[t, rows, 0:p], w_d[i % 2, 0:p])
            if t == full_tiles:
                acc[rows, :] = part
            else:
                acc[rows, :] += part

        each(seq, 256, down)
        if i + 2 < len(order):
            down_load(i + 2, 6).start()
        if i == 2:
            pump.step()
    gather_attn.finish()
    scatter_out = Scatter(acc, (near_out, near_in2, far_out, far_in2), mp_send.at[6], mp_recv.at[6])
    scatter_out.start()
    load_wo.wait()

    def mix_back(rows):
        dmixed[rows, :] = dot_nt(da_all[rows, :], wo[...]).astype(BF16)

    each(seq, 256, mix_back)

    def fill_out(grad):
        def block(b, _):
            lanes = pl.ds(pl.multiple_of(b * 512, 512), 512)
            top = dot_tn(da_all[:, lanes], mixed[...])
            grad[b, :, :, :, 0:512] = top.astype(BF16).reshape(2, 4, 64, 512)
            return 0

        lax.fori_loop(0, 4, block, 0)

    def done_out(total):
        o_out[...] = total

    pump.add(512, fill_out, done_out)
    pump.step()

    load_normed = load(normed_hbm, n2, 1)
    d_probs_s, d_raw_s = da, dgus.at[0]
    for h in range(heads):
        qcols = slice(h * FEAT, (h + 1) * FEAT)
        kcols = slice(64 + h * FEAT, 64 + (h + 1) * FEAT)
        vcols = slice(h * VDIM, (h + 1) * VDIM)
        raw_s[...] = dot_nt(qk[:, qcols], qk[:, kcols])
        d_probs_s[...] = dot_nt(dmixed[:, vcols], v_all[:, vcols])

        def attend(rows):
            scaled, kernel, inv_den, probs, causal = pair_weights(raw_s[rows, :], rows.start, ends)
            d_probs = d_probs_s[rows, :]
            drop = jnp.sum(kernel * d_probs, axis=1, keepdims=True) * inv_den
            d_kernel = (d_probs - drop) * inv_den
            d_scores = probs * (d_probs - jnp.sum(probs * d_probs, axis=1, keepdims=True))
            d_raw = FEAT ** (-0.5) * (
                jnp.where(causal, d_kernel * (1.0 + scaled), 0.0) + d_scores
            )
            d_raw_s[rows, :] = d_raw.astype(BF16)
            mass_s[rows, :] = (kernel * inv_den + probs).astype(BF16)

        each(seq, 32, attend)
        dqkv[:, qcols] = dot_nn(d_raw_s[...], qk[:, kcols]).astype(BF16)
        dqkv[:, kcols] = dot_tn(d_raw_s[...], qk[:, qcols]).astype(BF16)
        dqkv[:, 128 + h * VDIM : 128 + (h + 1) * VDIM] = dot_tn(
            mass_s[...], dmixed[:, vcols]
        ).astype(BF16)
        if h == 0:

            def output(rows, total):
                block_out[rows, :] = (h1[rows, :] + total).astype(BF16)

            scatter_out.finish(output)
        if h == 1:
            pump.step()
            assert not pump.queue or pump.queue[0][0] < 768
            load_normed.start()

    def normed_back(rows):
        acc[rows, :] = dot_nn(dqkv[rows, 0:128], wqk[...]) + dot_nt(dqkv[rows, 128:640], wv[...])

    each(seq, 256, normed_back)
    scatter_in = Scatter(acc, bufs, mp_send.at[7], mp_recv.at[7])
    scatter_in.start()
    load_normed.wait()

    def fill_qkv(grad):
        def block(b, _):
            lanes = pl.ds(pl.multiple_of(b * 512, 512), 512)
            top = dot_tn(n2[:, lanes], dqkv[...])
            grad[b, :, :, :, 0:640] = top.astype(BF16).reshape(2, 4, 64, 640)
            return 0

        lax.fori_loop(0, 4, block, 0)

    def done_qkv(total):
        o_query[...] = total[:, 0:64]
        o_key[...] = total[:, 64:128]
        o_value[...] = total[:, 128:640]
        part = weigh(total[:, 0:128], wqk[:, chunk])
        rows_v = wv[pl.ds(pl.multiple_of(dp * 64, 64), 64), :].astype(F32)
        part += jnp.sum(total[:, 128:640] * rows_v, axis=1, keepdims=True)
        gsum[1] = jnp.broadcast_to(part, gsum.shape[1:])

    pump.add(640, fill_qkv, done_qkv)
    pump.step()

    def norm_one_back(rows, d_normed):
        values = x_own[rows, :].astype(F32)
        inverse = norm_rows(values)
        unit = values * inverse
        e = d_normed * gain_a
        grad_in[rows, :] = dhid[rows, :] + inverse * (
            e - unit * jnp.mean(e * unit, axis=-1, keepdims=True)
        )

    pump.step()
    scatter_in.finish(norm_one_back)
    pump.drain()

    near = remote(gsum, gnear, mp_send.at[8, 0], mp_recv.at[8, 0], mate)
    near.start()
    near.wait()
    gsum[...] += gnear[...]
    far = remote(gsum, gfar, mp_send.at[8, 1], mp_recv.at[8, 1], pair)
    far.start()
    far.wait()
    first = (dp % 2) * 64 + mp * 16
    pick = (row + (dp % 2) * 64) == lane
    for i, gain in enumerate((gain_attn, gain_ffn)):
        sums = jnp.where(pick, gsum[1 - i] + gfar[1 - i], 0.0)
        line = jnp.sum(sums, axis=0, keepdims=True) / gain[:, chunk]
        gains_out[i : i + 1, :] = pltpu.roll(
            jnp.broadcast_to(line, (8, 128)), (128 - first) % 128, 1
        )[0:1, :]


def layer(lengths, x_own, g_own, gain_attn, gain_ffn, wq, wk, wv, wo, wg, wu, wd):
    tok, width = x_own.shape
    seq, ff = 4 * tok, wd.shape[0]
    tiles = -(-ff // FF_TILE)
    wide = 3 * FF_TILE
    vmem, hbm = pl.BlockSpec(memory_space=pltpu.VMEM), pl.BlockSpec(memory_space=pl.ANY)
    shape = jax.ShapeDtypeStruct
    sems = pltpu.SemaphoreType.DMA
    scratch = [
        pltpu.VMEM((seq, width), BF16),
        pltpu.VMEM((seq, width), BF16),
        pltpu.VMEM((seq, width), BF16),
        pltpu.VMEM((tok, width), BF16),
        pltpu.VMEM((tok, width), F32),
        pltpu.VMEM((tok, width), F32),
        pltpu.VMEM((2, 2 * FF_TILE, width), BF16),
        pltpu.VMEM((2, FF_TILE, width), BF16),
        pltpu.VMEM((128, width), BF16),
        pltpu.VMEM(wv.shape, BF16),
        pltpu.VMEM((2, ff, 128), BF16),
        pltpu.VMEM((seq, 128), BF16),
        pltpu.VMEM((seq, 512), BF16),
        pltpu.VMEM((seq, 512), BF16),
        pltpu.VMEM((seq, width), F32),
        pltpu.VMEM((tiles, seq, FF_TILE), BF16),
        pltpu.VMEM((tiles, seq, 2 * FF_TILE), BF16),
        pltpu.VMEM((seq, 512), F32),
        pltpu.VMEM((seq, 512), F32),
        pltpu.VMEM((seq, 512), BF16),
        pltpu.VMEM((seq, 640), BF16),
        pltpu.VMEM((2, 64, 128), F32),
        pltpu.VMEM((2, 64, 128), F32),
        pltpu.VMEM((2, 64, 128), F32),
        pltpu.VMEM((2, tok, width), BF16),
        pltpu.VMEM((2, tok, width), BF16),
        pltpu.VMEM((tok, width), BF16),
        pltpu.VMEM((tok, width), BF16),
        pltpu.VMEM((2, tok, width), BF16),
        pltpu.VMEM((tok, width), BF16),
    ]
    scratch += [pltpu.VMEM((4, 2, 4, 64, wide), BF16) for _ in range(SETS)]
    scratch += [b for _ in range(SETS) for b in sum_buffers(wide)[:5]]
    scratch += [
        sems((SETS, 2, 13)),
        sems((SETS, 2, 13)),
        pltpu.SemaphoreType.REGULAR((SETS,)),
        sems((9, 2 * PARTS + 1)),
        sems((9, 2 * PARTS + 1)),
        sems((16,)),
    ]
    return pl.pallas_call(
        layer_kernel,
        out_shape=[
            shape((tok, width), BF16),
            shape((tok, width), F32),
            shape((2, 128), F32),
            shape((64, wq.shape[0]), F32),
            shape((64, wk.shape[0]), F32),
            shape((64, wv.shape[1]), F32),
            shape((64, wo.shape[0]), F32),
            shape((64, ff), F32),
            shape((64, ff), F32),
            shape((64, ff), F32),
            shape((seq, width), BF16),
        ],
        in_specs=[pl.BlockSpec(memory_space=pltpu.SMEM)] + [vmem] * 4 + [hbm] * 7,
        out_specs=[vmem] * 10 + [hbm],
        scratch_shapes=scratch,
        compiler_params=pltpu.CompilerParams(
            collective_id=0, has_side_effects=True, vmem_limit_bytes=63 << 20
        ),
        name="layer",
    )(lengths, x_own, g_own, gain_attn, gain_ffn, wq, wk, wv, wo, wg, wu, wd)


def hand_out_kernel(n, *refs):
    sems = refs[2 * n + 3]
    copies = [pltpu.make_async_copy(refs[i], refs[n + 1 + i], sems.at[i]) for i in range(n)]
    for c in copies:
        c.start()
    gains, first, second = refs[n], refs[2 * n + 1], refs[2 * n + 2]
    first[...] = gains[0:1, 0:16]
    second[...] = gains[1:2, 0:16]
    for c in copies:
        c.wait()


def hand_out(arrays, gains):
    n = len(arrays)
    vmem, hbm = pl.BlockSpec(memory_space=pltpu.VMEM), pl.BlockSpec(memory_space=pl.ANY)
    shape = jax.ShapeDtypeStruct
    return pl.pallas_call(
        functools.partial(hand_out_kernel, n),
        out_shape=[shape(a.shape, a.dtype) for a in arrays] + [shape((1, 16), F32)] * 2,
        in_specs=[vmem] * (n + 1),
        out_specs=[hbm] * n + [vmem] * 2,
        scratch_shapes=[pltpu.SemaphoreType.DMA((n,))],
        name="hand_out",
    )(*arrays, gains)


def on_device(
    block_input,
    lengths,
    gain_attn,
    gain_ffn,
    w_query,
    w_key,
    w_value,
    w_out,
    w_gate,
    w_up,
    w_down,
    cotangent,
):
    width = block_input.shape[-1]
    out = layer(
        lengths,
        block_input.reshape(-1, width),
        cotangent.reshape(-1, width),
        gain_attn.reshape(1, -1),
        gain_ffn.reshape(1, -1),
        w_query.T,
        w_key.T,
        w_value,
        w_out,
        w_gate.T,
        w_up.T,
        w_down,
    )
    (
        block_output,
        grad_input,
        grad_query,
        grad_key,
        grad_value,
        grad_out,
        grad_gate,
        grad_up,
        grad_down,
        grad_gain_attn,
        grad_gain_ffn,
    ) = hand_out([out[0], out[1], *out[3:10]], out[2])
    return (
        block_output.reshape(block_input.shape),
        grad_input.reshape(block_input.shape),
        grad_gain_attn.reshape(-1),
        grad_gain_ffn.reshape(-1),
        grad_query,
        grad_key,
        grad_value,
        grad_out.T,
        grad_gate,
        grad_up,
        grad_down.T,
    )


def solution(mesh):
    return jax.shard_map(
        on_device,
        mesh=mesh,
        in_specs=(
            P("dp", "mp", None),
            P("dp", None),
            P(),
            P(),
            P(None, "mp"),
            P(None, "mp"),
            P(None, "mp"),
            P("mp", None),
            P(None, "mp"),
            P(None, "mp"),
            P("mp", None),
            P("dp", "mp", None),
        ),
        out_specs=(
            P("dp", "mp", None),
            P("dp", "mp", None),
            P(("dp", "mp")),
            P(("dp", "mp")),
            P("dp", "mp"),
            P("dp", "mp"),
            P("dp", "mp"),
            P("mp", "dp"),
            P("dp", "mp"),
            P("dp", "mp"),
            P("mp", "dp"),
        ),
        check_vma=False,
    )
```

```python
import functools

import jax
import jax.numpy as jnp
from jax import lax
from jax.experimental import pallas as pl
from jax.experimental.pallas import tpu as pltpu
from jax.sharding import PartitionSpec as P

MESH = pl.DeviceIdType.MESH
F32 = jnp.float32
BF16 = jnp.bfloat16

FEAT = 16
VDIM = 128
WINDOW = 64
SETS = 3
FF_TILE = 256
PARTS = 4

norm_eps = 1e-05
masked_score = -1e30


def place():
    dp, mp = lax.axis_index("dp"), lax.axis_index("mp")
    return dp // 8, (dp // 4) % 2, dp % 4, mp // 2, mp % 2


def device(x, yh, z, yl, core):
    return (x * 8 + yh * 4 + z, yl * 2 + core)


def greet(devices):
    barrier = pltpu.get_barrier_semaphore()
    for target in devices:
        pl.semaphore_signal(barrier, inc=1, device_id=target, device_id_type=MESH)
    pl.semaphore_wait(barrier, len(devices))


def remote(src, dst, send_sem, recv_sem, target):
    return pltpu.make_async_remote_copy(
        src_ref=src,
        dst_ref=dst,
        send_sem=send_sem,
        recv_sem=recv_sem,
        device_id=target,
        device_id_type=MESH,
    )


def dot_nn(a, b):
    return lax.dot_general(a, b, (((1,), (0,)), ((), ())), preferred_element_type=F32)


def dot_nt(a, b):
    return lax.dot_general(a, b, (((1,), (1,)), ((), ())), preferred_element_type=F32)


def dot_tn(a, b):
    return lax.dot_general(a, b, (((0,), (0,)), ((), ())), preferred_element_type=F32)


def each(count, step, body, base=0):
    def run(i, _):
        body(pl.ds(pl.multiple_of(base + i * step, step), step))
        return 0

    lax.fori_loop(0, count // step, run, 0)


class Gather:
    def __init__(self, own, full, send, recv):
        self.own, self.full, self.send, self.recv = own, full, send, recv
        x, yh, z, yl, core = place()
        self.mate, self.pair = device(x, yh, z, yl, 1 - core), device(x, yh, z, 1 - yl, core)
        self.tok = own.shape[0]
        self.piece = self.tok // PARTS
        self.mine, self.far = yl * 2 + core, (1 - yl) * 2 + core

    def rows(self, part, i):
        start = part * self.tok + i * self.piece
        return pl.ds(pl.multiple_of(start, self.piece), self.piece)

    def far_copy(self, i):
        return remote(
            self.own.at[pl.ds(i * self.piece, self.piece)],
            self.full.at[self.rows(self.mine, i)],
            self.send.at[i],
            self.recv.at[i],
            self.pair,
        )

    def near_copy(self):
        return remote(
            self.own,
            self.full.at[pl.ds(pl.multiple_of(self.mine * self.tok, self.tok), self.tok)],
            self.send.at[PARTS],
            self.recv.at[PARTS],
            self.mate,
        )

    def pass_copy(self, i):
        rows = self.rows(self.far, i)
        return remote(
            self.full.at[rows],
            self.full.at[rows],
            self.send.at[PARTS + 1 + i],
            self.recv.at[PARTS + 1 + i],
            self.mate,
        )

    def start(self):
        for i in range(PARTS):
            self.far_copy(i).start()
        self.start_near()

    def start_near(self):
        self.near_copy().start()
        at = pl.ds(pl.multiple_of(self.mine * self.tok, self.tok), self.tok)
        self.full[at, :] = self.own[...]

    def finish_near(self):
        self.near_copy().wait()

    def finish_far(self):
        for i in range(PARTS):
            self.far_copy(i).wait_recv()
            self.pass_copy(i).start()
        for i in range(PARTS):
            self.far_copy(i).wait_send()
            self.pass_copy(i).wait()

    def finish(self):
        self.finish_near()
        self.finish_far()


class Scatter:
    def __init__(self, part, bufs, send, recv):
        self.part = part
        self.near_out, near_in, self.far_out, self.far_in = bufs
        if near_in is not None:
            self.near_in = [near_in.at[k] for k in (0, 1)]
        self.send, self.recv = send, recv
        x, yh, z, yl, core = place()
        self.yl, self.core = yl, core
        self.mate, self.pair = device(x, yh, z, yl, 1 - core), device(x, yh, z, 1 - yl, core)
        self.tok = self.far_in.shape[0]
        self.piece = self.tok // PARTS

    def near_copy(self, k):
        return remote(
            self.near_out, self.near_in[k], self.send.at[k], self.recv.at[k], self.mate
        )

    def far_copy(self, i):
        rows = pl.ds(i * self.piece, self.piece)
        return remote(
            self.far_out.at[rows],
            self.far_in.at[rows],
            self.send.at[2 + i],
            self.recv.at[2 + i],
            self.pair,
        )

    def start_near(self, k):
        side = self.yl if k else 1 - self.yl
        start = pl.multiple_of((side * 2 + 1 - self.core) * self.tok, self.tok)

        if k:
            self.near_copy(0).wait_send()

        def cast(rows):
            self.near_out[rows, :] = self.part[
                pl.ds(pl.multiple_of(start + rows.start, 16), 16), :
            ].astype(BF16)

        each(self.tok, 16, cast)
        self.near_copy(k).start()

    def start_far(self):
        self.near_copy(0).wait_recv()
        far = pl.multiple_of(((1 - self.yl) * 2 + self.core) * self.tok, self.tok)
        for i in range(PARTS):

            def join(rows, i=i):
                at = pl.ds(pl.multiple_of(i * self.piece + rows.start, 16), 16)
                src = pl.ds(pl.multiple_of(far + i * self.piece + rows.start, 16), 16)
                self.far_out[at, :] = (
                    self.part[src, :] + self.near_in[0][at, :].astype(F32)
                ).astype(BF16)

            each(self.piece, 16, join)
            self.far_copy(i).start()

    def fold(self, use):
        self.near_copy(1).wait_recv()
        own = pl.multiple_of((self.yl * 2 + self.core) * self.tok, self.tok)

        def join(rows):
            src = pl.ds(pl.multiple_of(own + rows.start, 16), 16)
            use(rows, self.part[src, :] + self.near_in[1][rows, :].astype(F32))

        each(self.tok, 16, join)
        self.near_copy(1).wait_send()

    def finish_far(self, use):
        for i in range(PARTS):
            self.far_copy(i).wait()
        each(self.tok, 16, lambda rows: use(rows, self.far_in[rows, :].astype(F32)))

    def finish(self, use, after=None):
        self.near_copy(1).wait_recv()
        own = pl.multiple_of((self.yl * 2 + self.core) * self.tok, self.tok)
        for i in range(PARTS):
            self.far_copy(i).wait_recv()

            def join(rows, i=i):
                at = pl.ds(pl.multiple_of(i * self.piece + rows.start, 16), 16)
                src = pl.ds(pl.multiple_of(own + i * self.piece + rows.start, 16), 16)
                use(
                    at,
                    self.part[src, :]
                    + self.near_in[1][at, :].astype(F32)
                    + self.far_in[at, :].astype(F32),
                )

            each(self.piece, 16, join)
            if after is not None:
                after(i)
        self.near_copy(1).wait_send()
        for i in range(PARTS):
            self.far_copy(i).wait_send()


def add_into(dst, terms, rows, step):
    def body(i, _):
        at = pl.ds(pl.multiple_of(i * step, step), step)
        total = dst[at, :].astype(F32)
        for term in terms:
            total = total + term[at, :].astype(F32)
        dst[at, :] = total.astype(dst.dtype)
        return 0

    lax.fori_loop(0, rows // step, body, 0)


class RowSum:
    def __init__(self, grad, bufs, send, recv):
        self.grad = grad
        self.t1, self.m1, self.t2, self.m2, self.last = bufs
        self.send, self.recv = send, recv
        self.x, self.yh, self.z, self.yl, self.core = place()

    def near(self, path, stage, step):
        if (path == 0) == (stage == 0):
            return device((self.x + step + 4) % 4, self.yh, self.z, self.yl, self.core)
        return device(self.x, self.yh, (self.z + step + 4) % 4, self.yl, self.core)

    def at(self, path, stage):
        return self.x if (path == 0) == (stage == 0) else self.z

    def block(self, path, b, k):
        return self.grad.at[b, 0, k] if path == 0 else self.grad.at[k, 1, b]

    def copy(self, src, dst, path, slot, target):
        return remote(src, dst, self.send.at[path, slot], self.recv.at[path, slot], target)

    def transit_one(self, path, side):
        b = (self.at(path, 0) + 2) % 4
        return self.copy(
            self.block(path, b, pl.ds(2 * side, 2)),
            self.t1.at[path, side],
            path,
            side,
            self.near(path, 0, 1 - 2 * side),
        )

    def main_one(self, path, side, half):
        step = 1 - 2 * side
        b = (self.at(path, 0) + step + 4) % 4
        src = (
            self.t1.at[path, side]
            if half == side
            else self.block(path, b, pl.ds(2 * half, 2))
        )
        return self.copy(
            src,
            self.m1.at[path, side, pl.ds(2 * half, 2)],
            path,
            2 + 2 * side + half,
            self.near(path, 0, step),
        )

    def transit_two(self, path, side):
        k = (self.at(path, 1) + 2) % 4
        return self.copy(
            self.m1.at[path, 0, k, pl.ds(32 * side, 32)],
            self.t2.at[path, side],
            path,
            6 + side,
            self.near(path, 1, 1 - 2 * side),
        )

    def main_two(self, path, side, half):
        step = 1 - 2 * side
        k = (self.at(path, 1) + step + 4) % 4
        rows = pl.ds(32 * half, 32)
        src = self.t2.at[path, side] if half == side else self.m1.at[path, 0, k, rows]
        return self.copy(
            src,
            self.m2.at[path, side, rows],
            path,
            8 + 2 * side + half,
            self.near(path, 1, step),
        )

    def last_copy(self):
        target = device(self.x, 1 - self.yh, self.z, self.yl, self.core)
        return self.copy(self.m2.at[1 - self.yh, 0], self.last, 0, 12, target)

    def start_one(self):
        for path in (0, 1):
            for side in (0, 1):
                self.transit_one(path, side).start()
        for path in (0, 1):
            for side in (0, 1):
                self.main_one(path, side, 1 - side).start()

    def pass_one(self):
        for path in (0, 1):
            for side in (0, 1):
                self.transit_one(path, side).wait_recv()
                b = (self.at(path, 0) + 1 - 2 * side + 4) % 4
                for k in (0, 1):
                    add_into(
                        self.t1.at[path, side, k],
                        (self.block(path, b, 2 * side + k),),
                        64,
                        64,
                    )
                self.main_one(path, side, side).start()

    def join_one(self):
        for path in (0, 1):
            for side in (0, 1):
                for half in (0, 1):
                    self.main_one(path, side, half).wait_recv()
            b = self.at(path, 0)

            def body(k, _):
                add_into(
                    self.m1.at[path, 0, k],
                    (self.m1.at[path, 1, k], self.block(path, b, k)),
                    64,
                    64,
                )
                return 0

            lax.fori_loop(0, 4, body, 0)
            for side in (0, 1):
                self.transit_two(path, side).start()
            for side in (0, 1):
                self.main_two(path, side, 1 - side).start()

    def pass_two(self):
        for path in (0, 1):
            for side in (0, 1):
                self.transit_two(path, side).wait_recv()
                k = (self.at(path, 1) + 1 - 2 * side + 4) % 4
                add_into(
                    self.t2.at[path, side],
                    (self.m1.at[path, 0, k, pl.ds(32 * side, 32)],),
                    32,
                    32,
                )
                self.main_two(path, side, side).start()

    def join_two(self):
        for path in (0, 1):
            for side in (0, 1):
                for half in (0, 1):
                    self.main_two(path, side, half).wait_recv()
            k = self.at(path, 1)
            add_into(self.m2.at[path, 0], (self.m2.at[path, 1], self.m1.at[path, 0, k]), 64, 64)
        self.last_copy().start()

    def finish(self, use):
        self.last_copy().wait_recv()
        use(self.m2[self.yh, 0].astype(F32) + self.last[...].astype(F32))
        for path in (0, 1):
            for side in (0, 1):
                self.transit_one(path, side).wait_send()
                self.transit_two(path, side).wait_send()
                for half in (0, 1):
                    self.main_one(path, side, half).wait_send()
                    self.main_two(path, side, half).wait_send()
        self.last_copy().wait_send()


def sum_buffers(width):
    return [
        pltpu.VMEM((2, 2, 2, 64, width), BF16),
        pltpu.VMEM((2, 2, 4, 64, width), BF16),
        pltpu.VMEM((2, 2, 32, width), BF16),
        pltpu.VMEM((2, 2, 64, width), BF16),
        pltpu.VMEM((64, width), BF16),
        pltpu.SemaphoreType.DMA((2, 13)),
        pltpu.SemaphoreType.DMA((2, 13)),
    ]


def sum_neighbours():
    x, yh, z, yl, core = place()
    return (
        device((x + 1) % 4, yh, z, yl, core),
        device((x + 3) % 4, yh, z, yl, core),
        device(x, yh, (z + 1) % 4, yl, core),
        device(x, yh, (z + 3) % 4, yl, core),
        device(x, 1 - yh, z, yl, core),
    )


class Pump:
    def __init__(self, grads, sets, sends, recvs, credit):
        self.grads, self.sets, self.sends, self.recvs, self.credit = (
            grads,
            sets,
            sends,
            recvs,
            credit,
        )
        self.units, self.turn = [], 0

    def add(self, width, fill, done, loads=()):
        slot = len(self.units) % SETS
        lanes = pl.ds(0, width)

        def view(ref):
            return ref.at[tuple([slice(None)] * (len(ref.shape) - 1) + [lanes])]

        rows = RowSum(
            view(self.grads[slot]),
            [view(b) for b in self.sets[slot]],
            self.sends.at[slot],
            self.recvs.at[slot],
        )
        self.units.append((rows, fill, done, loads))

    def stage(self, index, number):
        rows, fill, done, loads = self.units[index]
        slot = index % SETS
        if number == 0:
            fill(self.grads[slot])
        elif number == 1:
            if index >= SETS:
                pl.semaphore_wait(self.credit.at[slot], 5)
            rows.start_one()
        elif number < 6:
            if number == 5:
                for c in loads:
                    c.start()
            (rows.pass_one, rows.join_one, rows.pass_two, rows.join_two)[number - 2]()
        else:
            rows.finish(done)
            if index + SETS < UNITS:
                for target in sum_neighbours():
                    pl.semaphore_signal(
                        self.credit.at[slot], inc=1, device_id=target, device_id_type=MESH
                    )

    def tick(self):
        for index, number in PLAN[self.turn]:
            self.stage(index, number)
        self.turn += 1


UNITS = 8
PLAN = (
    (),
    ((0, 0), (0, 1),),
    (),
    ((1, 0), (1, 1),),
    ((0, 2),),
    (),
    (),
    (),
    ((1, 2),),
    (),
    ((2, 0), (0, 3), (2, 1),),
    ((1, 3),),
    (),
    ((0, 4),),
    ((2, 2), (1, 4), (0, 5), (2, 3), (1, 5), (0, 6), (3, 0), (3, 1),),
    ((1, 6), (2, 4),),
    (),
    (),
    (),
    (),
    (),
    (),
    ((4, 0), (3, 2), (4, 1), (2, 5),),
    (),
    ((3, 3), (2, 6),),
    (),
    (),
    ((4, 2),),
    (),
    ((5, 0), (3, 4), (5, 1),),
    (),
    ((4, 3),),
    ((3, 5),),
    (),
    (),
    ((5, 2), (3, 6), (6, 0), (4, 4), (6, 1), (5, 3), (4, 5), (6, 2),),
    ((4, 6), (5, 4), (7, 0), (7, 1), (6, 3), (5, 5), (7, 2), (5, 6), (6, 4), (7, 3), (6, 5), (7, 4), (6, 6), (7, 5), (7, 6),),
)


def norm_rows(values):
    return lax.rsqrt(jnp.mean(values * values, axis=-1, keepdims=True) + norm_eps)


def doc_of(positions, ends):
    return sum((positions >= e).astype(jnp.int32) for e in ends)


def add_product(total, left, right, first):
    for j in range(0, total.shape[1], 512):
        cols = slice(j, j + 512)
        part = dot_nn(left[...], right[:, cols])
        if first:
            total[:, cols] = part
        else:
            total[:, cols] += part


def layer_kernel(
    lengths,
    x_own,
    g_own,
    gain_attn,
    gain_ffn,
    wq_hbm,
    wk_hbm,
    wv_hbm,
    wo_hbm,
    wg_hbm,
    wu_hbm,
    wd_hbm,
    block_out,
    grad_in,
    gains_out,
    o_query,
    o_key,
    o_value,
    o_out,
    o_gate,
    o_up,
    o_down,
    normed_hbm,
    n2,
    g_all,
    da_all,
    own,
    h1,
    w_gu,
    w_d,
    wqk,
    wv,
    cols_gu,
    qk,
    v_ones,
    mixed,
    linear,
    windowed,
    stats,
    mask,
    band,
    acc,
    acts,
    dgus,
    dgu_last,
    gu,
    d_acts,
    dmixed,
    dqkv,
    gsum,
    gline,
    glines,
    near_out,
    near_in,
    far_out,
    far_in,
    *rest,
):
    grads = rest[:SETS]
    sets = [rest[SETS + 5 * i : SETS + 5 * i + 5] for i in range(SETS)]
    sends, recvs, credit, mp_send, mp_recv, wsem = rest[6 * SETS :]
    x, yh, z, yl, core = place()
    dp, mp = lax.axis_index("dp"), lax.axis_index("mp")
    mate, pair = device(x, yh, z, yl, 1 - core), device(x, yh, z, 1 - yl, core)
    seq, width = n2.shape
    ff = wd_hbm.shape[0]
    full_tiles = ff // FF_TILE
    last = ff - full_tiles * FF_TILE
    pad = -(-last // 128) * 128
    order = [full_tiles] + list(range(full_tiles))
    heads = wv.shape[1] // VDIM
    ends = [lengths[0, 0], lengths[0, 0] + lengths[0, 1]]
    ends.append(ends[1] + lengths[0, 2])
    near_base = pl.multiple_of(yl * 256, 256)
    far_base = pl.multiple_of((1 - yl) * 256, 256)

    def valid(t):
        return last if t == full_tiles else FF_TILE

    def wide(t):
        return pad if t == full_tiles else FF_TILE

    def dgu(t):
        return dgu_last if t == full_tiles else dgus.at[t]

    def load(src, dst, i):
        return pltpu.make_async_copy(src, dst, wsem.at[i])

    def gu_loads(i):
        t, s = order[i], i % 2
        rows = pl.ds(t * FF_TILE, valid(t))
        return [
            load(wg_hbm.at[rows], w_gu.at[s, pl.ds(0, valid(t))], 3 * s),
            load(wu_hbm.at[rows], w_gu.at[s, pl.ds(wide(t), valid(t))], 3 * s + 1),
        ]

    def down_load(i, sem):
        t, s = order[i], i % 2
        return load(
            wd_hbm.at[pl.ds(t * FF_TILE, valid(t))], w_d.at[s, pl.ds(0, valid(t))], sem + s
        )

    small = [
        load(wq_hbm, wqk.at[pl.ds(0, 64)], 8),
        load(wk_hbm, wqk.at[pl.ds(64, 64)], 9),
        load(wv_hbm, wv, 10),
        load(wo_hbm, w_gu.at[1], 11),
    ]
    chunk = pl.ds(pl.multiple_of((dp // 2) * 128, 128), 128)

    def columns(t):
        rows, some, s = pl.ds(t * FF_TILE, valid(t)), pl.ds(0, valid(t)), order.index(t) % 2
        return [
            load(w.at[rows, chunk], cols_gu.at[s, i, some], 12 + 2 * s + i)
            for i, w in enumerate((wg_hbm, wu_hbm))
        ]

    for c in small:
        c.start()
    gain_a, gain_f = gain_attn[...], gain_ffn[...]
    tok = own.shape[0]

    def norm_one(rows):
        values = x_own[rows, :].astype(F32)
        own[rows, :] = (values * norm_rows(values) * gain_a).astype(BF16)

    each(tok, 16, norm_one)
    greet(sum_neighbours() + (mate, pair, device(x, yh, z, 1 - yl, 1 - core)))
    gather_one = Gather(own, da_all, mp_send.at[0], mp_recv.at[0])
    gather_one.start()
    gather_g = Gather(g_own, g_all, mp_send.at[1], mp_recv.at[1])
    gather_g.start()
    for at in (pl.ds(last, pad - last), pl.ds(pad + last, pad - last)):
        w_gu[0, at, :] = jnp.zeros((pad - last, width), BF16)
    w_d[0, pl.ds(last, pad - last), :] = jnp.zeros((pad - last, width), BF16)
    for c in gu_loads(0):
        c.start()
    for i in (0, 1):
        down_load(i, 6).start()
    for c in small:
        c.wait()

    def masks(rows):
        t = rows.start + lax.broadcasted_iota(jnp.int32, (32, 1), 0)
        col = lax.broadcasted_iota(jnp.int32, (1, seq), 1)
        seen = (t >= col) & (doc_of(t, ends) == doc_of(col, ends))
        mask[rows, :] = jnp.where(seen, 1.0, 0.0).astype(BF16)
        col = band_start(rows.start // 128) + lax.broadcasted_iota(jnp.int32, (1, 256), 1)
        seen = (t >= col) & (t - col < WINDOW) & (doc_of(t, ends) == doc_of(col, ends))
        band[rows, :] = jnp.where(seen, 0.0, masked_score).astype(BF16)

    def band_start(block):
        return pl.multiple_of(jnp.maximum(block - 1, 0) * 128, 128)

    each(seq, 32, masks)
    for h in range(heads):
        v_ones[:, 256 * h + 128 : 256 * h + 256] = jnp.ones((seq, 128), BF16)
    shrink = jnp.where(
        lax.broadcasted_iota(jnp.int32, (1, 128), 1) < 64, FEAT ** (-0.5), 1.0
    )

    def project(rows):
        qk[rows, :] = (dot_nt(da_all[rows, :], wqk[...]) * shrink).astype(BF16)
        value = dot_nn(da_all[rows, :], wv[...]).astype(BF16)
        for h in range(heads):
            v_ones[rows, 256 * h : 256 * h + 128] = value[:, 128 * h : 128 * h + 128]

    gather_one.finish_near()
    each(256, 256, project, near_base)
    gather_one.finish_far()
    each(256, 256, project, far_base)
    keep_normed = load(da_all, normed_hbm, 16)
    keep_normed.start()

    def query_cols(h):
        return slice(h * FEAT, (h + 1) * FEAT)

    def key_cols(h):
        return slice(64 + h * FEAT, 64 + (h + 1) * FEAT)

    def value_cols(h):
        return slice(h * VDIM, (h + 1) * VDIM)

    def attend_forward(base, hs):
        half = [pl.ds(pl.multiple_of(base + 128 * i, 128), 128) for i in (0, 1)]
        first = [band_start(base // 128 + i) for i in (0, 1)]

        def raw_at(h, rows):
            return gu.at[slice(256 * (h % 2) + rows.start, 256 * (h % 2) + rows.stop)]

        for h in hs:
            raw_at(h, slice(0, 256))[...] = dot_nt(
                qk[pl.ds(base, 256), query_cols(h)], qk[:, key_cols(h)]
            )
        for h in hs:

            def taylor(sub, h=h):
                at = pl.ds(pl.multiple_of(base + sub.start, 64), 64)
                src = pl.ds(pl.multiple_of(256 * (h % 2) + sub.start, 64), 64)
                score = gu[src, :]
                dgus[h, sub, :] = ((0.5 * score + 1.0) * score + 1.0).astype(BF16) * mask[at, :]

            each(256, 64, taylor)
        for h in hs:
            both = slice(256 * h, 256 * h + 256)
            one = dot_nn(dgus[h, 0:256, :], v_ones[:, both])
            for i in (0, 1):
                sub = slice(128 * i, 128 * i + 128)
                scores = raw_at(h, sub)[:, pl.ds(first[i], 256)] + band[half[i], :].astype(F32)
                top = jnp.max(scores, axis=1, keepdims=True)
                weights = jnp.exp(scores - top).astype(BF16)
                two = dot_nn(weights, v_ones[pl.ds(first[i], 256), both])
                inv_den = 1.0 / one[sub, 128:256]
                lin = one[sub, 0:128] * inv_den
                win = two[:, 0:128] / two[:, 128:256]
                linear[half[i], value_cols(h)] = lin.astype(BF16)
                windowed[half[i], value_cols(h)] = win.astype(BF16)
                mixed[half[i], value_cols(h)] = (lin + win).astype(BF16)
                stats[half[i], h : h + 1] = inv_den[:, 0:1]
                stats[half[i], heads + h : heads + h + 1] = top + jnp.log(two[:, 128:129])

    def project_out(rows):
        acc[rows, :] = dot_nn(mixed[rows, :], w_gu[1])

    bufs = (near_out, near_in, far_out, far_in)
    scatter_one = Scatter(acc, bufs, mp_send.at[2], mp_recv.at[2])
    for h in range(0, heads, 2):
        attend_forward(far_base, range(h, h + 2))
    each(256, 256, project_out, far_base)
    scatter_one.start_near(0)
    attend_forward(near_base, range(2))
    scatter_one.start_far()
    attend_forward(near_base, range(2, heads))
    each(256, 256, project_out, near_base)
    scatter_one.start_near(1)
    for c in gu_loads(1):
        c.start()
    gather_g.finish()
    keep_normed.wait()

    gather_two = Gather(own, n2, mp_send.at[3], mp_recv.at[3])

    def norm_two(rows, total):
        hidden = x_own[rows, :].astype(F32) + total
        h1[rows, :] = hidden
        own[rows, :] = (hidden * norm_rows(hidden) * gain_f).astype(BF16)

    scatter_one.finish(norm_two, lambda i: gather_two.far_copy(i).start())
    gather_two.start_near()

    def at_act(t):
        return slice(FF_TILE * (t % 2), FF_TILE * (t % 2) + wide(t))

    for i, t in enumerate(order):
        down_load(i, 6).wait()

        def back_down(rows, i=i, t=t, p=wide(t)):
            d_acts[t // 2, rows, at_act(t)] = dot_nt(g_all[rows, :], w_d[i % 2, 0:p]).astype(BF16)

        each(seq, seq, back_down)
        if i + 2 < len(order):
            down_load(i + 2, 6).start()
    for i in (0, 1):
        down_load(i, 6).start()
    gather_two.finish()

    load_normed = load(normed_hbm, n2, 1)
    pump = Pump(grads, sets, sends, recvs, credit)
    lane = lax.broadcasted_iota(jnp.int32, (64, 128), 1)
    row = lax.broadcasted_iota(jnp.int32, (64, 128), 0)
    own_lane = lane == row + (dp % 2) * 64

    def weigh(total, block):
        full = dot_nn(total.astype(BF16), block)
        return jnp.sum(jnp.where(own_lane, full, 0.0), axis=1, keepdims=True)

    def halves(grad, block):
        def run(i, _):
            block(grad.at[pl.ds(2 * i, 2)], pl.ds(pl.multiple_of(i * 1024, 1024), 1024))
            return 0

        lax.fori_loop(0, 2, run, 0)

    def fill_ffn(t):
        p = wide(t)

        def fill(grad):
            def top(half, lanes):
                part = dot_tn(n2[:, lanes], dgu(t)[...])
                half[..., 0 : 2 * p] = part.astype(BF16).reshape(2, 2, 4, 64, 2 * p)

            def bottom(half, lanes):
                part = dot_tn(g_all[:, lanes], acts[t, :, 0:p])
                half[..., 2 * p : 3 * p] = part.astype(BF16).reshape(2, 2, 4, 64, p)

            halves(grad, top)
            halves(grad, bottom)
            if t == full_tiles - 1:
                load_normed.start()

        return fill

    def done_ffn(t):
        def done(total):
            n, p = valid(t), wide(t)
            cols = slice(t * FF_TILE, t * FF_TILE + n)
            value_gate, value_up = total[:, 0:n], total[:, p : p + n]
            o_gate[:, cols] = value_gate
            o_up[:, cols] = value_up
            o_down[:, cols] = total[:, 2 * p : 2 * p + n]
            for c in columns(t):
                c.wait()
            s = order.index(t) % 2
            column = weigh(value_gate, cols_gu[s, 0, 0:n, :])
            column += weigh(value_up, cols_gu[s, 1, 0:n, :])
            if t == full_tiles:
                gsum[0] = jnp.broadcast_to(column, gsum.shape[1:])
            else:
                gsum[0] += jnp.broadcast_to(column, gsum.shape[1:])

        return done

    for i, t in enumerate(order):
        s, p = i % 2, wide(t)
        pump.tick()
        for c in gu_loads(i):
            c.wait()

        def forward(rows, t=t, s=s, p=p):
            gu[rows, 0 : 2 * p] = dot_nt(n2[rows, :], w_gu[s, 0 : 2 * p])

            def pointwise(at):
                gate, up = gu[at, 0:p], gu[at, p : 2 * p]
                d_act = d_acts[t // 2, at, at_act(t)].astype(F32)
                sig = jax.nn.sigmoid(gate)
                silu = gate * sig
                acts[t, at, 0:p] = (silu * up).astype(BF16)
                dgu(t)[at, 0:p] = (d_act * up * (sig * (1.0 + gate * (1.0 - sig)))).astype(BF16)
                dgu(t)[at, p : 2 * p] = (d_act * silu).astype(BF16)

            each(seq, 128, pointwise)

        each(seq, seq, forward)

        pump.add(3 * p, fill_ffn(t), done_ffn(t), columns(t))
        pump.tick()
        add_product(acc, dgu(t), w_gu.at[s, 0 : 2 * p], t == full_tiles)

        if i + 2 < len(order):
            for c in gu_loads(i + 2):
                c.start()

    wo = w_gu.at[0]
    load_wo = load(wo_hbm, wo, 0)
    load_wo.start()
    scatter_two = Scatter(acc, bufs, mp_send.at[4], mp_recv.at[4])
    pump.tick()
    scatter_two.start_near(0)
    pump.tick()
    scatter_two.start_far()
    scatter_two.start_near(1)
    pump.tick()

    def norm_two_back(rows, d_normed_two):
        hidden = h1[rows, :]
        inverse = norm_rows(hidden)
        unit = hidden * inverse
        e = d_normed_two * gain_f
        d_hidden = g_own[rows, :].astype(F32) + inverse * (
            e - unit * jnp.mean(e * unit, axis=-1, keepdims=True)
        )
        grad_in[rows, :] = d_hidden
        own[rows, :] = d_hidden.astype(BF16)

    gather_attn = Gather(own, da_all, mp_send.at[5], mp_recv.at[5])
    scatter_two.finish(norm_two_back, lambda i: gather_attn.far_copy(i).start())
    pump.tick()
    gather_attn.start_near()

    for i, t in enumerate(order):
        pump.tick()
        down_load(i, 6).wait()

        p = wide(t)
        add_product(acc, acts.at[t, :, 0:p], w_d.at[i % 2, 0:p], t == full_tiles)
        if i + 2 < len(order):
            down_load(i + 2, 6).start()
    pump.tick()
    gather_attn.finish()
    far_in2 = w_gu.at[1, pl.ds(2 * tok, tok)]
    scatter_out = Scatter(acc, (near_out, None, far_out, far_in2), mp_send.at[6], mp_recv.at[6])
    scatter_out.near_in = [w_gu.at[1, pl.ds(k * tok, tok)] for k in (0, 1)]
    pump.tick()
    scatter_out.start_near(0)
    pump.tick()
    load_wo.wait()

    def mix_back(rows):
        dmixed[rows, :] = dot_nt(da_all[rows, :], wo[...]).astype(BF16)

    each(seq, seq, mix_back)

    def fill_out(grad):
        def block(half, lanes):
            top = dot_tn(da_all[:, lanes], mixed[...])
            half[..., 0:512] = top.astype(BF16).reshape(2, 2, 4, 64, 512)

        halves(grad, block)

    def done_out(total):
        o_out[...] = total

    pump.add(512, fill_out, done_out)
    pump.tick()
    scatter_out.start_far()
    scatter_out.start_near(1)

    def keep(rows, total):
        h1[rows, :] += total

    pump.tick()
    scatter_out.fold(keep)

    raw_s, d_probs_s = acc.at[:, 0:512], acc.at[:, 512:1024]
    d_raw_s, mass_s = dgus.at[0], dgus.at[1]
    for i in range(1, 4):
        above = (slice(128 * (i - 1), 128 * i), slice(128 * i, seq))
        d_raw_s[above] = jnp.zeros((128, seq - 128 * i), BF16)
        mass_s[above] = jnp.zeros((128, seq - 128 * i), BF16)
    for h in range(heads):
        pump.tick()
        vcols = value_cols(h)
        for i in range(4):
            rows, reach = slice(128 * i, 128 * i + 128), 128 * i + 128
            raw_s[rows, 0:reach] = dot_nt(qk[rows, query_cols(h)], qk[0:reach, key_cols(h)])
            d_probs_s[rows, 0:reach] = dot_nt(
                dmixed[rows, vcols], v_ones[0:reach, 256 * h : 256 * h + 128]
            )
        for i in range(4):
            rows, reach = slice(128 * i, 128 * i + 128), 128 * i + 128
            cols = slice(max(0, 128 * i - 128), reach)

            def part(at, h=h, vcols=vcols, reach=reach, cols=cols):
                d_mix = dmixed[at, vcols].astype(F32)
                drop_lin = jnp.sum(d_mix * linear[at, vcols].astype(F32), axis=1, keepdims=True)
                drop_win = jnp.sum(d_mix * windowed[at, vcols].astype(F32), axis=1, keepdims=True)
                scale = stats[at, h : h + 1]
                total = stats[at, heads + h : heads + h + 1]
                score, d_probs = raw_s[at, 0:reach], d_probs_s[at, 0:reach]
                seen = mask[at, 0:reach]
                kernel = ((0.5 * score + 1.0) * score + 1.0) * scale
                mass_s[at, 0:reach] = kernel.astype(BF16) * seen
                d_kernel = (d_probs - drop_lin) * scale * (1.0 + score)
                d_raw_s[at, 0:reach] = d_kernel.astype(BF16) * seen
                probs = jnp.exp(raw_s[at, cols] + (band[at, 0 : cols.stop - cols.start].astype(F32) - total))
                d_scores = probs * (d_probs_s[at, cols] - drop_win)
                mass_s[at, cols] = (mass_s[at, cols].astype(F32) + probs).astype(BF16)
                d_raw_s[at, cols] = (d_raw_s[at, cols].astype(F32) + d_scores).astype(BF16)

            each(128, 64, part, 128 * i)
        dqkv[:, query_cols(h)] = (
            FEAT ** (-0.5) * dot_nn(d_raw_s[...], qk[:, key_cols(h)])
        ).astype(BF16)
        dqkv[:, key_cols(h)] = dot_tn(d_raw_s[...], qk[:, query_cols(h)]).astype(BF16)
        dqkv[:, 128 + h * VDIM : 128 + (h + 1) * VDIM] = dot_tn(
            mass_s[...], dmixed[:, vcols]
        ).astype(BF16)

    def fill_qkv(grad):
        load_normed.wait()

        def block(half, lanes):
            top = dot_tn(n2[:, lanes], dqkv[...])
            half[..., 0:640] = top.astype(BF16).reshape(2, 2, 4, 64, 640)

        halves(grad, block)

    def done_qkv(total):
        o_query[...] = total[:, 0:64]
        o_key[...] = total[:, 64:128]
        o_value[...] = total[:, 128:640]
        part = weigh(total[:, 0:128], wqk[:, chunk])
        rows_v = wv[pl.ds(pl.multiple_of(dp * 64, 64), 64), :].astype(F32)
        part += jnp.sum(total[:, 128:640] * rows_v, axis=1, keepdims=True)
        gsum[1] = jnp.broadcast_to(part, gsum.shape[1:])

    pump.add(640, fill_qkv, done_qkv)
    pump.tick()

    def normed_back(rows):
        acc[rows, :] = dot_nt(dqkv[rows, 128:640], wv[...])

    each(seq, seq, normed_back)
    add_product(acc, dqkv.at[:, 0:128], wqk, False)
    scatter_in = Scatter(acc, bufs, mp_send.at[7], mp_recv.at[7])
    pump.tick()
    scatter_in.start_near(0)

    def output(rows, total):
        block_out[rows, :] = (h1[rows, :] + total).astype(BF16)

    pump.tick()
    scatter_out.finish_far(output)
    pump.tick()
    scatter_in.start_far()
    scatter_in.start_near(1)


    def norm_one_back(rows, d_normed):
        values = x_own[rows, :].astype(F32)
        inverse = norm_rows(values)
        unit = values * inverse
        e = d_normed * gain_a
        grad_in[rows, :] += inverse * (
            e - unit * jnp.mean(e * unit, axis=-1, keepdims=True)
        )

    pump.tick()
    scatter_in.finish(norm_one_back)
    pump.tick()

    pick = (row + (dp % 2) * 64) == lane
    for i in (0, 1):
        line = jnp.sum(jnp.where(pick, gsum[1 - i], 0.0), axis=0, keepdims=True)
        gline[8 * i : 8 * i + 8, :] = jnp.broadcast_to(line, (8, 128))
    others = (mate, pair, device(x, yh, z, 1 - yl, 1 - core))
    shares = [
        remote(gline, glines.at[i], mp_send.at[8, i], mp_recv.at[8, i], target)
        for i, target in enumerate(others)
    ]
    for c in shares:
        c.start()
    for c in shares:
        c.wait()
    total = gline[...] + glines[0] + glines[1] + glines[2]
    first = (dp % 2) * 64 + mp * 16
    for i, gain in enumerate((gain_attn, gain_ffn)):
        line = total[8 * i : 8 * i + 8, :] / gain[:, chunk]
        gains_out[i : i + 1, :] = pltpu.roll(line, (128 - first) % 128, 1)[0:1, :]


def layer(lengths, x_own, g_own, gain_attn, gain_ffn, wq, wk, wv, wo, wg, wu, wd):
    tok, width = x_own.shape
    seq, ff = 4 * tok, wd.shape[0]
    tiles = -(-ff // FF_TILE)
    pad = -(-(ff % FF_TILE) // 128) * 128
    wide = 3 * FF_TILE
    vmem, hbm = pl.BlockSpec(memory_space=pltpu.VMEM), pl.BlockSpec(memory_space=pl.ANY)
    shape = jax.ShapeDtypeStruct
    sems = pltpu.SemaphoreType.DMA
    scratch = [
        pltpu.VMEM((seq, width), BF16),
        pltpu.VMEM((seq, width), BF16),
        pltpu.VMEM((seq, width), BF16),
        pltpu.VMEM((tok, width), BF16),
        pltpu.VMEM((tok, width), F32),
        pltpu.VMEM((2, 2 * FF_TILE, width), BF16),
        pltpu.VMEM((2, FF_TILE, width), BF16),
        pltpu.VMEM((128, width), BF16),
        pltpu.VMEM(wv.shape, BF16),
        pltpu.VMEM((2, 2, FF_TILE, 128), BF16),
        pltpu.VMEM((seq, 128), BF16),
        pltpu.VMEM((seq, 1024), BF16),
        pltpu.VMEM((seq, 512), BF16),
        pltpu.VMEM((seq, 512), BF16),
        pltpu.VMEM((seq, 512), BF16),
        pltpu.VMEM((seq, 128), F32),
        pltpu.VMEM((seq, seq), BF16),
        pltpu.VMEM((seq, 256), BF16),
        pltpu.VMEM((seq, width), F32),
        pltpu.VMEM((tiles, seq, FF_TILE), BF16),
        pltpu.VMEM((tiles - 1, seq, 2 * FF_TILE), BF16),
        pltpu.VMEM((seq, 2 * pad), BF16),
        pltpu.VMEM((seq, 512), F32),
        pltpu.VMEM((-(-tiles // 2), seq, 2 * FF_TILE), BF16),
        pltpu.VMEM((seq, 512), BF16),
        pltpu.VMEM((seq, 640), BF16),
        pltpu.VMEM((2, 64, 128), F32),
        pltpu.VMEM((16, 128), F32),
        pltpu.VMEM((3, 16, 128), F32),
        pltpu.VMEM((tok, width), BF16),
        pltpu.VMEM((2, tok, width), BF16),
        pltpu.VMEM((tok, width), BF16),
        pltpu.VMEM((tok, width), BF16),
    ]
    scratch += [pltpu.VMEM((4, 2, 4, 64, wide), BF16) for _ in range(SETS)]
    scratch += [b for _ in range(SETS) for b in sum_buffers(wide)[:5]]
    scratch += [
        sems((SETS, 2, 13)),
        sems((SETS, 2, 13)),
        pltpu.SemaphoreType.REGULAR((SETS,)),
        sems((9, 2 * PARTS + 1)),
        sems((9, 2 * PARTS + 1)),
        sems((17,)),
    ]
    return pl.pallas_call(
        layer_kernel,
        out_shape=[
            shape((tok, width), BF16),
            shape((tok, width), F32),
            shape((2, 128), F32),
            shape((64, wq.shape[0]), F32),
            shape((64, wk.shape[0]), F32),
            shape((64, wv.shape[1]), F32),
            shape((64, wo.shape[0]), F32),
            shape((64, ff), F32),
            shape((64, ff), F32),
            shape((64, ff), F32),
            shape((seq, width), BF16),
        ],
        in_specs=[pl.BlockSpec(memory_space=pltpu.SMEM)] + [vmem] * 4 + [hbm] * 7,
        out_specs=[vmem] * 10 + [hbm],
        scratch_shapes=scratch,
        compiler_params=pltpu.CompilerParams(
            collective_id=0, has_side_effects=True, vmem_limit_bytes=65400 << 10
        ),
        name="layer",
    )(lengths, x_own, g_own, gain_attn, gain_ffn, wq, wk, wv, wo, wg, wu, wd)


def hand_out_kernel(n, *refs):
    sems = refs[2 * n + 3]
    copies = [pltpu.make_async_copy(refs[i], refs[n + 1 + i], sems.at[i]) for i in range(n)]
    for c in copies:
        c.start()
    gains, first, second = refs[n], refs[2 * n + 1], refs[2 * n + 2]
    first[...] = gains[0:1, 0:16]
    second[...] = gains[1:2, 0:16]
    for c in copies:
        c.wait()


def hand_out(arrays, gains):
    n = len(arrays)
    vmem, hbm = pl.BlockSpec(memory_space=pltpu.VMEM), pl.BlockSpec(memory_space=pl.ANY)
    shape = jax.ShapeDtypeStruct
    return pl.pallas_call(
        functools.partial(hand_out_kernel, n),
        out_shape=[shape(a.shape, a.dtype) for a in arrays] + [shape((1, 16), F32)] * 2,
        in_specs=[vmem] * (n + 1),
        out_specs=[hbm] * n + [vmem] * 2,
        scratch_shapes=[pltpu.SemaphoreType.DMA((n,))],
        name="hand_out",
    )(*arrays, gains)


def on_device(
    block_input,
    lengths,
    gain_attn,
    gain_ffn,
    w_query,
    w_key,
    w_value,
    w_out,
    w_gate,
    w_up,
    w_down,
    cotangent,
):
    width = block_input.shape[-1]
    out = layer(
        lengths,
        block_input.reshape(-1, width),
        cotangent.reshape(-1, width),
        gain_attn.reshape(1, -1),
        gain_ffn.reshape(1, -1),
        w_query.T,
        w_key.T,
        w_value,
        w_out,
        w_gate.T,
        w_up.T,
        w_down,
    )
    (
        block_output,
        grad_input,
        grad_query,
        grad_key,
        grad_value,
        grad_out,
        grad_gate,
        grad_up,
        grad_down,
        grad_gain_attn,
        grad_gain_ffn,
    ) = hand_out([out[0], out[1], *out[3:10]], out[2])
    return (
        block_output.reshape(block_input.shape),
        grad_input.reshape(block_input.shape),
        grad_gain_attn.reshape(-1),
        grad_gain_ffn.reshape(-1),
        grad_query,
        grad_key,
        grad_value,
        grad_out.T,
        grad_gate,
        grad_up,
        grad_down.T,
    )


def solution(mesh):
    return jax.shard_map(
        on_device,
        mesh=mesh,
        in_specs=(
            P("dp", "mp", None),
            P("dp", None),
            P(),
            P(),
            P(None, "mp"),
            P(None, "mp"),
            P(None, "mp"),
            P("mp", None),
            P(None, "mp"),
            P(None, "mp"),
            P("mp", None),
            P("dp", "mp", None),
        ),
        out_specs=(
            P("dp", "mp", None),
            P("dp", "mp", None),
            P(("dp", "mp")),
            P(("dp", "mp")),
            P("dp", "mp"),
            P("dp", "mp"),
            P("dp", "mp"),
            P("mp", "dp"),
            P("dp", "mp"),
            P("dp", "mp"),
            P("mp", "dp"),
        ),
        check_vma=False,
    )
```

```python
import functools

import jax
import jax.numpy as jnp
from jax import lax
from jax.experimental import pallas as pl
from jax.experimental.pallas import tpu as pltpu
from jax.sharding import PartitionSpec as P

MESH = pl.DeviceIdType.MESH
F32 = jnp.float32
BF16 = jnp.bfloat16

FEAT = 16
VDIM = 128
WINDOW = 64
SETS = 4
FF_TILE = 256
PARTS = 4

norm_eps = 1e-05
masked_score = -1e30


def place():
    dp, mp = lax.axis_index("dp"), lax.axis_index("mp")
    return dp // 8, (dp // 4) % 2, dp % 4, mp // 2, mp % 2


def device(x, yh, z, yl, core):
    return (x * 8 + yh * 4 + z, yl * 2 + core)


def greet(devices):
    barrier = pltpu.get_barrier_semaphore()
    for target in devices:
        pl.semaphore_signal(barrier, inc=1, device_id=target, device_id_type=MESH)
    pl.semaphore_wait(barrier, len(devices))


def remote(src, dst, send_sem, recv_sem, target):
    return pltpu.make_async_remote_copy(
        src_ref=src,
        dst_ref=dst,
        send_sem=send_sem,
        recv_sem=recv_sem,
        device_id=target,
        device_id_type=MESH,
    )


def dot_nn(a, b):
    return lax.dot_general(a, b, (((1,), (0,)), ((), ())), preferred_element_type=F32)


def dot_nt(a, b):
    return lax.dot_general(a, b, (((1,), (1,)), ((), ())), preferred_element_type=F32)


def dot_tn(a, b):
    return lax.dot_general(a, b, (((0,), (0,)), ((), ())), preferred_element_type=F32)


def each(count, step, body, base=0):
    def run(i, _):
        body(pl.ds(pl.multiple_of(base + i * step, step), step))
        return 0

    lax.fori_loop(0, count // step, run, 0)


class Gather:
    def __init__(self, own, full, send, recv):
        self.own, self.full, self.send, self.recv = own, full, send, recv
        x, yh, z, yl, core = place()
        self.mate, self.pair = device(x, yh, z, yl, 1 - core), device(x, yh, z, 1 - yl, core)
        self.tok = own.shape[0]
        self.piece = self.tok // PARTS
        self.mine, self.far = yl * 2 + core, (1 - yl) * 2 + core

    def rows(self, part, i):
        start = part * self.tok + i * self.piece
        return pl.ds(pl.multiple_of(start, self.piece), self.piece)

    def far_copy(self, i):
        return remote(
            self.own.at[pl.ds(i * self.piece, self.piece)],
            self.full.at[self.rows(self.mine, i)],
            self.send.at[i],
            self.recv.at[i],
            self.pair,
        )

    def near_copy(self):
        return remote(
            self.own,
            self.full.at[pl.ds(pl.multiple_of(self.mine * self.tok, self.tok), self.tok)],
            self.send.at[PARTS],
            self.recv.at[PARTS],
            self.mate,
        )

    def pass_copy(self, i):
        rows = self.rows(self.far, i)
        return remote(
            self.full.at[rows],
            self.full.at[rows],
            self.send.at[PARTS + 1 + i],
            self.recv.at[PARTS + 1 + i],
            self.mate,
        )

    def start(self):
        for i in range(PARTS):
            self.far_copy(i).start()
        self.start_near()

    def start_near(self):
        self.near_copy().start()
        at = pl.ds(pl.multiple_of(self.mine * self.tok, self.tok), self.tok)
        self.full[at, :] = self.own[...]

    def finish_near(self):
        self.near_copy().wait()

    def finish_far(self):
        for i in range(PARTS):
            self.far_copy(i).wait_recv()
            self.pass_copy(i).start()
        for i in range(PARTS):
            self.far_copy(i).wait_send()
            self.pass_copy(i).wait()

    def finish(self):
        self.finish_near()
        self.finish_far()


class Scatter:
    def __init__(self, part, bufs, send, recv):
        self.part = part
        self.near_out, near_in, self.far_out, self.far_in = bufs
        if near_in is not None:
            self.near_in = [near_in.at[k] for k in (0, 1)]
        self.send, self.recv = send, recv
        x, yh, z, yl, core = place()
        self.yl, self.core = yl, core
        self.mate, self.pair = device(x, yh, z, yl, 1 - core), device(x, yh, z, 1 - yl, core)
        self.tok = self.far_in.shape[0]
        self.piece = self.tok // PARTS

    def near_copy(self, k):
        return remote(
            self.near_out, self.near_in[k], self.send.at[k], self.recv.at[k], self.mate
        )

    def far_copy(self, i):
        rows = pl.ds(i * self.piece, self.piece)
        return remote(
            self.far_out.at[rows],
            self.far_in.at[rows],
            self.send.at[2 + i],
            self.recv.at[2 + i],
            self.pair,
        )

    def start_near(self, k):
        side = self.yl if k else 1 - self.yl
        start = pl.multiple_of((side * 2 + 1 - self.core) * self.tok, self.tok)

        if k:
            self.near_copy(0).wait_send()

        def cast(rows):
            self.near_out[rows, :] = self.part[
                pl.ds(pl.multiple_of(start + rows.start, 16), 16), :
            ].astype(BF16)

        each(self.tok, 16, cast)
        self.near_copy(k).start()

    def start_far(self):
        self.near_copy(0).wait_recv()
        far = pl.multiple_of(((1 - self.yl) * 2 + self.core) * self.tok, self.tok)
        for i in range(PARTS):

            def join(rows, i=i):
                at = pl.ds(pl.multiple_of(i * self.piece + rows.start, 16), 16)
                src = pl.ds(pl.multiple_of(far + i * self.piece + rows.start, 16), 16)
                self.far_out[at, :] = (
                    self.part[src, :] + self.near_in[0][at, :].astype(F32)
                ).astype(BF16)

            each(self.piece, 16, join)
            self.far_copy(i).start()

    def fold(self, use):
        self.near_copy(1).wait_recv()
        own = pl.multiple_of((self.yl * 2 + self.core) * self.tok, self.tok)

        def join(rows):
            src = pl.ds(pl.multiple_of(own + rows.start, 16), 16)
            use(rows, self.part[src, :] + self.near_in[1][rows, :].astype(F32))

        each(self.tok, 16, join)
        self.near_copy(1).wait_send()

    def finish_far(self, use):
        for i in range(PARTS):
            self.far_copy(i).wait()
        each(self.tok, 16, lambda rows: use(rows, self.far_in[rows, :].astype(F32)))

    def finish(self, use, after=None):
        self.near_copy(1).wait_recv()
        own = pl.multiple_of((self.yl * 2 + self.core) * self.tok, self.tok)
        for i in range(PARTS):
            self.far_copy(i).wait_recv()

            def join(rows, i=i):
                at = pl.ds(pl.multiple_of(i * self.piece + rows.start, 16), 16)
                src = pl.ds(pl.multiple_of(own + i * self.piece + rows.start, 16), 16)
                use(
                    at,
                    self.part[src, :]
                    + self.near_in[1][at, :].astype(F32)
                    + self.far_in[at, :].astype(F32),
                )

            each(self.piece, 16, join)
            if after is not None:
                after(i)
        self.near_copy(1).wait_send()
        for i in range(PARTS):
            self.far_copy(i).wait_send()


def add_into(dst, terms, rows, step):
    def body(i, _):
        at = pl.ds(pl.multiple_of(i * step, step), step)
        total = dst[at, :].astype(F32)
        for term in terms:
            total = total + term[at, :].astype(F32)
        dst[at, :] = total.astype(dst.dtype)
        return 0

    lax.fori_loop(0, rows // step, body, 0)


class RowSum:
    def __init__(self, grad, bufs, send, recv):
        self.grad = grad
        self.t1, self.m1, self.t2, self.m2, self.last = bufs
        self.send, self.recv = send, recv
        self.x, self.yh, self.z, self.yl, self.core = place()

    def near(self, path, stage, step):
        if (path == 0) == (stage == 0):
            return device((self.x + step + 4) % 4, self.yh, self.z, self.yl, self.core)
        return device(self.x, self.yh, (self.z + step + 4) % 4, self.yl, self.core)

    def at(self, path, stage):
        return self.x if (path == 0) == (stage == 0) else self.z

    def block(self, path, b, k):
        return self.grad.at[b, 0, k] if path == 0 else self.grad.at[k, 1, b]

    def copy(self, src, dst, path, slot, target):
        return remote(src, dst, self.send.at[path, slot], self.recv.at[path, slot], target)

    def transit_one(self, path, side):
        b = (self.at(path, 0) + 2) % 4
        return self.copy(
            self.block(path, b, pl.ds(2 * side, 2)),
            self.t1.at[path, side],
            path,
            side,
            self.near(path, 0, 1 - 2 * side),
        )

    def main_one(self, path, side, half):
        step = 1 - 2 * side
        b = (self.at(path, 0) + step + 4) % 4
        src = (
            self.t1.at[path, side]
            if half == side
            else self.block(path, b, pl.ds(2 * half, 2))
        )
        return self.copy(
            src,
            self.m1.at[path, side, pl.ds(2 * half, 2)],
            path,
            2 + 2 * side + half,
            self.near(path, 0, step),
        )

    def transit_two(self, path, side):
        k = (self.at(path, 1) + 2) % 4
        return self.copy(
            self.m1.at[path, 0, k, pl.ds(32 * side, 32)],
            self.t2.at[path, side],
            path,
            6 + side,
            self.near(path, 1, 1 - 2 * side),
        )

    def main_two(self, path, side, half):
        step = 1 - 2 * side
        k = (self.at(path, 1) + step + 4) % 4
        rows = pl.ds(32 * half, 32)
        src = self.t2.at[path, side] if half == side else self.m1.at[path, 0, k, rows]
        return self.copy(
            src,
            self.m2.at[path, side, rows],
            path,
            8 + 2 * side + half,
            self.near(path, 1, step),
        )

    def last_copy(self):
        target = device(self.x, 1 - self.yh, self.z, self.yl, self.core)
        return self.copy(self.m2.at[1 - self.yh, 0], self.last, 0, 12, target)

    def start_one(self):
        for path in (0, 1):
            for side in (0, 1):
                self.transit_one(path, side).start()
        for path in (0, 1):
            for side in (0, 1):
                self.main_one(path, side, 1 - side).start()

    def pass_one(self):
        for path in (0, 1):
            for side in (0, 1):
                self.transit_one(path, side).wait_recv()
                b = (self.at(path, 0) + 1 - 2 * side + 4) % 4
                for k in (0, 1):
                    add_into(
                        self.t1.at[path, side, k],
                        (self.block(path, b, 2 * side + k),),
                        64,
                        64,
                    )
                self.main_one(path, side, side).start()

    def join_one(self):
        for path in (0, 1):
            for side in (0, 1):
                for half in (0, 1):
                    self.main_one(path, side, half).wait_recv()
            b = self.at(path, 0)

            def body(k, _):
                add_into(
                    self.m1.at[path, 0, k],
                    (self.m1.at[path, 1, k], self.block(path, b, k)),
                    64,
                    64,
                )
                return 0

            lax.fori_loop(0, 4, body, 0)
            for side in (0, 1):
                self.transit_two(path, side).start()
            for side in (0, 1):
                self.main_two(path, side, 1 - side).start()

    def pass_two(self):
        for path in (0, 1):
            for side in (0, 1):
                self.transit_two(path, side).wait_recv()
                k = (self.at(path, 1) + 1 - 2 * side + 4) % 4
                add_into(
                    self.t2.at[path, side],
                    (self.m1.at[path, 0, k, pl.ds(32 * side, 32)],),
                    32,
                    32,
                )
                self.main_two(path, side, side).start()

    def join_two(self):
        for path in (0, 1):
            for side in (0, 1):
                for half in (0, 1):
                    self.main_two(path, side, half).wait_recv()
            k = self.at(path, 1)
            add_into(self.m2.at[path, 0], (self.m2.at[path, 1], self.m1.at[path, 0, k]), 64, 64)
        self.last_copy().start()

    def finish(self, use):
        self.last_copy().wait_recv()
        use(self.m2[self.yh, 0].astype(F32) + self.last[...].astype(F32))
        for path in (0, 1):
            for side in (0, 1):
                self.transit_one(path, side).wait_send()
                self.transit_two(path, side).wait_send()
                for half in (0, 1):
                    self.main_one(path, side, half).wait_send()
                    self.main_two(path, side, half).wait_send()
        self.last_copy().wait_send()


def sum_buffers(width):
    return [
        pltpu.VMEM((2, 2, 2, 64, width), BF16),
        pltpu.VMEM((2, 2, 4, 64, width), BF16),
        pltpu.VMEM((2, 2, 32, width), BF16),
        pltpu.VMEM((2, 2, 64, width), BF16),
        pltpu.VMEM((64, width), BF16),
        pltpu.SemaphoreType.DMA((2, 13)),
        pltpu.SemaphoreType.DMA((2, 13)),
    ]


def sum_neighbours():
    x, yh, z, yl, core = place()
    return (
        device((x + 1) % 4, yh, z, yl, core),
        device((x + 3) % 4, yh, z, yl, core),
        device(x, yh, (z + 1) % 4, yl, core),
        device(x, yh, (z + 3) % 4, yl, core),
        device(x, 1 - yh, z, yl, core),
    )


class Pump:
    def __init__(self, grads, sets, sends, recvs, credit):
        self.grads, self.sets, self.sends, self.recvs, self.credit = (
            grads,
            sets,
            sends,
            recvs,
            credit,
        )
        self.units, self.turn = [], 0

    def add(self, width, fill, done, loads=()):
        slot = len(self.units) % SETS
        lanes = pl.ds(0, width)

        def view(ref):
            return ref.at[tuple([slice(None)] * (len(ref.shape) - 1) + [lanes])]

        rows = RowSum(
            view(self.grads[slot]),
            [view(b) for b in self.sets[slot]],
            self.sends.at[slot],
            self.recvs.at[slot],
        )
        self.units.append((rows, fill, done, loads))

    def stage(self, index, number):
        rows, fill, done, loads = self.units[index]
        slot = index % SETS
        if number == 0:
            fill(self.grads[slot])
        elif number == 1:
            if index >= SETS:
                pl.semaphore_wait(self.credit.at[slot], 5)
            rows.start_one()
        elif number < 6:
            if number == 5:
                for c in loads:
                    c.start()
            (rows.pass_one, rows.join_one, rows.pass_two, rows.join_two)[number - 2]()
        else:
            rows.finish(done)
            if index + SETS < UNITS:
                for target in sum_neighbours():
                    pl.semaphore_signal(
                        self.credit.at[slot], inc=1, device_id=target, device_id_type=MESH
                    )

    def tick(self):
        for index, number in PLAN[self.turn]:
            self.stage(index, number)
        self.turn += 1


UNITS = 8
PLAN = (
    (),
    ((0, 0), (0, 1),),
    (),
    ((1, 0), (1, 1),),
    ((0, 2),),
    (),
    (),
    ((2, 0), (1, 2), (2, 1),),
    (),
    ((0, 3),),
    (),
    (),
    ((1, 3),),
    (),
    ((2, 2), (3, 0), (0, 4), (3, 1), (1, 4), (2, 3), (0, 5), (3, 2),),
    ((0, 6), (4, 0), (1, 5), (2, 4), (4, 1),),
    (),
    (),
    (),
    ((3, 3),),
    (),
    ((1, 6),),
    ((2, 5), (5, 0), (5, 1), (4, 2), (2, 6), (3, 4),),
    (),
    (),
    (),
    ((5, 2),),
    (),
    (),
    (),
    ((6, 0), (3, 5), (4, 3), (6, 1),),
    (),
    ((5, 3), (3, 6),),
    ((4, 4), (7, 0), (7, 1),),
    ((6, 2),),
    ((5, 4), (4, 5), (7, 2), (4, 6), (6, 3), (5, 5), (7, 3),),
    ((6, 4), (5, 6), (7, 4), (6, 5), (7, 5), (6, 6), (7, 6),),
)


def norm_rows(values):
    return lax.rsqrt(jnp.mean(values * values, axis=-1, keepdims=True) + norm_eps)


def doc_of(positions, ends):
    return sum((positions >= e).astype(jnp.int32) for e in ends)


def add_product(total, left, right, first):
    for j in range(0, total.shape[1], 512):
        cols = slice(j, j + 512)
        part = dot_nn(left[...], right[:, cols])
        if first:
            total[:, cols] = part
        else:
            total[:, cols] += part


def layer_kernel(
    lengths,
    x_own,
    g_own,
    gain_attn,
    gain_ffn,
    wq_hbm,
    wk_hbm,
    wv_hbm,
    wo_hbm,
    wg_hbm,
    wu_hbm,
    wd_hbm,
    block_out,
    grad_in,
    gains_out,
    o_query,
    o_key,
    o_value,
    o_out,
    o_gate,
    o_up,
    o_down,
    normed_hbm,
    n2,
    g_all,
    da_all,
    own,
    h1,
    w_gu,
    w_d,
    wqk,
    wv,
    cols_gu,
    qk,
    v_ones,
    mixed,
    linear,
    windowed,
    stats,
    mask,
    band,
    acc,
    acts,
    dgus,
    dgu_last,
    gu,
    d_acts,
    dqk,
    gsum,
    gline,
    glines,
    near_out,
    near_in,
    far_out,
    far_in,
    *rest,
):
    grads = rest[:SETS]
    sets = [rest[SETS + 5 * i : SETS + 5 * i + 5] for i in range(SETS)]
    sends, recvs, credit, mp_send, mp_recv, wsem = rest[6 * SETS :]
    x, yh, z, yl, core = place()
    dp, mp = lax.axis_index("dp"), lax.axis_index("mp")
    mate, pair = device(x, yh, z, yl, 1 - core), device(x, yh, z, 1 - yl, core)
    seq, width = n2.shape
    ff = wd_hbm.shape[0]
    full_tiles = ff // FF_TILE
    last = ff - full_tiles * FF_TILE
    pad = -(-last // 128) * 128
    order = [full_tiles] + list(range(full_tiles))
    heads = wv.shape[1] // VDIM
    ends = [lengths[0, 0], lengths[0, 0] + lengths[0, 1]]
    ends.append(ends[1] + lengths[0, 2])
    near_base = pl.multiple_of(yl * 256, 256)
    far_base = pl.multiple_of((1 - yl) * 256, 256)

    def valid(t):
        return last if t == full_tiles else FF_TILE

    def wide(t):
        return pad if t == full_tiles else FF_TILE

    dmixed, dv = d_acts.at[0], d_acts.at[1]

    def dgu(t):
        return dgu_last if t == full_tiles else dgus.at[t]

    def load(src, dst, i):
        return pltpu.make_async_copy(src, dst, wsem.at[i])

    def gu_loads(i):
        t, s = order[i], i % 2
        rows = pl.ds(t * FF_TILE, valid(t))
        return [
            load(wg_hbm.at[rows], w_gu.at[s, pl.ds(0, valid(t))], 3 * s),
            load(wu_hbm.at[rows], w_gu.at[s, pl.ds(wide(t), valid(t))], 3 * s + 1),
        ]

    def down_load(i, sem):
        t, s = order[i], i % 2
        return load(
            wd_hbm.at[pl.ds(t * FF_TILE, valid(t))], w_d.at[s, pl.ds(0, valid(t))], sem + s
        )

    small = [
        load(wq_hbm, wqk.at[pl.ds(0, 64)], 8),
        load(wk_hbm, wqk.at[pl.ds(64, 64)], 9),
        load(wv_hbm, wv, 10),
        load(wo_hbm, w_gu.at[1], 11),
    ]
    chunk = pl.ds(pl.multiple_of((dp // 2) * 128, 128), 128)

    def columns(t):
        rows, some, s = pl.ds(t * FF_TILE, valid(t)), pl.ds(0, valid(t)), order.index(t) % 2
        return [
            load(w.at[rows, chunk], cols_gu.at[s, i, some], 12 + 2 * s + i)
            for i, w in enumerate((wg_hbm, wu_hbm))
        ]

    for c in small:
        c.start()
    gain_a, gain_f = gain_attn[...], gain_ffn[...]
    tok = own.shape[0]

    def norm_one(rows):
        values = x_own[rows, :].astype(F32)
        own[rows, :] = (values * norm_rows(values) * gain_a).astype(BF16)

    each(tok, 16, norm_one)
    greet(sum_neighbours() + (mate, pair, device(x, yh, z, 1 - yl, 1 - core)))
    gather_one = Gather(own, da_all, mp_send.at[0], mp_recv.at[0])
    gather_one.start()
    gather_g = Gather(g_own, g_all, mp_send.at[1], mp_recv.at[1])
    gather_g.start()
    for at in (pl.ds(last, pad - last), pl.ds(pad + last, pad - last)):
        w_gu[0, at, :] = jnp.zeros((pad - last, width), BF16)
    w_d[0, pl.ds(last, pad - last), :] = jnp.zeros((pad - last, width), BF16)
    for c in gu_loads(0):
        c.start()
    for i in (0, 1):
        down_load(i, 6).start()
    for c in small:
        c.wait()

    def masks(rows):
        t = rows.start + lax.broadcasted_iota(jnp.int32, (32, 1), 0)
        col = lax.broadcasted_iota(jnp.int32, (1, seq), 1)
        seen = (t >= col) & (doc_of(t, ends) == doc_of(col, ends))
        mask[rows, :] = jnp.where(seen, 1.0, 0.0).astype(BF16)
        col = band_start(rows.start // 128) + lax.broadcasted_iota(jnp.int32, (1, 256), 1)
        seen = (t >= col) & (t - col < WINDOW) & (doc_of(t, ends) == doc_of(col, ends))
        band[rows, :] = jnp.where(seen, 0.0, masked_score).astype(BF16)

    def band_start(block):
        return pl.multiple_of(jnp.maximum(block - 1, 0) * 128, 128)

    each(seq, 32, masks)
    for h in range(heads):
        v_ones[:, 256 * h + 128 : 256 * h + 256] = jnp.ones((seq, 128), BF16)
    shrink = jnp.where(
        lax.broadcasted_iota(jnp.int32, (1, 128), 1) < 64, FEAT ** (-0.5), 1.0
    )

    def project(rows):
        qk[rows, :] = (dot_nt(da_all[rows, :], wqk[...]) * shrink).astype(BF16)
        value = dot_nn(da_all[rows, :], wv[...]).astype(BF16)
        for h in range(heads):
            v_ones[rows, 256 * h : 256 * h + 128] = value[:, 128 * h : 128 * h + 128]

    gather_one.finish_near()
    each(256, 256, project, near_base)
    gather_one.finish_far()
    each(256, 256, project, far_base)
    keep_normed = load(da_all, normed_hbm, 16)
    keep_normed.start()

    def query_cols(h):
        return slice(h * FEAT, (h + 1) * FEAT)

    def key_cols(h):
        return slice(64 + h * FEAT, 64 + (h + 1) * FEAT)

    def value_cols(h):
        return slice(h * VDIM, (h + 1) * VDIM)

    def attend_forward(base, hs):
        half = [pl.ds(pl.multiple_of(base + 128 * i, 128), 128) for i in (0, 1)]
        first = [band_start(base // 128 + i) for i in (0, 1)]

        def raw_at(h, rows):
            return gu.at[rows]

        for h in hs:
            raw_at(h, slice(0, 256))[...] = dot_nt(
                qk[pl.ds(base, 256), query_cols(h)], qk[:, key_cols(h)]
            )
        for h in hs:

            def taylor(sub, h=h):
                at = pl.ds(pl.multiple_of(base + sub.start, 64), 64)
                score = gu[sub, :]
                dgus[h, sub, :] = ((0.5 * score + 1.0) * score + 1.0).astype(BF16) * mask[at, :]

            each(256, 64, taylor)
        for h in hs:
            both = slice(256 * h, 256 * h + 256)
            one = dot_nn(dgus[h, 0:256, :], v_ones[:, both])
            for i in (0, 1):
                sub = slice(128 * i, 128 * i + 128)
                scores = raw_at(h, sub)[:, pl.ds(first[i], 256)] + band[half[i], :].astype(F32)
                top = jnp.max(scores, axis=1, keepdims=True)
                weights = jnp.exp(scores - top).astype(BF16)
                two = dot_nn(weights, v_ones[pl.ds(first[i], 256), both])
                inv_den = 1.0 / one[sub, 128:256]
                lin = one[sub, 0:128] * inv_den
                win = two[:, 0:128] / two[:, 128:256]
                linear[half[i], value_cols(h)] = lin.astype(BF16)
                windowed[half[i], value_cols(h)] = win.astype(BF16)
                mixed[half[i], value_cols(h)] = (lin + win).astype(BF16)
                stats[half[i], h : h + 1] = inv_den[:, 0:1]
                stats[half[i], heads + h : heads + h + 1] = top + jnp.log(two[:, 128:129])

    def project_out(rows):
        acc[rows, :] = dot_nn(mixed[rows, :], w_gu[1])

    bufs = (near_out, near_in, far_out, far_in)
    scatter_one = Scatter(acc, bufs, mp_send.at[2], mp_recv.at[2])
    for h in range(heads):
        attend_forward(far_base, (h,))
    each(256, 256, project_out, far_base)
    scatter_one.start_near(0)
    for h in range(heads):
        attend_forward(near_base, (h,))
        if h == 1:
            scatter_one.start_far()
    each(256, 256, project_out, near_base)
    scatter_one.start_near(1)
    for c in gu_loads(1):
        c.start()
    gather_g.finish()
    keep_normed.wait()

    gather_two = Gather(own, n2, mp_send.at[3], mp_recv.at[3])

    def norm_two(rows, total):
        hidden = x_own[rows, :].astype(F32) + total
        h1[rows, :] = hidden
        own[rows, :] = (hidden * norm_rows(hidden) * gain_f).astype(BF16)

    scatter_one.finish(norm_two, lambda i: gather_two.far_copy(i).start())
    gather_two.start_near()

    def at_act(t):
        return slice(FF_TILE * (t % 2), FF_TILE * (t % 2) + wide(t))

    for i, t in enumerate(order):
        down_load(i, 6).wait()

        def back_down(rows, i=i, t=t, p=wide(t)):
            d_acts[t // 2, rows, at_act(t)] = dot_nt(g_all[rows, :], w_d[i % 2, 0:p]).astype(BF16)

        each(seq, seq, back_down)
        if i + 2 < len(order):
            down_load(i + 2, 6).start()
    for i in (0, 1):
        down_load(i, 6).start()
    gather_two.finish()

    load_normed = load(normed_hbm, n2, 1)
    pump = Pump(grads, sets, sends, recvs, credit)
    lane = lax.broadcasted_iota(jnp.int32, (64, 128), 1)
    row = lax.broadcasted_iota(jnp.int32, (64, 128), 0)
    own_lane = lane == row + (dp % 2) * 64

    def weigh(total, block):
        full = dot_nn(total.astype(BF16), block)
        return jnp.sum(jnp.where(own_lane, full, 0.0), axis=1, keepdims=True)

    def halves(grad, block):
        def run(i, _):
            block(grad.at[pl.ds(2 * i, 2)], pl.ds(pl.multiple_of(i * 1024, 1024), 1024))
            return 0

        lax.fori_loop(0, 2, run, 0)

    def fill_ffn(t):
        p = wide(t)

        def fill(grad):
            def top(half, lanes):
                part = dot_tn(n2[:, lanes], dgu(t)[...])
                half[..., 0 : 2 * p] = part.astype(BF16).reshape(2, 2, 4, 64, 2 * p)

            def bottom(half, lanes):
                part = dot_tn(g_all[:, lanes], acts[t, :, 0:p])
                half[..., 2 * p : 3 * p] = part.astype(BF16).reshape(2, 2, 4, 64, p)

            halves(grad, top)
            halves(grad, bottom)
            if t == full_tiles - 1:
                load_normed.start()

        return fill

    def done_ffn(t):
        def done(total):
            n, p = valid(t), wide(t)
            cols = slice(t * FF_TILE, t * FF_TILE + n)
            value_gate, value_up = total[:, 0:n], total[:, p : p + n]
            o_gate[:, cols] = value_gate
            o_up[:, cols] = value_up
            o_down[:, cols] = total[:, 2 * p : 2 * p + n]
            for c in columns(t):
                c.wait()
            s = order.index(t) % 2
            column = weigh(value_gate, cols_gu[s, 0, 0:n, :])
            column += weigh(value_up, cols_gu[s, 1, 0:n, :])
            if t == full_tiles:
                gsum[0] = jnp.broadcast_to(column, gsum.shape[1:])
            else:
                gsum[0] += jnp.broadcast_to(column, gsum.shape[1:])

        return done

    for i, t in enumerate(order):
        s, p = i % 2, wide(t)
        pump.tick()
        for c in gu_loads(i):
            c.wait()

        def forward(rows, t=t, s=s, p=p):
            gu[:, 0 : 2 * p] = dot_nt(n2[rows, :], w_gu[s, 0 : 2 * p])

            def pointwise(sub):
                at = pl.ds(pl.multiple_of(rows.start + sub.start, 128), 128)
                gate, up = gu[sub, 0:p], gu[sub, p : 2 * p]
                d_act = d_acts[t // 2, at, at_act(t)].astype(F32)
                sig = jax.nn.sigmoid(gate)
                silu = gate * sig
                acts[t, at, 0:p] = (silu * up).astype(BF16)
                dgu(t)[at, 0:p] = (d_act * up * (sig * (1.0 + gate * (1.0 - sig)))).astype(BF16)
                dgu(t)[at, p : 2 * p] = (d_act * silu).astype(BF16)

            each(256, 128, pointwise)

        each(seq, 256, forward)

        pump.add(3 * p, fill_ffn(t), done_ffn(t), columns(t))
        pump.tick()
        add_product(acc, dgu(t), w_gu.at[s, 0 : 2 * p], t == full_tiles)

        if i + 2 < len(order):
            for c in gu_loads(i + 2):
                c.start()

    wo = w_gu.at[0]
    load_wo = load(wo_hbm, wo, 0)
    load_wo.start()
    scatter_two = Scatter(acc, bufs, mp_send.at[4], mp_recv.at[4])
    pump.tick()
    scatter_two.start_near(0)
    pump.tick()
    scatter_two.start_far()
    scatter_two.start_near(1)
    pump.tick()

    def norm_two_back(rows, d_normed_two):
        hidden = h1[rows, :]
        inverse = norm_rows(hidden)
        unit = hidden * inverse
        e = d_normed_two * gain_f
        d_hidden = g_own[rows, :].astype(F32) + inverse * (
            e - unit * jnp.mean(e * unit, axis=-1, keepdims=True)
        )
        grad_in[rows, :] = d_hidden
        own[rows, :] = d_hidden.astype(BF16)

    gather_attn = Gather(own, da_all, mp_send.at[5], mp_recv.at[5])
    scatter_two.finish(norm_two_back, lambda i: gather_attn.far_copy(i).start())
    pump.tick()
    gather_attn.start_near()

    for i, t in enumerate(order):
        pump.tick()
        down_load(i, 6).wait()

        p = wide(t)
        add_product(acc, acts.at[t, :, 0:p], w_d.at[i % 2, 0:p], t == full_tiles)
        if i + 2 < len(order):
            down_load(i + 2, 6).start()
    pump.tick()
    gather_attn.finish()
    far_in2 = w_gu.at[1, pl.ds(2 * tok, tok)]
    scatter_out = Scatter(acc, (near_out, None, far_out, far_in2), mp_send.at[6], mp_recv.at[6])
    scatter_out.near_in = [w_gu.at[1, pl.ds(k * tok, tok)] for k in (0, 1)]
    pump.tick()
    scatter_out.start_near(0)
    pump.tick()
    load_wo.wait()

    def mix_back(rows):
        dmixed[rows, :] = dot_nt(da_all[rows, :], wo[...]).astype(BF16)

    each(seq, seq, mix_back)

    def fill_out(grad):
        def block(half, lanes):
            top = dot_tn(da_all[:, lanes], mixed[...])
            half[..., 0:512] = top.astype(BF16).reshape(2, 2, 4, 64, 512)

        halves(grad, block)

    def done_out(total):
        o_out[...] = total

    pump.add(512, fill_out, done_out)
    pump.tick()
    scatter_out.start_far()
    scatter_out.start_near(1)

    def keep(rows, total):
        h1[rows, :] += total

    pump.tick()
    scatter_out.fold(keep)

    raw_s, d_probs_s = acc.at[:, 0:512], acc.at[:, 512:1024]
    d_raw_s, mass_s = dgus.at[0], dgus.at[1]
    for i in range(1, 4):
        above = (slice(128 * (i - 1), 128 * i), slice(128 * i, seq))
        d_raw_s[above] = jnp.zeros((128, seq - 128 * i), BF16)
        mass_s[above] = jnp.zeros((128, seq - 128 * i), BF16)
    for h in range(heads):
        pump.tick()
        vcols = value_cols(h)
        for i in range(4):
            rows, reach = slice(128 * i, 128 * i + 128), 128 * i + 128
            raw_s[rows, 0:reach] = dot_nt(qk[rows, query_cols(h)], qk[0:reach, key_cols(h)])
            d_probs_s[rows, 0:reach] = dot_nt(
                dmixed[rows, vcols], v_ones[0:reach, 256 * h : 256 * h + 128]
            )
        for i in range(4):
            rows, reach = slice(128 * i, 128 * i + 128), 128 * i + 128
            cols = slice(max(0, 128 * i - 128), reach)

            def part(at, h=h, vcols=vcols, reach=reach, cols=cols):
                d_mix = dmixed[at, vcols].astype(F32)
                drop_lin = jnp.sum(d_mix * linear[at, vcols].astype(F32), axis=1, keepdims=True)
                drop_win = jnp.sum(d_mix * windowed[at, vcols].astype(F32), axis=1, keepdims=True)
                scale = stats[at, h : h + 1]
                total = stats[at, heads + h : heads + h + 1]
                score, d_probs = raw_s[at, 0:reach], d_probs_s[at, 0:reach]
                seen = mask[at, 0:reach]
                kernel = ((0.5 * score + 1.0) * score + 1.0) * scale
                mass_s[at, 0:reach] = kernel.astype(BF16) * seen
                d_kernel = (d_probs - drop_lin) * scale * (1.0 + score)
                d_raw_s[at, 0:reach] = d_kernel.astype(BF16) * seen
                probs = jnp.exp(raw_s[at, cols] + (band[at, 0 : cols.stop - cols.start].astype(F32) - total))
                d_scores = probs * (d_probs_s[at, cols] - drop_win)
                mass_s[at, cols] = (mass_s[at, cols].astype(F32) + probs).astype(BF16)
                d_raw_s[at, cols] = (d_raw_s[at, cols].astype(F32) + d_scores).astype(BF16)

            each(128, 64, part, 128 * i)
        dqk[:, query_cols(h)] = (
            FEAT ** (-0.5) * dot_nn(d_raw_s[...], qk[:, key_cols(h)])
        ).astype(BF16)
        dqk[:, key_cols(h)] = dot_tn(d_raw_s[...], qk[:, query_cols(h)]).astype(BF16)
        dv[:, vcols] = dot_tn(mass_s[...], dmixed[:, vcols]).astype(BF16)

    def fill_qkv(grad):
        load_normed.wait()

        def block(half, lanes):
            for src, at in ((dqk, slice(0, 128)), (dv, slice(128, 640))):
                top = dot_tn(n2[:, lanes], src[...])
                half[..., at] = top.astype(BF16).reshape(2, 2, 4, 64, at.stop - at.start)

        halves(grad, block)

    def done_qkv(total):
        o_query[...] = total[:, 0:64]
        o_key[...] = total[:, 64:128]
        o_value[...] = total[:, 128:640]
        part = weigh(total[:, 0:128], wqk[:, chunk])
        rows_v = wv[pl.ds(pl.multiple_of(dp * 64, 64), 64), :].astype(F32)
        part += jnp.sum(total[:, 128:640] * rows_v, axis=1, keepdims=True)
        gsum[1] = jnp.broadcast_to(part, gsum.shape[1:])

    pump.add(640, fill_qkv, done_qkv)
    pump.tick()

    def normed_back(rows):
        acc[rows, :] = dot_nt(dv[rows, :], wv[...])

    each(seq, seq, normed_back)
    add_product(acc, dqk, wqk, False)
    scatter_in = Scatter(acc, bufs, mp_send.at[7], mp_recv.at[7])
    pump.tick()
    scatter_in.start_near(0)

    def output(rows, total):
        block_out[rows, :] = (h1[rows, :] + total).astype(BF16)

    pump.tick()
    scatter_out.finish_far(output)
    pump.tick()
    scatter_in.start_far()
    scatter_in.start_near(1)


    def norm_one_back(rows, d_normed):
        values = x_own[rows, :].astype(F32)
        inverse = norm_rows(values)
        unit = values * inverse
        e = d_normed * gain_a
        grad_in[rows, :] += inverse * (
            e - unit * jnp.mean(e * unit, axis=-1, keepdims=True)
        )

    pump.tick()
    scatter_in.finish(norm_one_back)
    pump.tick()

    pick = (row + (dp % 2) * 64) == lane
    for i in (0, 1):
        line = jnp.sum(jnp.where(pick, gsum[1 - i], 0.0), axis=0, keepdims=True)
        gline[8 * i : 8 * i + 8, :] = jnp.broadcast_to(line, (8, 128))
    others = (mate, pair, device(x, yh, z, 1 - yl, 1 - core))
    shares = [
        remote(gline, glines.at[i], mp_send.at[8, i], mp_recv.at[8, i], target)
        for i, target in enumerate(others)
    ]
    for c in shares:
        c.start()
    for c in shares:
        c.wait()
    total = gline[...] + glines[0] + glines[1] + glines[2]
    first = (dp % 2) * 64 + mp * 16
    for i, gain in enumerate((gain_attn, gain_ffn)):
        line = total[8 * i : 8 * i + 8, :] / gain[:, chunk]
        gains_out[i : i + 1, :] = pltpu.roll(line, (128 - first) % 128, 1)[0:1, :]


def layer(lengths, x_own, g_own, gain_attn, gain_ffn, wq, wk, wv, wo, wg, wu, wd):
    tok, width = x_own.shape
    seq, ff = 4 * tok, wd.shape[0]
    tiles = -(-ff // FF_TILE)
    pad = -(-(ff % FF_TILE) // 128) * 128
    wide = 3 * FF_TILE
    vmem, hbm = pl.BlockSpec(memory_space=pltpu.VMEM), pl.BlockSpec(memory_space=pl.ANY)
    shape = jax.ShapeDtypeStruct
    sems = pltpu.SemaphoreType.DMA
    scratch = [
        pltpu.VMEM((seq, width), BF16),
        pltpu.VMEM((seq, width), BF16),
        pltpu.VMEM((seq, width), BF16),
        pltpu.VMEM((tok, width), BF16),
        pltpu.VMEM((tok, width), F32),
        pltpu.VMEM((2, 2 * FF_TILE, width), BF16),
        pltpu.VMEM((2, FF_TILE, width), BF16),
        pltpu.VMEM((128, width), BF16),
        pltpu.VMEM(wv.shape, BF16),
        pltpu.VMEM((2, 2, FF_TILE, 128), BF16),
        pltpu.VMEM((seq, 128), BF16),
        pltpu.VMEM((seq, 1024), BF16),
        pltpu.VMEM((seq, 512), BF16),
        pltpu.VMEM((seq, 512), BF16),
        pltpu.VMEM((seq, 512), BF16),
        pltpu.VMEM((seq, 128), F32),
        pltpu.VMEM((seq, seq), BF16),
        pltpu.VMEM((seq, 256), BF16),
        pltpu.VMEM((seq, width), F32),
        pltpu.VMEM((tiles, seq, FF_TILE), BF16),
        pltpu.VMEM((tiles - 1, seq, 2 * FF_TILE), BF16),
        pltpu.VMEM((seq, 2 * pad), BF16),
        pltpu.VMEM((256, 512), F32),
        pltpu.VMEM((-(-tiles // 2), seq, 2 * FF_TILE), BF16),
        pltpu.VMEM((seq, 128), BF16),
        pltpu.VMEM((2, 64, 128), F32),
        pltpu.VMEM((16, 128), F32),
        pltpu.VMEM((3, 16, 128), F32),
        pltpu.VMEM((tok, width), BF16),
        pltpu.VMEM((2, tok, width), BF16),
        pltpu.VMEM((tok, width), BF16),
        pltpu.VMEM((tok, width), BF16),
    ]
    scratch += [pltpu.VMEM((4, 2, 4, 64, wide), BF16) for _ in range(SETS)]
    scratch += [b for _ in range(SETS) for b in sum_buffers(wide)[:5]]
    scratch += [
        sems((SETS, 2, 13)),
        sems((SETS, 2, 13)),
        pltpu.SemaphoreType.REGULAR((SETS,)),
        sems((9, 2 * PARTS + 1)),
        sems((9, 2 * PARTS + 1)),
        sems((17,)),
    ]
    return pl.pallas_call(
        layer_kernel,
        out_shape=[
            shape((tok, width), BF16),
            shape((tok, width), F32),
            shape((2, 128), F32),
            shape((64, wq.shape[0]), F32),
            shape((64, wk.shape[0]), F32),
            shape((64, wv.shape[1]), F32),
            shape((64, wo.shape[0]), F32),
            shape((64, ff), F32),
            shape((64, ff), F32),
            shape((64, ff), F32),
            shape((seq, width), BF16),
        ],
        in_specs=[pl.BlockSpec(memory_space=pltpu.SMEM)] + [vmem] * 4 + [hbm] * 7,
        out_specs=[vmem] * 10 + [hbm],
        scratch_shapes=scratch,
        compiler_params=pltpu.CompilerParams(
            collective_id=0, has_side_effects=True, vmem_limit_bytes=65400 << 10
        ),
        name="layer",
    )(lengths, x_own, g_own, gain_attn, gain_ffn, wq, wk, wv, wo, wg, wu, wd)


def hand_out_kernel(n, *refs):
    sems = refs[2 * n + 3]
    copies = [pltpu.make_async_copy(refs[i], refs[n + 1 + i], sems.at[i]) for i in range(n)]
    for c in copies:
        c.start()
    gains, first, second = refs[n], refs[2 * n + 1], refs[2 * n + 2]
    first[...] = gains[0:1, 0:16]
    second[...] = gains[1:2, 0:16]
    for c in copies:
        c.wait()


def hand_out(arrays, gains):
    n = len(arrays)
    vmem, hbm = pl.BlockSpec(memory_space=pltpu.VMEM), pl.BlockSpec(memory_space=pl.ANY)
    shape = jax.ShapeDtypeStruct
    return pl.pallas_call(
        functools.partial(hand_out_kernel, n),
        out_shape=[shape(a.shape, a.dtype) for a in arrays] + [shape((1, 16), F32)] * 2,
        in_specs=[vmem] * (n + 1),
        out_specs=[hbm] * n + [vmem] * 2,
        scratch_shapes=[pltpu.SemaphoreType.DMA((n,))],
        name="hand_out",
    )(*arrays, gains)


def on_device(
    block_input,
    lengths,
    gain_attn,
    gain_ffn,
    w_query,
    w_key,
    w_value,
    w_out,
    w_gate,
    w_up,
    w_down,
    cotangent,
):
    width = block_input.shape[-1]
    out = layer(
        lengths,
        block_input.reshape(-1, width),
        cotangent.reshape(-1, width),
        gain_attn.reshape(1, -1),
        gain_ffn.reshape(1, -1),
        w_query.T,
        w_key.T,
        w_value,
        w_out,
        w_gate.T,
        w_up.T,
        w_down,
    )
    (
        block_output,
        grad_input,
        grad_query,
        grad_key,
        grad_value,
        grad_out,
        grad_gate,
        grad_up,
        grad_down,
        grad_gain_attn,
        grad_gain_ffn,
    ) = hand_out([out[0], out[1], *out[3:10]], out[2])
    return (
        block_output.reshape(block_input.shape),
        grad_input.reshape(block_input.shape),
        grad_gain_attn.reshape(-1),
        grad_gain_ffn.reshape(-1),
        grad_query,
        grad_key,
        grad_value,
        grad_out.T,
        grad_gate,
        grad_up,
        grad_down.T,
    )


def solution(mesh):
    return jax.shard_map(
        on_device,
        mesh=mesh,
        in_specs=(
            P("dp", "mp", None),
            P("dp", None),
            P(),
            P(),
            P(None, "mp"),
            P(None, "mp"),
            P(None, "mp"),
            P("mp", None),
            P(None, "mp"),
            P(None, "mp"),
            P("mp", None),
            P("dp", "mp", None),
        ),
        out_specs=(
            P("dp", "mp", None),
            P("dp", "mp", None),
            P(("dp", "mp")),
            P(("dp", "mp")),
            P("dp", "mp"),
            P("dp", "mp"),
            P("dp", "mp"),
            P("mp", "dp"),
            P("dp", "mp"),
            P("dp", "mp"),
            P("mp", "dp"),
        ),
        check_vma=False,
    )
```

```python
import functools

import jax
import jax.numpy as jnp
from jax import lax
from jax.experimental import pallas as pl
from jax.experimental.pallas import tpu as pltpu
from jax.sharding import PartitionSpec as P

MESH = pl.DeviceIdType.MESH
F32 = jnp.float32
BF16 = jnp.bfloat16

FEAT = 16
VDIM = 128
WINDOW = 64
SETS = 4
FF_TILE = 256
PARTS = 4

norm_eps = 1e-05
masked_score = -1e30


def place():
    dp, mp = lax.axis_index("dp"), lax.axis_index("mp")
    return dp // 8, (dp // 4) % 2, dp % 4, mp // 2, mp % 2


def device(x, yh, z, yl, core):
    return (x * 8 + yh * 4 + z, yl * 2 + core)


def greet(devices):
    barrier = pltpu.get_barrier_semaphore()
    for target in devices:
        pl.semaphore_signal(barrier, inc=1, device_id=target, device_id_type=MESH)
    pl.semaphore_wait(barrier, len(devices))


def remote(src, dst, send_sem, recv_sem, target):
    return pltpu.make_async_remote_copy(
        src_ref=src,
        dst_ref=dst,
        send_sem=send_sem,
        recv_sem=recv_sem,
        device_id=target,
        device_id_type=MESH,
    )


def dot_nn(a, b):
    return lax.dot_general(a, b, (((1,), (0,)), ((), ())), preferred_element_type=F32)


def dot_nt(a, b):
    return lax.dot_general(a, b, (((1,), (1,)), ((), ())), preferred_element_type=F32)


def dot_tn(a, b):
    return lax.dot_general(a, b, (((0,), (0,)), ((), ())), preferred_element_type=F32)


def each(count, step, body, base=0):
    def run(i, _):
        body(pl.ds(pl.multiple_of(base + i * step, step), step))
        return 0

    lax.fori_loop(0, count // step, run, 0)


class Gather:
    def __init__(self, own, full, send, recv):
        self.own, self.full, self.send, self.recv = own, full, send, recv
        x, yh, z, yl, core = place()
        self.mate, self.pair = device(x, yh, z, yl, 1 - core), device(x, yh, z, 1 - yl, core)
        self.tok = own.shape[0]
        self.piece = self.tok // PARTS
        self.mine, self.far = yl * 2 + core, (1 - yl) * 2 + core

    def rows(self, part, i):
        start = part * self.tok + i * self.piece
        return pl.ds(pl.multiple_of(start, self.piece), self.piece)

    def far_copy(self, i):
        return remote(
            self.own.at[pl.ds(i * self.piece, self.piece)],
            self.full.at[self.rows(self.mine, i)],
            self.send.at[i],
            self.recv.at[i],
            self.pair,
        )

    def near_copy(self):
        return remote(
            self.own,
            self.full.at[pl.ds(pl.multiple_of(self.mine * self.tok, self.tok), self.tok)],
            self.send.at[PARTS],
            self.recv.at[PARTS],
            self.mate,
        )

    def pass_copy(self, i):
        rows = self.rows(self.far, i)
        return remote(
            self.full.at[rows],
            self.full.at[rows],
            self.send.at[PARTS + 1 + i],
            self.recv.at[PARTS + 1 + i],
            self.mate,
        )

    def start(self):
        for i in range(PARTS):
            self.far_copy(i).start()
        self.start_near()

    def start_near(self):
        self.near_copy().start()
        at = pl.ds(pl.multiple_of(self.mine * self.tok, self.tok), self.tok)
        self.full[at, :] = self.own[...]

    def finish_near(self):
        self.near_copy().wait()

    def finish_far(self):
        for i in range(PARTS):
            self.far_copy(i).wait_recv()
            self.pass_copy(i).start()
        for i in range(PARTS):
            self.far_copy(i).wait_send()
            self.pass_copy(i).wait()

    def finish(self):
        self.finish_near()
        self.finish_far()


class Scatter:
    def __init__(self, part, bufs, send, recv):
        self.part = part
        self.near_out, near_in, self.far_out, self.far_in = bufs
        if near_in is not None:
            self.near_in = [near_in.at[k] for k in (0, 1)]
        self.send, self.recv = send, recv
        x, yh, z, yl, core = place()
        self.yl, self.core = yl, core
        self.mate, self.pair = device(x, yh, z, yl, 1 - core), device(x, yh, z, 1 - yl, core)
        self.tok = self.far_in.shape[0]
        self.piece = self.tok // PARTS

    def near_copy(self, k):
        return remote(
            self.near_out, self.near_in[k], self.send.at[k], self.recv.at[k], self.mate
        )

    def far_copy(self, i):
        rows = pl.ds(i * self.piece, self.piece)
        return remote(
            self.far_out.at[rows],
            self.far_in.at[rows],
            self.send.at[2 + i],
            self.recv.at[2 + i],
            self.pair,
        )

    def start_near(self, k):
        side = self.yl if k else 1 - self.yl
        start = pl.multiple_of((side * 2 + 1 - self.core) * self.tok, self.tok)

        if k:
            self.near_copy(0).wait_send()

        def cast(rows):
            self.near_out[rows, :] = self.part[
                pl.ds(pl.multiple_of(start + rows.start, 16), 16), :
            ].astype(BF16)

        each(self.tok, 16, cast)
        self.near_copy(k).start()

    def start_far(self):
        self.near_copy(0).wait_recv()
        far = pl.multiple_of(((1 - self.yl) * 2 + self.core) * self.tok, self.tok)
        for i in range(PARTS):

            def join(rows, i=i):
                at = pl.ds(pl.multiple_of(i * self.piece + rows.start, 16), 16)
                src = pl.ds(pl.multiple_of(far + i * self.piece + rows.start, 16), 16)
                self.far_out[at, :] = (
                    self.part[src, :] + self.near_in[0][at, :].astype(F32)
                ).astype(BF16)

            each(self.piece, 16, join)
            self.far_copy(i).start()

    def fold(self, use):
        self.near_copy(1).wait_recv()
        own = pl.multiple_of((self.yl * 2 + self.core) * self.tok, self.tok)

        def join(rows):
            src = pl.ds(pl.multiple_of(own + rows.start, 16), 16)
            use(rows, self.part[src, :] + self.near_in[1][rows, :].astype(F32))

        each(self.tok, 16, join)
        self.near_copy(1).wait_send()

    def finish_far(self, use):
        for i in range(PARTS):
            self.far_copy(i).wait()
        each(self.tok, 16, lambda rows: use(rows, self.far_in[rows, :].astype(F32)))

    def finish(self, use, after=None):
        self.near_copy(1).wait_recv()
        own = pl.multiple_of((self.yl * 2 + self.core) * self.tok, self.tok)
        for i in range(PARTS):
            self.far_copy(i).wait_recv()

            def join(rows, i=i):
                at = pl.ds(pl.multiple_of(i * self.piece + rows.start, 16), 16)
                src = pl.ds(pl.multiple_of(own + i * self.piece + rows.start, 16), 16)
                use(
                    at,
                    self.part[src, :]
                    + self.near_in[1][at, :].astype(F32)
                    + self.far_in[at, :].astype(F32),
                )

            each(self.piece, 16, join)
            if after is not None:
                after(i)
        self.near_copy(1).wait_send()
        for i in range(PARTS):
            self.far_copy(i).wait_send()


def add_into(dst, terms, rows, step):
    def body(i, _):
        at = pl.ds(pl.multiple_of(i * step, step), step)
        total = dst[at, :].astype(F32)
        for term in terms:
            total = total + term[at, :].astype(F32)
        dst[at, :] = total.astype(dst.dtype)
        return 0

    lax.fori_loop(0, rows // step, body, 0)


class RowSum:
    def __init__(self, grad, bufs, send, recv):
        self.grad = grad
        self.t1, self.m1, self.t2, self.m2, self.last = bufs
        self.send, self.recv = send, recv
        self.x, self.yh, self.z, self.yl, self.core = place()

    def near(self, path, stage, step):
        if (path == 0) == (stage == 0):
            return device((self.x + step + 4) % 4, self.yh, self.z, self.yl, self.core)
        return device(self.x, self.yh, (self.z + step + 4) % 4, self.yl, self.core)

    def at(self, path, stage):
        return self.x if (path == 0) == (stage == 0) else self.z

    def block(self, path, b, k):
        return self.grad.at[b, 0, k] if path == 0 else self.grad.at[k, 1, b]

    def copy(self, src, dst, path, slot, target):
        return remote(src, dst, self.send.at[path, slot], self.recv.at[path, slot], target)

    def transit_one(self, path, side):
        b = (self.at(path, 0) + 2) % 4
        return self.copy(
            self.block(path, b, pl.ds(2 * side, 2)),
            self.t1.at[path, side],
            path,
            side,
            self.near(path, 0, 1 - 2 * side),
        )

    def main_one(self, path, side, half):
        step = 1 - 2 * side
        b = (self.at(path, 0) + step + 4) % 4
        src = (
            self.t1.at[path, side]
            if half == side
            else self.block(path, b, pl.ds(2 * half, 2))
        )
        return self.copy(
            src,
            self.m1.at[path, side, pl.ds(2 * half, 2)],
            path,
            2 + 2 * side + half,
            self.near(path, 0, step),
        )

    def transit_two(self, path, side):
        k = (self.at(path, 1) + 2) % 4
        return self.copy(
            self.m1.at[path, 0, k, pl.ds(32 * side, 32)],
            self.t2.at[path, side],
            path,
            6 + side,
            self.near(path, 1, 1 - 2 * side),
        )

    def main_two(self, path, side, half):
        step = 1 - 2 * side
        k = (self.at(path, 1) + step + 4) % 4
        rows = pl.ds(32 * half, 32)
        src = self.t2.at[path, side] if half == side else self.m1.at[path, 0, k, rows]
        return self.copy(
            src,
            self.m2.at[path, side, rows],
            path,
            8 + 2 * side + half,
            self.near(path, 1, step),
        )

    def last_copy(self):
        target = device(self.x, 1 - self.yh, self.z, self.yl, self.core)
        return self.copy(self.m2.at[1 - self.yh, 0], self.last, 0, 12, target)

    def start_one(self):
        for path in (0, 1):
            for side in (0, 1):
                self.transit_one(path, side).start()
        for path in (0, 1):
            for side in (0, 1):
                self.main_one(path, side, 1 - side).start()

    def pass_one(self):
        for path in (0, 1):
            for side in (0, 1):
                self.transit_one(path, side).wait_recv()
                b = (self.at(path, 0) + 1 - 2 * side + 4) % 4
                for k in (0, 1):
                    add_into(
                        self.t1.at[path, side, k],
                        (self.block(path, b, 2 * side + k),),
                        64,
                        64,
                    )
                self.main_one(path, side, side).start()

    def join_one(self):
        for path in (0, 1):
            for side in (0, 1):
                for half in (0, 1):
                    self.main_one(path, side, half).wait_recv()
            b = self.at(path, 0)

            def body(k, _):
                add_into(
                    self.m1.at[path, 0, k],
                    (self.m1.at[path, 1, k], self.block(path, b, k)),
                    64,
                    64,
                )
                return 0

            lax.fori_loop(0, 4, body, 0)
            for side in (0, 1):
                self.transit_two(path, side).start()
            for side in (0, 1):
                self.main_two(path, side, 1 - side).start()

    def pass_two(self):
        for path in (0, 1):
            for side in (0, 1):
                self.transit_two(path, side).wait_recv()
                k = (self.at(path, 1) + 1 - 2 * side + 4) % 4
                add_into(
                    self.t2.at[path, side],
                    (self.m1.at[path, 0, k, pl.ds(32 * side, 32)],),
                    32,
                    32,
                )
                self.main_two(path, side, side).start()

    def join_two(self):
        for path in (0, 1):
            for side in (0, 1):
                for half in (0, 1):
                    self.main_two(path, side, half).wait_recv()
            k = self.at(path, 1)
            add_into(self.m2.at[path, 0], (self.m2.at[path, 1], self.m1.at[path, 0, k]), 64, 64)
        self.last_copy().start()

    def finish(self, use):
        self.last_copy().wait_recv()
        use(self.m2[self.yh, 0].astype(F32) + self.last[...].astype(F32))
        for path in (0, 1):
            for side in (0, 1):
                self.transit_one(path, side).wait_send()
                self.transit_two(path, side).wait_send()
                for half in (0, 1):
                    self.main_one(path, side, half).wait_send()
                    self.main_two(path, side, half).wait_send()
        self.last_copy().wait_send()


def sum_buffers(width):
    return [
        pltpu.VMEM((2, 2, 2, 64, width), BF16),
        pltpu.VMEM((2, 2, 4, 64, width), BF16),
        pltpu.VMEM((2, 2, 32, width), BF16),
        pltpu.VMEM((2, 2, 64, width), BF16),
        pltpu.VMEM((64, width), BF16),
        pltpu.SemaphoreType.DMA((2, 13)),
        pltpu.SemaphoreType.DMA((2, 13)),
    ]


def sum_neighbours():
    x, yh, z, yl, core = place()
    return (
        device((x + 1) % 4, yh, z, yl, core),
        device((x + 3) % 4, yh, z, yl, core),
        device(x, yh, (z + 1) % 4, yl, core),
        device(x, yh, (z + 3) % 4, yl, core),
        device(x, 1 - yh, z, yl, core),
    )


class Pump:
    def __init__(self, grads, sets, sends, recvs, credit):
        self.grads, self.sets, self.sends, self.recvs, self.credit = (
            grads,
            sets,
            sends,
            recvs,
            credit,
        )
        self.units, self.turn = [], 0

    def add(self, width, fill, done, loads=()):
        slot = len(self.units) % SETS
        lanes = pl.ds(0, width)

        def view(ref):
            return ref.at[tuple([slice(None)] * (len(ref.shape) - 1) + [lanes])]

        rows = RowSum(
            view(self.grads[slot]),
            [view(b) for b in self.sets[slot]],
            self.sends.at[slot],
            self.recvs.at[slot],
        )
        self.units.append((rows, fill, done, loads))

    def stage(self, index, number):
        rows, fill, done, loads = self.units[index]
        slot = index % SETS
        if number == 0:
            fill(self.grads[slot])
        elif number == 1:
            if index >= SETS:
                pl.semaphore_wait(self.credit.at[slot], 5)
            rows.start_one()
        elif number < 6:
            if number == 5:
                for c in loads:
                    c.start()
            (rows.pass_one, rows.join_one, rows.pass_two, rows.join_two)[number - 2]()
        else:
            rows.finish(done)
            if index + SETS < UNITS:
                for target in sum_neighbours():
                    pl.semaphore_signal(
                        self.credit.at[slot], inc=1, device_id=target, device_id_type=MESH
                    )

    def tick(self):
        for index, number in PLAN[self.turn]:
            self.stage(index, number)
        self.turn += 1


UNITS = 8
PLAN = (
    (),
    ((0, 0), (0, 1),),
    (),
    ((1, 0), (1, 1),),
    ((0, 2),),
    (),
    (),
    ((2, 0), (1, 2), (2, 1),),
    (),
    ((0, 3),),
    (),
    (),
    ((1, 3),),
    (),
    ((2, 2), (3, 0), (0, 4), (3, 1), (1, 4), (2, 3), (0, 5), (3, 2),),
    ((0, 6), (4, 0), (1, 5), (2, 4), (4, 1),),
    (),
    (),
    (),
    ((3, 3),),
    (),
    ((1, 6),),
    ((2, 5), (5, 0), (5, 1), (4, 2), (2, 6), (3, 4),),
    (),
    (),
    (),
    ((5, 2),),
    (),
    (),
    (),
    ((6, 0), (3, 5), (4, 3), (6, 1),),
    (),
    ((5, 3), (3, 6),),
    ((4, 4), (7, 0), (7, 1),),
    ((6, 2),),
    ((5, 4), (4, 5), (7, 2), (4, 6), (6, 3), (5, 5), (7, 3),),
    ((6, 4), (5, 6), (7, 4), (6, 5), (7, 5), (6, 6), (7, 6),),
)


def norm_rows(values):
    return lax.rsqrt(jnp.mean(values * values, axis=-1, keepdims=True) + norm_eps)


def doc_of(positions, ends):
    return sum((positions >= e).astype(jnp.int32) for e in ends)


def add_product(total, left, right, first):
    for j in range(0, total.shape[1], 512):
        cols = slice(j, j + 512)
        part = dot_nn(left[...], right[:, cols])
        if first:
            total[:, cols] = part
        else:
            total[:, cols] += part


def layer_kernel(
    lengths,
    x_own,
    g_own,
    gain_attn,
    gain_ffn,
    wq_hbm,
    wk_hbm,
    wv_hbm,
    wo_hbm,
    wg_hbm,
    wu_hbm,
    wd_hbm,
    block_out,
    grad_in,
    gains_out,
    o_query,
    o_key,
    o_value,
    o_out,
    o_gate,
    o_up,
    o_down,
    normed_hbm,
    n2,
    g_all,
    da_all,
    own,
    h1,
    w_gu,
    w_d,
    wqk,
    wv,
    cols_gu,
    qk,
    v_ones,
    mixed,
    linear,
    windowed,
    stats,
    mask,
    band,
    acc,
    acts,
    dgus,
    dgu_last,
    gu,
    d_acts,
    dqk,
    gsum,
    gline,
    glines,
    near_out,
    near_in,
    far_out,
    far_in,
    *rest,
):
    grads = rest[:SETS]
    sets = [rest[SETS + 5 * i : SETS + 5 * i + 5] for i in range(SETS)]
    sends, recvs, credit, mp_send, mp_recv, wsem = rest[6 * SETS :]
    x, yh, z, yl, core = place()
    dp, mp = lax.axis_index("dp"), lax.axis_index("mp")
    mate, pair = device(x, yh, z, yl, 1 - core), device(x, yh, z, 1 - yl, core)
    seq, width = n2.shape
    ff = wd_hbm.shape[0]
    full_tiles = ff // FF_TILE
    last = ff - full_tiles * FF_TILE
    pad = -(-last // 128) * 128
    order = [full_tiles] + list(range(full_tiles))
    heads = wv.shape[1] // VDIM
    ends = [lengths[0, 0], lengths[0, 0] + lengths[0, 1]]
    ends.append(ends[1] + lengths[0, 2])
    near_base = pl.multiple_of(yl * 256, 256)
    far_base = pl.multiple_of((1 - yl) * 256, 256)

    def valid(t):
        return last if t == full_tiles else FF_TILE

    def wide(t):
        return pad if t == full_tiles else FF_TILE

    dmixed, dv = d_acts.at[0], d_acts.at[1]

    def dgu(t):
        return dgu_last if t == full_tiles else dgus.at[t]

    def load(src, dst, i):
        return pltpu.make_async_copy(src, dst, wsem.at[i])

    def gu_loads(i):
        t, s = order[i], i % 2
        rows = pl.ds(t * FF_TILE, valid(t))
        return [
            load(wg_hbm.at[rows], w_gu.at[s, pl.ds(0, valid(t))], 3 * s),
            load(wu_hbm.at[rows], w_gu.at[s, pl.ds(wide(t), valid(t))], 3 * s + 1),
        ]

    def down_load(i, sem):
        t, s = order[i], i % 2
        return load(
            wd_hbm.at[pl.ds(t * FF_TILE, valid(t))], w_d.at[s, pl.ds(0, valid(t))], sem + s
        )

    small = [
        load(wq_hbm, wqk.at[pl.ds(0, 64)], 8),
        load(wk_hbm, wqk.at[pl.ds(64, 64)], 9),
        load(wv_hbm, wv, 10),
        load(wo_hbm, w_gu.at[1], 11),
    ]
    chunk = pl.ds(pl.multiple_of((dp // 2) * 128, 128), 128)

    def columns(t):
        rows, some, s = pl.ds(t * FF_TILE, valid(t)), pl.ds(0, valid(t)), order.index(t) % 2
        return [
            load(w.at[rows, chunk], cols_gu.at[s, i, some], 12 + 2 * s + i)
            for i, w in enumerate((wg_hbm, wu_hbm))
        ]

    for c in small:
        c.start()
    gain_a, gain_f = gain_attn[...], gain_ffn[...]
    tok = own.shape[0]

    def norm_one(rows):
        values = x_own[rows, :].astype(F32)
        own[rows, :] = (values * norm_rows(values) * gain_a).astype(BF16)

    each(tok, 16, norm_one)
    greet(sum_neighbours() + (mate, pair, device(x, yh, z, 1 - yl, 1 - core)))
    gather_one = Gather(own, da_all, mp_send.at[0], mp_recv.at[0])
    gather_one.start()
    gather_g = Gather(g_own, g_all, mp_send.at[1], mp_recv.at[1])
    gather_g.start()
    for at in (pl.ds(last, pad - last), pl.ds(pad + last, pad - last)):
        w_gu[0, at, :] = jnp.zeros((pad - last, width), BF16)
    w_d[0, pl.ds(last, pad - last), :] = jnp.zeros((pad - last, width), BF16)
    for c in gu_loads(0):
        c.start()
    for i in (0, 1):
        down_load(i, 6).start()
    for c in small:
        c.wait()

    def masks(rows):
        t = rows.start + lax.broadcasted_iota(jnp.int32, (32, 1), 0)
        col = lax.broadcasted_iota(jnp.int32, (1, seq), 1)
        seen = (t >= col) & (doc_of(t, ends) == doc_of(col, ends))
        mask[rows, :] = jnp.where(seen, 1.0, 0.0).astype(BF16)
        col = band_start(rows.start // 128) + lax.broadcasted_iota(jnp.int32, (1, 256), 1)
        seen = (t >= col) & (t - col < WINDOW) & (doc_of(t, ends) == doc_of(col, ends))
        band[rows, :] = jnp.where(seen, 0.0, masked_score).astype(BF16)

    def band_start(block):
        return pl.multiple_of(jnp.maximum(block - 1, 0) * 128, 128)

    each(seq, 32, masks)
    for h in range(heads):
        v_ones[:, 256 * h + 128 : 256 * h + 256] = jnp.ones((seq, 128), BF16)
    shrink = jnp.where(
        lax.broadcasted_iota(jnp.int32, (1, 128), 1) < 64, FEAT ** (-0.5), 1.0
    )

    def project(rows):
        qk[rows, :] = (dot_nt(da_all[rows, :], wqk[...]) * shrink).astype(BF16)
        value = dot_nn(da_all[rows, :], wv[...]).astype(BF16)
        for h in range(heads):
            v_ones[rows, 256 * h : 256 * h + 128] = value[:, 128 * h : 128 * h + 128]

    gather_one.finish_near()
    each(256, 256, project, near_base)
    gather_one.finish_far()
    each(256, 256, project, far_base)
    keep_normed = load(da_all, normed_hbm, 16)
    keep_normed.start()

    def query_cols(h):
        return slice(h * FEAT, (h + 1) * FEAT)

    def key_cols(h):
        return slice(64 + h * FEAT, 64 + (h + 1) * FEAT)

    def value_cols(h):
        return slice(h * VDIM, (h + 1) * VDIM)

    def attend_forward(base, hs):
        half = [pl.ds(pl.multiple_of(base + 128 * i, 128), 128) for i in (0, 1)]
        first = [band_start(base // 128 + i) for i in (0, 1)]

        def raw_at(h, rows):
            return gu.at[rows]

        for h in hs:
            raw_at(h, slice(0, 256))[...] = dot_nt(
                qk[pl.ds(base, 256), query_cols(h)], qk[:, key_cols(h)]
            )
        for h in hs:

            def taylor(sub, h=h):
                at = pl.ds(pl.multiple_of(base + sub.start, 64), 64)
                score = gu[sub, :]
                dgus[h, sub, :] = ((0.5 * score + 1.0) * score + 1.0).astype(BF16) * mask[at, :]

            each(256, 64, taylor)
        for h in hs:
            both = slice(256 * h, 256 * h + 256)
            one = dot_nn(dgus[h, 0:256, :], v_ones[:, both])
            for i in (0, 1):
                sub = slice(128 * i, 128 * i + 128)
                scores = raw_at(h, sub)[:, pl.ds(first[i], 256)] + band[half[i], :].astype(F32)
                top = jnp.max(scores, axis=1, keepdims=True)
                weights = jnp.exp(scores - top).astype(BF16)
                two = dot_nn(weights, v_ones[pl.ds(first[i], 256), both])
                inv_den = 1.0 / one[sub, 128:256]
                lin = one[sub, 0:128] * inv_den
                win = two[:, 0:128] / two[:, 128:256]
                linear[half[i], value_cols(h)] = lin.astype(BF16)
                windowed[half[i], value_cols(h)] = win.astype(BF16)
                mixed[half[i], value_cols(h)] = (lin + win).astype(BF16)
                stats[half[i], h : h + 1] = inv_den[:, 0:1]
                stats[half[i], heads + h : heads + h + 1] = top + jnp.log(two[:, 128:129])

    def project_out(rows):
        acc[rows, :] = dot_nn(mixed[rows, :], w_gu[1])

    bufs = (near_out, near_in, far_out, far_in)
    scatter_one = Scatter(acc, bufs, mp_send.at[2], mp_recv.at[2])
    for h in range(heads):
        attend_forward(far_base, (h,))
    each(256, 256, project_out, far_base)
    scatter_one.start_near(0)
    for h in range(heads):
        attend_forward(near_base, (h,))
        if h == 1:
            scatter_one.start_far()
    each(256, 256, project_out, near_base)
    scatter_one.start_near(1)
    for c in gu_loads(1):
        c.start()
    gather_g.finish()
    keep_normed.wait()

    gather_two = Gather(own, n2, mp_send.at[3], mp_recv.at[3])

    def norm_two(rows, total):
        hidden = x_own[rows, :].astype(F32) + total
        h1[rows, :] = hidden
        own[rows, :] = (hidden * norm_rows(hidden) * gain_f).astype(BF16)

    scatter_one.finish(norm_two, lambda i: gather_two.far_copy(i).start())
    gather_two.start_near()

    def at_act(t):
        return slice(FF_TILE * (t % 2), FF_TILE * (t % 2) + wide(t))

    for i, t in enumerate(order):
        down_load(i, 6).wait()

        def back_down(rows, i=i, t=t, p=wide(t)):
            d_acts[t // 2, rows, at_act(t)] = dot_nt(g_all[rows, :], w_d[i % 2, 0:p]).astype(BF16)

        each(seq, seq, back_down)
        if i + 2 < len(order):
            down_load(i + 2, 6).start()
    for i in (0, 1):
        down_load(i, 6).start()
    gather_two.finish()

    load_normed = load(normed_hbm, n2, 1)
    pump = Pump(grads, sets, sends, recvs, credit)
    lane = lax.broadcasted_iota(jnp.int32, (64, 128), 1)
    row = lax.broadcasted_iota(jnp.int32, (64, 128), 0)
    own_lane = lane == row + (dp % 2) * 64

    def weigh(total, block):
        full = dot_nn(total.astype(BF16), block)
        return jnp.sum(jnp.where(own_lane, full, 0.0), axis=1, keepdims=True)

    def halves(grad, block):
        def run(i, _):
            block(grad.at[pl.ds(2 * i, 2)], pl.ds(pl.multiple_of(i * 1024, 1024), 1024))
            return 0

        lax.fori_loop(0, 2, run, 0)

    def fill_ffn(t):
        p = wide(t)

        def fill(grad):
            def top(half, lanes):
                part = dot_tn(n2[:, lanes], dgu(t)[...])
                half[..., 0 : 2 * p] = part.astype(BF16).reshape(2, 2, 4, 64, 2 * p)

            def bottom(half, lanes):
                part = dot_tn(g_all[:, lanes], acts[t, :, 0:p])
                half[..., 2 * p : 3 * p] = part.astype(BF16).reshape(2, 2, 4, 64, p)

            halves(grad, top)
            halves(grad, bottom)
            if t == full_tiles - 1:
                load_normed.start()

        return fill

    def done_ffn(t):
        def done(total):
            n, p = valid(t), wide(t)
            cols = slice(t * FF_TILE, t * FF_TILE + n)
            value_gate, value_up = total[:, 0:n], total[:, p : p + n]
            o_gate[:, cols] = value_gate
            o_up[:, cols] = value_up
            o_down[:, cols] = total[:, 2 * p : 2 * p + n]
            for c in columns(t):
                c.wait()
            s = order.index(t) % 2
            column = weigh(value_gate, cols_gu[s, 0, 0:n, :])
            column += weigh(value_up, cols_gu[s, 1, 0:n, :])
            if t == full_tiles:
                gsum[0] = jnp.broadcast_to(column, gsum.shape[1:])
            else:
                gsum[0] += jnp.broadcast_to(column, gsum.shape[1:])

        return done

    for i, t in enumerate(order):
        s, p = i % 2, wide(t)
        pump.tick()
        for c in gu_loads(i):
            c.wait()

        def forward(rows, t=t, s=s, p=p):
            gu[:, 0 : 2 * p] = dot_nt(n2[rows, :], w_gu[s, 0 : 2 * p])

            def pointwise(sub):
                at = pl.ds(pl.multiple_of(rows.start + sub.start, 128), 128)
                gate, up = gu[sub, 0:p], gu[sub, p : 2 * p]
                d_act = d_acts[t // 2, at, at_act(t)].astype(F32)
                sig = jax.nn.sigmoid(gate)
                silu = gate * sig
                acts[t, at, 0:p] = (silu * up).astype(BF16)
                dgu(t)[at, 0:p] = (d_act * up * (sig * (1.0 + gate * (1.0 - sig)))).astype(BF16)
                dgu(t)[at, p : 2 * p] = (d_act * silu).astype(BF16)

            each(256, 128, pointwise)

        each(seq, 256, forward)

        pump.add(3 * p, fill_ffn(t), done_ffn(t), columns(t))
        pump.tick()
        if i + 1 < len(order):
            add_product(acc, dgu(t), w_gu.at[s, 0 : 2 * p], t == full_tiles)
        else:
            far_rows, near_rows = pl.ds(far_base, 256), pl.ds(near_base, 256)
            last_product = (dgu(t), w_gu.at[s, 0 : 2 * p])
            add_product(acc.at[far_rows], last_product[0].at[far_rows], last_product[1], False)

        if i + 2 < len(order):
            for c in gu_loads(i + 2):
                c.start()

    wo = w_gu.at[0]
    load_wo = load(wo_hbm, wo, 0)
    load_wo.start()
    scatter_two = Scatter(acc, bufs, mp_send.at[4], mp_recv.at[4])
    pump.tick()
    scatter_two.start_near(0)
    add_product(acc.at[near_rows], last_product[0].at[near_rows], last_product[1], False)
    pump.tick()
    scatter_two.start_far()
    scatter_two.start_near(1)
    pump.tick()

    def norm_two_back(rows, d_normed_two):
        hidden = h1[rows, :]
        inverse = norm_rows(hidden)
        unit = hidden * inverse
        e = d_normed_two * gain_f
        d_hidden = g_own[rows, :].astype(F32) + inverse * (
            e - unit * jnp.mean(e * unit, axis=-1, keepdims=True)
        )
        grad_in[rows, :] = d_hidden
        own[rows, :] = d_hidden.astype(BF16)

    gather_attn = Gather(own, da_all, mp_send.at[5], mp_recv.at[5])
    scatter_two.finish(norm_two_back, lambda i: gather_attn.far_copy(i).start())
    pump.tick()
    gather_attn.start_near()

    for i, t in enumerate(order):
        pump.tick()
        down_load(i, 6).wait()

        p = wide(t)
        add_product(acc, acts.at[t, :, 0:p], w_d.at[i % 2, 0:p], t == full_tiles)
        if i + 2 < len(order):
            down_load(i + 2, 6).start()
    pump.tick()
    gather_attn.finish()
    far_in2 = w_gu.at[1, pl.ds(2 * tok, tok)]
    scatter_out = Scatter(acc, (near_out, None, far_out, far_in2), mp_send.at[6], mp_recv.at[6])
    scatter_out.near_in = [w_gu.at[1, pl.ds(k * tok, tok)] for k in (0, 1)]
    pump.tick()
    scatter_out.start_near(0)
    pump.tick()
    load_wo.wait()

    def mix_back(rows):
        dmixed[rows, :] = dot_nt(da_all[rows, :], wo[...]).astype(BF16)

    each(seq, seq, mix_back)

    def fill_out(grad):
        def block(half, lanes):
            top = dot_tn(da_all[:, lanes], mixed[...])
            half[..., 0:512] = top.astype(BF16).reshape(2, 2, 4, 64, 512)

        halves(grad, block)

    def done_out(total):
        o_out[...] = total

    pump.add(512, fill_out, done_out)
    pump.tick()
    scatter_out.start_far()
    scatter_out.start_near(1)

    def keep(rows, total):
        h1[rows, :] += total

    pump.tick()
    scatter_out.fold(keep)

    raw_s, d_probs_s = acc.at[:, 0:512], acc.at[:, 512:1024]
    d_raw_s, mass_s = dgus.at[0], dgus.at[1]
    for i in range(1, 4):
        above = (slice(128 * (i - 1), 128 * i), slice(128 * i, seq))
        d_raw_s[above] = jnp.zeros((128, seq - 128 * i), BF16)
        mass_s[above] = jnp.zeros((128, seq - 128 * i), BF16)
    for h in range(heads):
        pump.tick()
        vcols = value_cols(h)
        for i in range(4):
            rows, reach = slice(128 * i, 128 * i + 128), 128 * i + 128
            raw_s[rows, 0:reach] = dot_nt(qk[rows, query_cols(h)], qk[0:reach, key_cols(h)])
            d_probs_s[rows, 0:reach] = dot_nt(
                dmixed[rows, vcols], v_ones[0:reach, 256 * h : 256 * h + 128]
            )
        for i in range(4):
            rows, reach = slice(128 * i, 128 * i + 128), 128 * i + 128
            cols = slice(max(0, 128 * i - 128), reach)

            def part(at, h=h, vcols=vcols, reach=reach, cols=cols):
                d_mix = dmixed[at, vcols].astype(F32)
                drop_lin = jnp.sum(d_mix * linear[at, vcols].astype(F32), axis=1, keepdims=True)
                drop_win = jnp.sum(d_mix * windowed[at, vcols].astype(F32), axis=1, keepdims=True)
                scale = stats[at, h : h + 1]
                total = stats[at, heads + h : heads + h + 1]
                score, d_probs = raw_s[at, 0:reach], d_probs_s[at, 0:reach]
                seen = mask[at, 0:reach]
                kernel = ((0.5 * score + 1.0) * score + 1.0) * scale
                mass_s[at, 0:reach] = kernel.astype(BF16) * seen
                d_kernel = (d_probs - drop_lin) * scale * (1.0 + score)
                d_raw_s[at, 0:reach] = d_kernel.astype(BF16) * seen
                probs = jnp.exp(raw_s[at, cols] + (band[at, 0 : cols.stop - cols.start].astype(F32) - total))
                d_scores = probs * (d_probs_s[at, cols] - drop_win)
                mass_s[at, cols] = (mass_s[at, cols].astype(F32) + probs).astype(BF16)
                d_raw_s[at, cols] = (d_raw_s[at, cols].astype(F32) + d_scores).astype(BF16)

            each(128, 64, part, 128 * i)
        dqk[:, query_cols(h)] = (
            FEAT ** (-0.5) * dot_nn(d_raw_s[...], qk[:, key_cols(h)])
        ).astype(BF16)
        dqk[:, key_cols(h)] = dot_tn(d_raw_s[...], qk[:, query_cols(h)]).astype(BF16)
        dv[:, vcols] = dot_tn(mass_s[...], dmixed[:, vcols]).astype(BF16)

    def fill_qkv(grad):
        load_normed.wait()

        def block(half, lanes):
            for src, at in ((dqk, slice(0, 128)), (dv, slice(128, 640))):
                top = dot_tn(n2[:, lanes], src[...])
                half[..., at] = top.astype(BF16).reshape(2, 2, 4, 64, at.stop - at.start)

        halves(grad, block)

    def done_qkv(total):
        o_query[...] = total[:, 0:64]
        o_key[...] = total[:, 64:128]
        o_value[...] = total[:, 128:640]
        part = weigh(total[:, 0:128], wqk[:, chunk])
        rows_v = wv[pl.ds(pl.multiple_of(dp * 64, 64), 64), :].astype(F32)
        part += jnp.sum(total[:, 128:640] * rows_v, axis=1, keepdims=True)
        gsum[1] = jnp.broadcast_to(part, gsum.shape[1:])

    pump.add(640, fill_qkv, done_qkv)
    pump.tick()

    def normed_back(rows):
        acc[rows, :] = dot_nt(dv[rows, :], wv[...])

    each(256, 256, normed_back, far_base)
    add_product(acc.at[far_rows], dqk.at[far_rows], wqk, False)
    scatter_in = Scatter(acc, bufs, mp_send.at[7], mp_recv.at[7])
    pump.tick()
    scatter_in.start_near(0)
    each(256, 256, normed_back, near_base)
    add_product(acc.at[near_rows], dqk.at[near_rows], wqk, False)

    def output(rows, total):
        block_out[rows, :] = (h1[rows, :] + total).astype(BF16)

    pump.tick()
    scatter_out.finish_far(output)
    pump.tick()
    scatter_in.start_far()
    scatter_in.start_near(1)


    def norm_one_back(rows, d_normed):
        values = x_own[rows, :].astype(F32)
        inverse = norm_rows(values)
        unit = values * inverse
        e = d_normed * gain_a
        grad_in[rows, :] += inverse * (
            e - unit * jnp.mean(e * unit, axis=-1, keepdims=True)
        )

    pump.tick()
    scatter_in.finish(norm_one_back)
    pump.tick()

    pick = (row + (dp % 2) * 64) == lane
    for i in (0, 1):
        line = jnp.sum(jnp.where(pick, gsum[1 - i], 0.0), axis=0, keepdims=True)
        gline[8 * i : 8 * i + 8, :] = jnp.broadcast_to(line, (8, 128))
    others = (mate, pair, device(x, yh, z, 1 - yl, 1 - core))
    shares = [
        remote(gline, glines.at[i], mp_send.at[8, i], mp_recv.at[8, i], target)
        for i, target in enumerate(others)
    ]
    for c in shares:
        c.start()
    for c in shares:
        c.wait()
    total = gline[...] + glines[0] + glines[1] + glines[2]
    first = (dp % 2) * 64 + mp * 16
    for i, gain in enumerate((gain_attn, gain_ffn)):
        line = total[8 * i : 8 * i + 8, :] / gain[:, chunk]
        gains_out[i : i + 1, :] = pltpu.roll(line, (128 - first) % 128, 1)[0:1, :]


def layer(lengths, x_own, g_own, gain_attn, gain_ffn, wq, wk, wv, wo, wg, wu, wd):
    tok, width = x_own.shape
    seq, ff = 4 * tok, wd.shape[0]
    tiles = -(-ff // FF_TILE)
    pad = -(-(ff % FF_TILE) // 128) * 128
    wide = 3 * FF_TILE
    vmem, hbm = pl.BlockSpec(memory_space=pltpu.VMEM), pl.BlockSpec(memory_space=pl.ANY)
    shape = jax.ShapeDtypeStruct
    sems = pltpu.SemaphoreType.DMA
    scratch = [
        pltpu.VMEM((seq, width), BF16),
        pltpu.VMEM((seq, width), BF16),
        pltpu.VMEM((seq, width), BF16),
        pltpu.VMEM((tok, width), BF16),
        pltpu.VMEM((tok, width), F32),
        pltpu.VMEM((2, 2 * FF_TILE, width), BF16),
        pltpu.VMEM((2, FF_TILE, width), BF16),
        pltpu.VMEM((128, width), BF16),
        pltpu.VMEM(wv.shape, BF16),
        pltpu.VMEM((2, 2, FF_TILE, 128), BF16),
        pltpu.VMEM((seq, 128), BF16),
        pltpu.VMEM((seq, 1024), BF16),
        pltpu.VMEM((seq, 512), BF16),
        pltpu.VMEM((seq, 512), BF16),
        pltpu.VMEM((seq, 512), BF16),
        pltpu.VMEM((seq, 128), F32),
        pltpu.VMEM((seq, seq), BF16),
        pltpu.VMEM((seq, 256), BF16),
        pltpu.VMEM((seq, width), F32),
        pltpu.VMEM((tiles, seq, FF_TILE), BF16),
        pltpu.VMEM((tiles - 1, seq, 2 * FF_TILE), BF16),
        pltpu.VMEM((seq, 2 * pad), BF16),
        pltpu.VMEM((256, 512), F32),
        pltpu.VMEM((-(-tiles // 2), seq, 2 * FF_TILE), BF16),
        pltpu.VMEM((seq, 128), BF16),
        pltpu.VMEM((2, 64, 128), F32),
        pltpu.VMEM((16, 128), F32),
        pltpu.VMEM((3, 16, 128), F32),
        pltpu.VMEM((tok, width), BF16),
        pltpu.VMEM((2, tok, width), BF16),
        pltpu.VMEM((tok, width), BF16),
        pltpu.VMEM((tok, width), BF16),
    ]
    scratch += [pltpu.VMEM((4, 2, 4, 64, wide), BF16) for _ in range(SETS)]
    scratch += [b for _ in range(SETS) for b in sum_buffers(wide)[:5]]
    scratch += [
        sems((SETS, 2, 13)),
        sems((SETS, 2, 13)),
        pltpu.SemaphoreType.REGULAR((SETS,)),
        sems((9, 2 * PARTS + 1)),
        sems((9, 2 * PARTS + 1)),
        sems((17,)),
    ]
    return pl.pallas_call(
        layer_kernel,
        out_shape=[
            shape((tok, width), BF16),
            shape((tok, width), F32),
            shape((2, 128), F32),
            shape((64, wq.shape[0]), F32),
            shape((64, wk.shape[0]), F32),
            shape((64, wv.shape[1]), F32),
            shape((64, wo.shape[0]), F32),
            shape((64, ff), F32),
            shape((64, ff), F32),
            shape((64, ff), F32),
            shape((seq, width), BF16),
        ],
        in_specs=[pl.BlockSpec(memory_space=pltpu.SMEM)] + [vmem] * 4 + [hbm] * 7,
        out_specs=[vmem] * 10 + [hbm],
        scratch_shapes=scratch,
        compiler_params=pltpu.CompilerParams(
            collective_id=0, has_side_effects=True, vmem_limit_bytes=65400 << 10
        ),
        name="layer",
    )(lengths, x_own, g_own, gain_attn, gain_ffn, wq, wk, wv, wo, wg, wu, wd)


def hand_out_kernel(n, *refs):
    sems = refs[2 * n + 3]
    copies = [pltpu.make_async_copy(refs[i], refs[n + 1 + i], sems.at[i]) for i in range(n)]
    for c in copies:
        c.start()
    gains, first, second = refs[n], refs[2 * n + 1], refs[2 * n + 2]
    first[...] = gains[0:1, 0:16]
    second[...] = gains[1:2, 0:16]
    for c in copies:
        c.wait()


def hand_out(arrays, gains):
    n = len(arrays)
    vmem, hbm = pl.BlockSpec(memory_space=pltpu.VMEM), pl.BlockSpec(memory_space=pl.ANY)
    shape = jax.ShapeDtypeStruct
    return pl.pallas_call(
        functools.partial(hand_out_kernel, n),
        out_shape=[shape(a.shape, a.dtype) for a in arrays] + [shape((1, 16), F32)] * 2,
        in_specs=[vmem] * (n + 1),
        out_specs=[hbm] * n + [vmem] * 2,
        scratch_shapes=[pltpu.SemaphoreType.DMA((n,))],
        name="hand_out",
    )(*arrays, gains)


def on_device(
    block_input,
    lengths,
    gain_attn,
    gain_ffn,
    w_query,
    w_key,
    w_value,
    w_out,
    w_gate,
    w_up,
    w_down,
    cotangent,
):
    width = block_input.shape[-1]
    out = layer(
        lengths,
        block_input.reshape(-1, width),
        cotangent.reshape(-1, width),
        gain_attn.reshape(1, -1),
        gain_ffn.reshape(1, -1),
        w_query.T,
        w_key.T,
        w_value,
        w_out,
        w_gate.T,
        w_up.T,
        w_down,
    )
    (
        block_output,
        grad_input,
        grad_query,
        grad_key,
        grad_value,
        grad_out,
        grad_gate,
        grad_up,
        grad_down,
        grad_gain_attn,
        grad_gain_ffn,
    ) = hand_out([out[0], out[1], *out[3:10]], out[2])
    return (
        block_output.reshape(block_input.shape),
        grad_input.reshape(block_input.shape),
        grad_gain_attn.reshape(-1),
        grad_gain_ffn.reshape(-1),
        grad_query,
        grad_key,
        grad_value,
        grad_out.T,
        grad_gate,
        grad_up,
        grad_down.T,
    )


def solution(mesh):
    return jax.shard_map(
        on_device,
        mesh=mesh,
        in_specs=(
            P("dp", "mp", None),
            P("dp", None),
            P(),
            P(),
            P(None, "mp"),
            P(None, "mp"),
            P(None, "mp"),
            P("mp", None),
            P(None, "mp"),
            P(None, "mp"),
            P("mp", None),
            P("dp", "mp", None),
        ),
        out_specs=(
            P("dp", "mp", None),
            P("dp", "mp", None),
            P(("dp", "mp")),
            P(("dp", "mp")),
            P("dp", "mp"),
            P("dp", "mp"),
            P("dp", "mp"),
            P("mp", "dp"),
            P("dp", "mp"),
            P("dp", "mp"),
            P("mp", "dp"),
        ),
        check_vma=False,
    )
```
